32 devices in a mesh: section: 2 (over x), dp: 16 (over z, y, core).
Axes of the slice: x: 2, y: 2, z: 4, core: 2. Of those that a mesh axis runs over, the one named last changes fastest.
Arguments:
- tokens: bfloat16 [7680, 1024], P('dp'), may hold values from -6 to 6
- cotangent: bfloat16 [7680, 1024], P('dp'), may hold values from -6 to 6
- norm_gains: float32 [2, 2, 1024], P('section'), may hold values from 0.1 to 1.9
- norm_biases: float32 [2, 2, 1024], P('section'), may hold values from -3 to 3
- w_qkv: bfloat16 [2, 1024, 3072], P('section'), may hold values from -0.1875 to 0.1875
- w_out: bfloat16 [2, 1024, 1024], P('section'), may hold values from -0.375 to 0.375
- w_up: bfloat16 [2, 1024, 2048], P('section'), may hold values from -0.1875 to 0.1875
- w_down: bfloat16 [2, 2048, 1024], P('section'), may hold values from -0.125 to 0.125
Outputs:
- mixed: bfloat16 [2, 7680, 1024], P('section', 'dp')
- grad_inputs: bfloat16 [2, 7680, 1024], P('section', 'dp')
- grad_qkv: float32 [2, 1024, 3072], P('section', 'dp')
- grad_out: float32 [2, 1024, 1024], P('section', None, 'dp')
- grad_up: float32 [2, 1024, 2048], P('section', 'dp')
- grad_down: float32 [2, 2048, 1024], P('section', None, 'dp')
- grad_gains: float32 [2, 2, 1024], P('section', None, 'dp')
- grad_biases: float32 [2, 2, 1024], P('section', None, 'dp')
The draws below stay inside these ranges and needn't reach their ends.
All inputs are finite; a program needn't handle non-finite values.
Results may differ from the reference program's by a relative error of at most 0.015.
Values may be sent and summed in bfloat16 or wider, within the bound.
A program may use at most 256 MiB of HBM per device.

```python
import math
import jax
import jax.numpy as jnp
from jax import lax

D = 1024
FF = 2048
HEADS = 8
HEAD_DIM = 128
ITEM_LEN = 15
TOK_DEV = 480
TOKENS = 7680
N_DP = 16


def spiked(values, stream_key, source, target, parts, factor):
    owner, partner = [(jnp.arange(values.shape[dim]) // (values.shape[dim] // parts)).reshape([-1 if axis == dim else 1 for axis in range(values.ndim)]) for dim in (source, target)]
    chosen = jax.random.permutation(stream_key, parts)[partner]
    strong = (owner == chosen) | (owner == (partner + parts // 2) % parts)
    return jnp.where(strong, factor * values, values)


def level_of(own_key, dims, split, least, high):
    level, own = 1.0, jax.random.fold_in(own_key, 6)
    for position, parts in split:
        heights = jnp.exp(jax.random.uniform(jax.random.fold_in(own, position), (parts,), jnp.float32, least / len(split), high / len(split)))
        level = level * jnp.repeat(heights, dims[position] // parts).reshape([-1 if axis == position else 1 for axis in range(len(dims))])
    return level


def bell_draw(own_key, extent, width, limit, split=(), held_as=jnp.bfloat16):
    loudness = level_of(own_key, extent, split, -0.22, 0.18) if split else 1.0
    drawn = jax.random.normal(own_key, extent, jnp.float32) * width * loudness
    return jnp.minimum(jnp.maximum(drawn, -limit), limit).astype(held_as)


def gaussian_with(own_key, shape, spread, bound, shards, heavy, dtype=jnp.bfloat16):
    array = spread * jax.random.normal(own_key, shape, jnp.float32)
    if shards:
        array = array * level_of(own_key, shape, shards, -0.22, 0.18)
    return jnp.clip(spiked(array, jax.random.fold_in(own_key, 3), *heavy), -bound, bound).astype(dtype)


def setup_inputs(seed: int = 0) -> dict:
    keys = jax.random.split(jax.random.key(seed), 9)
    tokens = gaussian_with(keys[0], (TOKENS, D), 1.0, 6.0, ((0, 16),), (0, 1, 16, 2.0))
    cotangent = gaussian_with(keys[1], (TOKENS, D), 1.0, 6.0, ((0, 16),), (0, 1, 16, 2.0))
    norm_gains = jnp.clip(1.0 + 0.18 * jax.random.normal(keys[2], (2, 2, D), jnp.float32), 0.1, 1.9)
    norm_biases = bell_draw(keys[3], (2, 2, D), 0.5, 3.0, ((0, 2),), jnp.float32)
    w_qkv = bell_draw(keys[4], (2, D, 3 * D), D ** -0.5, 0.1875, ((0, 2),))
    w_out = bell_draw(keys[5], (2, D, D), (D // 4) ** -0.5, 0.375, ((0, 2),))
    w_up = bell_draw(keys[6], (2, D, FF), D ** -0.5, 0.1875, ((0, 2),))
    w_down = bell_draw(keys[7], (2, FF, D), FF ** -0.5, 0.125, ((0, 2),))
    return {"tokens": tokens, "cotangent": cotangent, "norm_gains": norm_gains, "norm_biases": norm_biases, "w_qkv": w_qkv, "w_out": w_out, "w_up": w_up, "w_down": w_down}


@jax.custom_vjp
def low(v):
    return lax.optimization_barrier(v.astype(jnp.bfloat16)).astype(jnp.float32)

@jax.custom_vjp
def low_back(v):
    return v

def low_keep(v):
    return (low(v), None)

def low_pass(kept, grad):
    return (grad,)

def back_keep(v):
    return (v, None)

def back_low(kept, grad):
    return (low(grad),)
low.defvjp(low_keep, low_pass)
low_back.defvjp(back_keep, back_low)
EPSILON = 1e-05
HIGHEST = lax.Precision.HIGHEST

def normalize(values, gain, offset):
    average = lax.optimization_barrier(jnp.mean(values, axis=-1, keepdims=True))
    centered = values - average
    variance = lax.optimization_barrier(jnp.mean(centered * centered, axis=-1, keepdims=True))
    return centered * lax.rsqrt(variance + EPSILON) * gain + offset

def gelu_tanh(u):
    return 0.5 * u * (1.0 + jnp.tanh(0.7978845608 * (u + 0.044715 * u * u * u)))

def layer(hidden, gains, biases, w_qkv, w_out, w_up, w_down):
    item_count = hidden.shape[0] // ITEM_LEN
    normed = low(normalize(hidden, gains[0], biases[0]))
    project = low_back(low(jnp.dot(normed, w_qkv, precision=HIGHEST)))
    shaped = project.reshape(item_count, ITEM_LEN, 3, HEADS, HEAD_DIM)
    queries = shaped[:, :, 0]
    key_part = shaped[:, :, 1]
    values = shaped[:, :, 2]
    scale = 1.0 / math.sqrt(HEAD_DIM)
    scores = jnp.einsum('ithd,ijhd->ihtj', queries, key_part, precision=HIGHEST) * scale
    scores = low_back(scores)
    row_ids = lax.broadcasted_iota(jnp.int32, (ITEM_LEN, ITEM_LEN), 0)
    col_ids = lax.broadcasted_iota(jnp.int32, (ITEM_LEN, ITEM_LEN), 1)
    scores = jnp.where(col_ids <= row_ids, scores, -1e+30)
    row_max = lax.optimization_barrier(jnp.max(scores, axis=-1, keepdims=True))
    exponent = jnp.exp(scores - row_max)
    probs = low(exponent / lax.optimization_barrier(jnp.sum(exponent, axis=-1, keepdims=True)))
    context = jnp.einsum('ihtj,ijhd->ithd', probs, values, precision=HIGHEST).reshape(hidden.shape[0], D)
    context = low_back(low(context))
    middle = hidden + low_back(jnp.dot(context, w_out, precision=HIGHEST))
    normed_two = low(normalize(middle, gains[1], biases[1]))
    upward = low_back(jnp.dot(normed_two, w_up, precision=HIGHEST))
    active = low(gelu_tanh(upward))
    return middle + low_back(jnp.dot(active, w_down, precision=HIGHEST))

def two_layers(inputs, probe, gains, biases, w_qkv, w_out, w_up, w_down):
    first_out = low(layer(low_back(inputs), gains[0], biases[0], w_qkv[0], w_out[0], w_up[0], w_down[0]))
    second_out = layer(low_back(first_out + probe), gains[1], biases[1], w_qkv[1], w_out[1], w_up[1], w_down[1])
    return (first_out, low(second_out))

def reference(tokens, cotangent, norm_gains, norm_biases, w_qkv, w_out, w_up, w_down):
    params = tuple((member.astype(jnp.float32) for member in (norm_gains, norm_biases, w_qkv, w_out, w_up, w_down)))
    block_rows = tokens.reshape(N_DP, TOK_DEV, D)
    cot_rows = cotangent.reshape(N_DP, TOK_DEV, D)

    def one_block(totals, pair):
        inputs = pair[0].astype(jnp.float32)
        probe = jnp.zeros_like(inputs)
        outputs, pullback = jax.vjp(two_layers, inputs, probe, *params)
        gradients = pullback((jnp.zeros_like(inputs), pair[1].astype(jnp.float32)))
        totals = tuple((total + grad for total, grad in zip(totals, gradients[2:])))
        result = (outputs[0].astype(jnp.bfloat16), outputs[1].astype(jnp.bfloat16), gradients[0].astype(jnp.bfloat16), gradients[1].astype(jnp.bfloat16))
        return (totals, result)
    start = tuple((jnp.zeros_like(member) for member in params))
    totals, results = lax.scan(one_block, start, (block_rows, cot_rows))
    mixed = jnp.stack([results[0].reshape(TOKENS, D), results[1].reshape(TOKENS, D)])
    grad_inputs = jnp.stack([results[2].reshape(TOKENS, D), results[3].reshape(TOKENS, D)])
    return (mixed, grad_inputs, totals[2], totals[3], totals[4], totals[5], totals[0], totals[1])
```

```python
import functools
import math

import jax
import jax.numpy as jnp
from jax import lax
from jax.experimental import pallas as pl
from jax.experimental.pallas import tpu as pltpu
from jax.sharding import PartitionSpec as P

HEADS = 8
HEAD_DIM = 128
ITEM_LEN = 15
MICRO = 2
EPSILON = 1e-05

RING, PAIR, CORES = 4, 2, 2
GROUP = RING * PAIR * CORES
PANEL = 256
MESH = pl.DeviceIdType.MESH
BF16, F32 = jnp.bfloat16, jnp.float32


def passed_along(block, axis, distance):
    devices = range(lax.axis_size(axis))
    route = [(i - distance, i) for i in devices if i - distance in devices]
    return lax.ppermute(block, axis, route)


def normalize(values, gain, offset):
    average = jnp.mean(values, axis=-1, keepdims=True)
    centered = values - average
    variance = jnp.mean(centered * centered, axis=-1, keepdims=True)
    return centered * lax.rsqrt(variance + EPSILON) * gain + offset


def gelu_tanh(u):
    return 0.5 * u * (1.0 + jnp.tanh(0.7978845608 * (u + 0.044715 * u * u * u)))


def item_mask(row_count):
    row_ids = lax.broadcasted_iota(jnp.int32, (row_count, row_count), 0)
    col_ids = lax.broadcasted_iota(jnp.int32, (row_count, row_count), 1)
    return (row_ids // ITEM_LEN == col_ids // ITEM_LEN) & (col_ids <= row_ids)


def forward(inputs, weights):
    gains, biases, w_qkv, w_out, w_up, w_down = weights
    row_count = inputs.shape[0]
    hidden = inputs.astype(jnp.float32)
    normed = normalize(hidden, gains[0], biases[0]).astype(jnp.bfloat16)
    project = jnp.dot(normed, w_qkv, preferred_element_type=jnp.float32).astype(jnp.bfloat16)
    shaped = project.reshape(row_count, 3, HEADS, HEAD_DIM)
    scale = 1.0 / math.sqrt(HEAD_DIM)
    scores = (
        jnp.einsum("rhd,chd->hrc", shaped[:, 0], shaped[:, 1], preferred_element_type=jnp.float32)
        * scale
    )
    scores = jnp.where(item_mask(row_count), scores, -1e30)
    row_max = jnp.max(scores, axis=-1, keepdims=True)
    exponent = jnp.exp(scores - row_max)
    probs = exponent / jnp.sum(exponent, axis=-1, keepdims=True)
    context = jnp.einsum(
        "hrc,chd->rhd", probs.astype(jnp.bfloat16), shaped[:, 2], preferred_element_type=jnp.float32
    )
    context = context.reshape(row_count, HEADS * HEAD_DIM).astype(jnp.bfloat16)
    middle = hidden + jnp.dot(context, w_out, preferred_element_type=jnp.float32)
    normed_two = normalize(middle, gains[1], biases[1]).astype(jnp.bfloat16)
    upward = jnp.dot(normed_two, w_up, preferred_element_type=jnp.float32)
    active = gelu_tanh(upward).astype(jnp.bfloat16)
    output = (middle + jnp.dot(active, w_down, preferred_element_type=jnp.float32)).astype(
        jnp.bfloat16
    )
    return (output, (hidden, normed, project, probs, context, middle, normed_two, upward, active))


def backward(incoming, cache, weights):
    gains, biases, w_qkv, w_out, w_up, w_down = weights
    hidden, normed, project, probs, context, middle, normed_two, upward, active = cache
    row_count = hidden.shape[0]
    scale = 1.0 / math.sqrt(HEAD_DIM)
    grad_active = jnp.einsum("rd,fd->rf", incoming, w_down, preferred_element_type=jnp.float32)
    unused, gelu_pull = jax.vjp(gelu_tanh, upward)
    grad_upward = gelu_pull(grad_active)[0].astype(jnp.bfloat16)
    grad_normed_two = jnp.einsum("rf,mf->rm", grad_upward, w_up, preferred_element_type=jnp.float32)
    unused, second_pull = jax.vjp(normalize, middle, gains[1], biases[1])
    grad_middle_norm, grad_gain_two, grad_bias_two = second_pull(grad_normed_two)
    grad_middle = incoming.astype(jnp.float32) + grad_middle_norm
    grad_attended = grad_middle.astype(jnp.bfloat16)
    grad_context = jnp.einsum("rn,mn->rm", grad_attended, w_out, preferred_element_type=jnp.float32)
    grad_context = grad_context.astype(jnp.bfloat16).reshape(row_count, HEADS, HEAD_DIM)
    shaped = project.reshape(row_count, 3, HEADS, HEAD_DIM)
    grad_probs = jnp.einsum(
        "rhd,chd->hrc", grad_context, shaped[:, 2], preferred_element_type=jnp.float32
    )
    grad_values = jnp.einsum(
        "hrc,rhd->chd", probs.astype(jnp.bfloat16), grad_context, preferred_element_type=jnp.float32
    )
    grad_scores = probs * (grad_probs - jnp.sum(probs * grad_probs, axis=-1, keepdims=True))
    grad_scores = grad_scores.astype(jnp.bfloat16)
    grad_queries = (
        jnp.einsum("hrc,chd->rhd", grad_scores, shaped[:, 1], preferred_element_type=jnp.float32)
        * scale
    )
    grad_keys = (
        jnp.einsum("hrc,rhd->chd", grad_scores, shaped[:, 0], preferred_element_type=jnp.float32)
        * scale
    )
    grad_project = jnp.stack([grad_queries, grad_keys, grad_values], axis=1)
    grad_project = grad_project.reshape(row_count, 3 * HEADS * HEAD_DIM).astype(jnp.bfloat16)
    grad_normed = jnp.einsum("rn,mn->rm", grad_project, w_qkv, preferred_element_type=jnp.float32)
    unused, first_pull = jax.vjp(normalize, hidden, gains[0], biases[0])
    grad_hidden_norm, grad_gain_one, grad_bias_one = first_pull(grad_normed)
    grad_hidden = (grad_middle + grad_hidden_norm).astype(jnp.bfloat16)
    vectors = (grad_gain_one, grad_gain_two, grad_bias_one, grad_bias_two)
    lefts = (incoming, normed_two, grad_attended, normed)
    rights = (active, grad_upward, context, grad_project)
    return (grad_hidden, vectors, lefts, rights)


def reduce_kernel(
    left_in, active_in, du_in, context_in, dqkv_in, vector_in,
    out, vector_out,
    left, right, parts, fin,
    z_one, z_two, z_pair, y_one, y_two, y_three, vectors,
    copy_sem, core_send, core_recv, fin_send, fin_recv,
    z_one_send, z_one_recv, z_two_send, z_two_recv, z_pair_send, z_pair_recv,
    y_one_send, y_one_recv, y_two_send, y_two_recv, y_three_send, y_three_recv,
    vector_send, vector_recv,
):
    rows = left.shape[2]
    half_rows = parts.shape[3] // 2
    panels = parts.shape[0]
    ring_panels, pair_panels = z_one.shape[0], y_one.shape[0]
    section = lax.axis_index("section")
    place = lax.axis_index("dp")
    first = (place // GROUP) * GROUP
    mine = place - first
    z, y, core = mine // (PAIR * CORES), (mine // CORES) % PAIR, mine % CORES
    other_y, other_core = 1 - y, 1 - core
    z_up, z_far, z_down = ((z + step) % RING for step in (1, 2, 3))

    def device(zz, yy, cc):
        return (section, first + (zz * PAIR + yy) * CORES + cc)

    up, down = device(z_up, y, core), device(z_down, y, core)
    beside, twin = device(z, other_y, core), device(z, y, other_core)

    barrier = pltpu.get_barrier_semaphore()
    for step in range(1, GROUP):
        peer = (section, first + (mine + step) % GROUP)
        pl.semaphore_signal(barrier, inc=1, device_id=peer, device_id_type=MESH)
    pl.semaphore_wait(barrier, GROUP - 1)

    def send(source, target, send_sem, recv_sem, to):
        return pltpu.make_async_remote_copy(
            src_ref=source, dst_ref=target, send_sem=send_sem, recv_sem=recv_sem,
            device_id=to, device_id_type=MESH,
        )

    inputs = (active_in, du_in, context_in, dqkv_in)
    offset, local, swaps = 0, [], []
    for i, ref in enumerate(inputs):
        width = ref.shape[1] // 2
        own = ref.at[:, pl.ds(pl.multiple_of(core * width, 128), width)]
        theirs = ref.at[:, pl.ds(pl.multiple_of(other_core * width, 128), width)]
        place_in = right.at[0, :, pl.ds(offset, width)]
        place_out = right.at[1, :, pl.ds(offset, width)]
        local.append((
            pltpu.make_async_copy(left_in.at[i], left.at[i, 0], copy_sem.at[0, i]),
            pltpu.make_async_copy(own, place_in, copy_sem.at[1, i]),
        ))
        swaps.append((
            send(left_in.at[i], left.at[i, 1], core_send.at[0, i], core_recv.at[0, i], twin),
            send(theirs, place_out, core_send.at[1, i], core_recv.at[1, i], twin),
        ))
        offset += width
    for pair_a, pair_b in zip(local, swaps):
        for copy in pair_a + pair_b:
            copy.start()

    def send_vector(step):
        peer = (mine + step) % GROUP
        start = pl.multiple_of((peer // CORES) * 128, 128)
        return send(
            vector_in.at[:, pl.ds(start, 128)], vectors.at[mine],
            vector_send.at[step], vector_recv.at[mine], (section, first + peer),
        )

    @pl.loop(1, GROUP)
    def _(step):
        send_vector(step).start()

    def z_one_send_of(i, p, way):
        rows_of = pl.ds(way * half_rows, half_rows)
        return send(parts.at[p, z_far, :, rows_of], z_one.at[i, way],
                    z_one_send.at[i, way], z_one_recv.at[i, way], (up, down)[way])

    def z_two_send_of(i, p, way):
        return send(parts.at[p, (z_up, z_down)[way]], z_two.at[i, way],
                    z_two_send.at[i, way], z_two_recv.at[i, way], (up, down)[way])

    def z_pair_send_of(i, p):
        return send(parts.at[p, z, other_y], z_pair.at[i], z_pair_send.at[i], z_pair_recv.at[i], beside)

    def y_one_send_of(i, p):
        return send(parts.at[p, :, other_y], y_one.at[i], y_one_send.at[i], y_one_recv.at[i], beside)

    def y_two_send_of(i, p, way):
        rows_of = pl.ds(way * half_rows, half_rows)
        return send(parts.at[p, z_far, y, rows_of], y_two.at[i, way],
                    y_two_send.at[i, way], y_two_recv.at[i, way], (up, down)[way])

    def y_three_send_of(i, p, way):
        return send(parts.at[p, (z_up, z_down)[way], y], y_three.at[i, way],
                    y_three_send.at[i, way], y_three_recv.at[i, way], (up, down)[way])

    def fin_of(p):
        return send(fin.at[p], out.at[core, :, pl.ds(pl.multiple_of(p * PANEL, PANEL), PANEL)],
                    fin_send.at[p], fin_recv.at[p], twin)

    def ring_panel(i):
        return jnp.minimum(2 * i + 1, pair_panels + i)

    def add(target, *refs):
        total = target[...].astype(F32)
        for ref in refs:
            total = total + ref[...].astype(F32)
        target[...] = total.astype(BF16)

    starts = [0]
    for ref in inputs:
        starts.append(starts[-1] + ref.shape[1] // 2 // PANEL)

    @pl.loop(0, panels)
    def _(p):
        which = 0
        for i, start in enumerate(starts[:-1]):
            which = which + (0 if i == 0 else (p >= start).astype(jnp.int32))

            @pl.when(p == start)
            def _(i=i):
                for copy in local[i]:
                    copy.wait()
                for copy in swaps[i]:
                    copy.wait_recv()

        columns = pl.ds(pl.multiple_of(p * PANEL, PANEL), PANEL)
        total = None
        for source in range(CORES):
            term = lax.dot_general(
                left[which, source], right[source, :, columns], (((0,), (0,)), ((), ())),
                preferred_element_type=F32,
            )
            total = term if total is None else total + term
        parts[p] = total.astype(BF16).reshape(parts.shape[1:])
        is_pair = (p % 2 == 0) & (p < 2 * pair_panels)

        @pl.when(is_pair)
        def _():
            y_one_send_of(p // 2, p).start()

        @pl.when(jnp.logical_not(is_pair))
        def _():
            i = p // 2 + p // (panels - 1)
            z_one_send_of(i, p, 0).start()
            z_one_send_of(i, p, 1).start()

    halves = [pl.ds(way * half_rows, half_rows) for way in range(2)]

    @pl.loop(0, ring_panels)
    def _(i):
        p = ring_panel(i)
        for way in range(2):
            z_one_send_of(i, p, way).wait_recv()
            add(parts.at[p, (z_up, z_down)[way], :, halves[way]], z_one.at[i, way])
            z_two_send_of(i, p, way).start()

    @pl.loop(0, ring_panels + 1)
    def _(i):
        @pl.when(i < pair_panels)
        def _():
            p = 2 * i
            y_one_send_of(i, p).wait_recv()
            for step in (2, 1, 3):
                zz = (z + step) % RING
                add(parts.at[p, zz, y], y_one.at[i, zz])
                if step == 2:
                    y_two_send_of(i, p, 0).start()
                    y_two_send_of(i, p, 1).start()

        @pl.when(i < ring_panels)
        def _():
            p = ring_panel(i)
            z_two_send_of(i, p, 0).wait_recv()
            z_two_send_of(i, p, 1).wait_recv()
            add(parts.at[p, z, other_y], z_two.at[i, 0, other_y], z_two.at[i, 1, other_y])
            z_pair_send_of(i, p).start()

        j = i - 1

        @pl.when((j >= 0) & (j < pair_panels))
        def _():
            p = 2 * j
            for way in range(2):
                y_two_send_of(j, p, way).wait_recv()
                add(parts.at[p, (z_up, z_down)[way], y, halves[way]], y_two.at[j, way])
                y_three_send_of(j, p, way).start()

    def finish(p, *refs):
        for kept in (True, False):
            which = core if kept else other_core
            rows_of = pl.ds(pl.multiple_of(which * half_rows, half_rows), half_rows)
            total = parts[p, z, y, rows_of].astype(F32)
            for ref in refs:
                total = total + ref[rows_of].astype(F32)
            if kept:
                out[core, :, pl.ds(pl.multiple_of(p * PANEL, PANEL), PANEL)] = total
            else:
                fin[p] = total
                fin_of(p).start()

    @pl.loop(0, ring_panels)
    def _(i):
        p = ring_panel(i)
        z_pair_send_of(i, p).wait_recv()
        finish(p, z_two.at[i, 0, y], z_two.at[i, 1, y], z_pair.at[i])

    @pl.loop(0, pair_panels)
    def _(i):
        p = 2 * i
        y_three_send_of(i, p, 0).wait_recv()
        y_three_send_of(i, p, 1).wait_recv()
        finish(p, y_one.at[i, z], y_three.at[i, 0], y_three.at[i, 1])

    own_start = pl.multiple_of((mine // CORES) * 128, 128)
    vector_total = vector_in[:, pl.ds(own_start, 128)]
    for step in range(1, GROUP):
        sender = (mine + step) % GROUP
        send(vector_in.at[:, pl.ds(0, 128)], vectors.at[sender], vector_send.at[step],
             vector_recv.at[sender], twin).wait_recv()
        vector_total = vector_total + vectors[sender]
    vector_out[...] = vector_total

    for pair in swaps:
        for copy in pair:
            copy.wait_send()

    @pl.loop(1, GROUP)
    def _(step):
        send_vector(step).wait_send()

    @pl.loop(0, ring_panels)
    def _(i):
        p = ring_panel(i)
        for way in range(2):
            z_one_send_of(i, p, way).wait_send()
            z_two_send_of(i, p, way).wait_send()
        z_pair_send_of(i, p).wait_send()

    @pl.loop(0, pair_panels)
    def _(i):
        p = 2 * i
        y_one_send_of(i, p).wait_send()
        for way in range(2):
            y_two_send_of(i, p, way).wait_send()
            y_three_send_of(i, p, way).wait_send()

    @pl.loop(0, panels)
    def _(p):
        fin_of(p).wait()


def reduced(lefts, rights, vectors):
    left = jnp.stack(lefts)
    rows, width = lefts[0].shape
    columns = sum(member.shape[1] for member in rights) // CORES
    panels = columns // PANEL
    pair_panels = panels * 7 // 16
    ring_panels = panels - pair_panels
    chunk = width // (RING * PAIR)
    half = chunk // 2
    dma = pltpu.SemaphoreType.DMA
    anywhere = pl.BlockSpec(memory_space=pl.ANY)
    in_vmem = pl.BlockSpec(memory_space=pltpu.VMEM)
    scratch = [
        pltpu.VMEM((4, CORES, rows, width), BF16),
        pltpu.VMEM((CORES, rows, columns), BF16),
        pltpu.VMEM((panels, RING, PAIR, chunk, PANEL), BF16),
        pltpu.VMEM((panels, half, PANEL), F32),
        pltpu.VMEM((ring_panels, 2, PAIR, half, PANEL), BF16),
        pltpu.VMEM((ring_panels, 2, PAIR, chunk, PANEL), BF16),
        pltpu.VMEM((ring_panels, chunk, PANEL), BF16),
        pltpu.VMEM((pair_panels, RING, chunk, PANEL), BF16),
        pltpu.VMEM((pair_panels, 2, half, PANEL), BF16),
        pltpu.VMEM((pair_panels, 2, chunk, PANEL), BF16),
        pltpu.VMEM((GROUP, 8, chunk), F32),
        dma((2, 4)), dma((2, 4)), dma((2, 4)), dma((panels,)), dma((panels,)),
        dma((ring_panels, 2)), dma((ring_panels, 2)), dma((ring_panels, 2)), dma((ring_panels, 2)),
        dma((ring_panels,)), dma((ring_panels,)),
        dma((pair_panels,)), dma((pair_panels,)),
        dma((pair_panels, 2)), dma((pair_panels, 2)), dma((pair_panels, 2)), dma((pair_panels, 2)),
        dma((GROUP,)), dma((GROUP,)),
    ]
    return pl.pallas_call(
        reduce_kernel,
        out_shape=(
            jax.ShapeDtypeStruct((CORES, half, columns), F32),
            jax.ShapeDtypeStruct((8, chunk), F32),
        ),
        in_specs=[anywhere] * 5 + [in_vmem],
        out_specs=(in_vmem, in_vmem),
        scratch_shapes=scratch,
        compiler_params=pltpu.CompilerParams(
            collective_id=1, has_side_effects=True, vmem_limit_bytes=56 * 2**20
        ),
        name="reduce_gradients",
    )(left, *rights, vectors)


def on_device(tokens, cotangent, norm_gains, norm_biases, w_qkv, w_out, w_up, w_down):
    weights = (norm_gains[0], norm_biases[0], w_qkv[0], w_out[0], w_up[0], w_down[0])
    section_index = lax.axis_index("section")
    is_first = section_index == 0
    width = tokens.shape[1]
    row_count = tokens.shape[0] // MICRO
    pieces = tokens.reshape(MICRO, row_count, width)
    cot_pieces = cotangent.reshape(MICRO, row_count, width)
    outgoing = jnp.zeros((row_count, width), jnp.bfloat16)
    caches = []
    produced = []
    for moment in range(MICRO + 1):
        arrived = passed_along(outgoing, "section", 1)
        own_piece = pieces[min(moment, MICRO - 1)]
        inputs = jnp.where(is_first, own_piece, arrived)
        outgoing, cache = forward(inputs, weights)
        caches.append(cache)
        produced.append(outgoing)
    mixed = lax.dynamic_slice_in_dim(jnp.stack(produced), section_index, MICRO, 0)
    mixed = mixed.reshape(1, MICRO * row_count, width)
    returning = jnp.zeros((row_count, width), jnp.bfloat16)
    returned, all_vectors, all_lefts, all_rights = [], [], [], []
    for moment in range(MICRO + 1):
        arrived = passed_along(returning, "section", -1)
        target = cot_pieces[max(MICRO - 1 - moment, 0)]
        incoming = jnp.where(is_first, arrived, target)
        returning, vectors, lefts, rights = backward(incoming, caches[MICRO - moment], weights)
        returned.append(returning)
        all_vectors.append(vectors)
        all_lefts.append(lefts)
        all_rights.append(rights)

    def chosen(members):
        stacked = jnp.stack(members[::-1])
        kept = lax.dynamic_slice_in_dim(stacked, section_index, MICRO, 0)
        return kept.reshape((MICRO * stacked.shape[1],) + stacked.shape[2:])

    lefts = [chosen(members) for members in zip(*all_lefts)]
    rights = [chosen(members) for members in zip(*all_rights)]
    vectors = [
        lax.dynamic_slice_in_dim(jnp.stack(members[::-1]), section_index, MICRO, 0).sum(0)
        for members in zip(*all_vectors)
    ]
    grad_inputs = chosen(returned)[None]
    return (mixed, grad_inputs) + shares(lefts, rights, vectors)


def shares(lefts, rights, vectors):
    groups = lax.axis_size("dp") // GROUP
    width = lefts[0].shape[1]
    if groups > 1:
        def ordered(member):
            split = member.reshape(member.shape[:-1] + (groups, RING * PAIR, CORES, -1))
            moved = jnp.moveaxis(split, -4, -2)
            return moved.reshape(member.shape)

        lefts = [ordered(member) for member in lefts]
        vectors = [ordered(member) for member in vectors]
    vectors = jnp.concatenate([jnp.stack(vectors), jnp.zeros((4, width), F32)])
    block, vector_block = reduced(lefts, rights, vectors)
    core = lax.axis_index("dp") % CORES
    vector_block = lax.dynamic_slice_in_dim(vector_block[:4], core * block.shape[1], block.shape[1], 1)
    pieces = []
    offset = 0
    for member in rights:
        half = member.shape[1] // CORES
        part = block[:, :, offset : offset + half]
        pieces.append(jnp.concatenate([part[0], part[1]], axis=1))
        offset += half
    vector_block = vector_block.T
    if groups > 1:
        same = [[g * GROUP + j for g in range(groups)] for j in range(GROUP)]

        def summed(member):
            return lax.psum_scatter(
                member, "dp", scatter_dimension=0, axis_index_groups=same, tiled=True
            )

        pieces = [summed(member) for member in pieces]
        vector_block = summed(vector_block)
    down, up, out, qkv = pieces
    vector_block = vector_block.T
    return (
        qkv[None], out.T[None], up[None], down.T[None],
        vector_block[None, 0:2], vector_block[None, 2:4],
    )


def solution(mesh):
    placed = (P("dp", None),) * 2 + (P("section", None, None),) * 6
    return jax.shard_map(
        on_device,
        mesh=mesh,
        in_specs=placed,
        out_specs=(
            P("section", "dp", None),
            P("section", "dp", None),
            P("section", "dp", None),
            P("section", None, "dp"),
            P("section", "dp", None),
            P("section", None, "dp"),
            P("section", None, "dp"),
            P("section", None, "dp"),
        ),
        check_vma=False,
    )
```

```python
import functools
import math

import jax
import jax.numpy as jnp
from jax import lax
from jax.experimental import pallas as pl
from jax.experimental.pallas import tpu as pltpu
from jax.sharding import PartitionSpec as P

HEADS = 8
HEAD_DIM = 128
ITEM_LEN = 15
MICRO = 2
EPSILON = 1e-05

LINE, PAIR, CORES = 4, 2, 2
GROUP = LINE * PAIR * CORES
PANEL = 256
AHEAD = 3
MESH = pl.DeviceIdType.MESH
BF16, F32 = jnp.bfloat16, jnp.float32


def passed_along(block, axis, distance):
    devices = range(lax.axis_size(axis))
    route = [(i - distance, i) for i in devices if i - distance in devices]
    return lax.ppermute(block, axis, route)


def normalize(values, gain, offset):
    average = jnp.mean(values, axis=-1, keepdims=True)
    centered = values - average
    variance = jnp.mean(centered * centered, axis=-1, keepdims=True)
    return centered * lax.rsqrt(variance + EPSILON) * gain + offset


def gelu_tanh(u):
    return 0.5 * u * (1.0 + jnp.tanh(0.7978845608 * (u + 0.044715 * u * u * u)))


def item_mask(row_count):
    row_ids = lax.broadcasted_iota(jnp.int32, (row_count, row_count), 0)
    col_ids = lax.broadcasted_iota(jnp.int32, (row_count, row_count), 1)
    return (row_ids // ITEM_LEN == col_ids // ITEM_LEN) & (col_ids <= row_ids)


def forward(inputs, weights):
    gains, biases, w_qkv, w_out, w_up, w_down = weights
    row_count = inputs.shape[0]
    hidden = inputs.astype(jnp.float32)
    normed = normalize(hidden, gains[0], biases[0]).astype(jnp.bfloat16)
    project = jnp.dot(normed, w_qkv, preferred_element_type=jnp.float32).astype(jnp.bfloat16)
    shaped = project.reshape(row_count, 3, HEADS, HEAD_DIM)
    scale = 1.0 / math.sqrt(HEAD_DIM)
    scores = (
        jnp.einsum("rhd,chd->hrc", shaped[:, 0], shaped[:, 1], preferred_element_type=jnp.float32)
        * scale
    )
    scores = jnp.where(item_mask(row_count), scores, -1e30)
    row_max = jnp.max(scores, axis=-1, keepdims=True)
    exponent = jnp.exp(scores - row_max)
    probs = exponent / jnp.sum(exponent, axis=-1, keepdims=True)
    context = jnp.einsum(
        "hrc,chd->rhd", probs.astype(jnp.bfloat16), shaped[:, 2], preferred_element_type=jnp.float32
    )
    context = context.reshape(row_count, HEADS * HEAD_DIM).astype(jnp.bfloat16)
    middle = hidden + jnp.dot(context, w_out, preferred_element_type=jnp.float32)
    normed_two = normalize(middle, gains[1], biases[1]).astype(jnp.bfloat16)
    upward = jnp.dot(normed_two, w_up, preferred_element_type=jnp.float32)
    active = gelu_tanh(upward).astype(jnp.bfloat16)
    output = (middle + jnp.dot(active, w_down, preferred_element_type=jnp.float32)).astype(
        jnp.bfloat16
    )
    return (output, (hidden, normed, project, probs, context, middle, normed_two, upward, active))


def backward(incoming, cache, weights):
    gains, biases, w_qkv, w_out, w_up, w_down = weights
    hidden, normed, project, probs, context, middle, normed_two, upward, active = cache
    row_count = hidden.shape[0]
    scale = 1.0 / math.sqrt(HEAD_DIM)
    grad_active = jnp.einsum("rd,fd->rf", incoming, w_down, preferred_element_type=jnp.float32)
    unused, gelu_pull = jax.vjp(gelu_tanh, upward)
    grad_upward = gelu_pull(grad_active)[0].astype(jnp.bfloat16)
    grad_normed_two = jnp.einsum("rf,mf->rm", grad_upward, w_up, preferred_element_type=jnp.float32)
    unused, second_pull = jax.vjp(normalize, middle, gains[1], biases[1])
    grad_middle_norm, grad_gain_two, grad_bias_two = second_pull(grad_normed_two)
    grad_middle = incoming.astype(jnp.float32) + grad_middle_norm
    grad_attended = grad_middle.astype(jnp.bfloat16)
    grad_context = jnp.einsum("rn,mn->rm", grad_attended, w_out, preferred_element_type=jnp.float32)
    grad_context = grad_context.astype(jnp.bfloat16).reshape(row_count, HEADS, HEAD_DIM)
    shaped = project.reshape(row_count, 3, HEADS, HEAD_DIM)
    grad_probs = jnp.einsum(
        "rhd,chd->hrc", grad_context, shaped[:, 2], preferred_element_type=jnp.float32
    )
    grad_values = jnp.einsum(
        "hrc,rhd->chd", probs.astype(jnp.bfloat16), grad_context, preferred_element_type=jnp.float32
    )
    grad_scores = probs * (grad_probs - jnp.sum(probs * grad_probs, axis=-1, keepdims=True))
    grad_scores = grad_scores.astype(jnp.bfloat16)
    grad_queries = (
        jnp.einsum("hrc,chd->rhd", grad_scores, shaped[:, 1], preferred_element_type=jnp.float32)
        * scale
    )
    grad_keys = (
        jnp.einsum("hrc,rhd->chd", grad_scores, shaped[:, 0], preferred_element_type=jnp.float32)
        * scale
    )
    grad_project = jnp.stack([grad_queries, grad_keys, grad_values], axis=1)
    grad_project = grad_project.reshape(row_count, 3 * HEADS * HEAD_DIM).astype(jnp.bfloat16)
    grad_normed = jnp.einsum("rn,mn->rm", grad_project, w_qkv, preferred_element_type=jnp.float32)
    unused, first_pull = jax.vjp(normalize, hidden, gains[0], biases[0])
    grad_hidden_norm, grad_gain_one, grad_bias_one = first_pull(grad_normed)
    grad_hidden = (grad_middle + grad_hidden_norm).astype(jnp.bfloat16)
    vectors = (grad_gain_one, grad_gain_two, grad_bias_one, grad_bias_two)
    lefts = (incoming, normed_two, grad_attended, normed)
    rights = (active, grad_upward, context, grad_project)
    return (grad_hidden, vectors, lefts, rights)


def reduce_kernel(
    left_in, active_in, du_in, context_in, dqkv_in, vector_in,
    out, vector_out,
    left, right, parts, fin,
    line_in, line_across, line_beside, pair_beside, pair_in, pair_across, vectors,
    copy_sem, core_send, core_recv, fin_send, fin_recv,
    line_in_send, line_in_recv, line_across_send, line_across_recv,
    line_out_send, line_out_recv, line_beside_send, line_beside_recv,
    pair_beside_send, pair_beside_recv, pair_in_send, pair_in_recv,
    pair_across_send, pair_across_recv, pair_out_send, pair_out_recv,
    vector_send, vector_recv,
):
    half_rows = parts.shape[3] // 2
    panels = parts.shape[0]
    lines, pairs = line_in.shape[0], pair_in.shape[0]
    section = lax.axis_index("section")
    place = lax.axis_index("dp")
    first = (place // GROUP) * GROUP
    mine = place - first
    z, y, core = mine // (PAIR * CORES), (mine // CORES) % PAIR, mine % CORES
    other_y, other_core = 1 - y, 1 - core
    far_side = z // 2
    is_end = (z == 0) | (z == LINE - 1)
    own = jnp.where(is_end, 0, 1)

    def numbered(zz):
        return zz + far_side * (LINE - 1 - 2 * zz)

    def device(zz, yy, cc):
        return (section, first + (zz * PAIR + yy) * CORES + cc)

    inner, end, across = (device(numbered(zz), y, core) for zz in (1, 0, 2))
    beside, twin = device(z, other_y, core), device(z, y, other_core)

    barrier = pltpu.get_barrier_semaphore()
    for step in range(1, GROUP):
        peer = (section, first + (mine + step) % GROUP)
        pl.semaphore_signal(barrier, inc=1, device_id=peer, device_id_type=MESH)
    pl.semaphore_wait(barrier, GROUP - 1)

    def send(source, target, send_sem, recv_sem, to):
        return pltpu.make_async_remote_copy(
            src_ref=source, dst_ref=target, send_sem=send_sem, recv_sem=recv_sem,
            device_id=to, device_id_type=MESH,
        )

    inputs = (active_in, du_in, context_in, dqkv_in)
    offset, local, swaps = 0, [], []
    for i, ref in enumerate(inputs):
        width = ref.shape[1] // 2
        kept = ref.at[:, pl.ds(pl.multiple_of(core * width, 128), width)]
        theirs = ref.at[:, pl.ds(pl.multiple_of(other_core * width, 128), width)]
        place_in = right.at[0, :, pl.ds(offset, width)]
        place_out = right.at[1, :, pl.ds(offset, width)]
        local.append((
            pltpu.make_async_copy(left_in.at[i], left.at[i, 0], copy_sem.at[0, i]),
            pltpu.make_async_copy(kept, place_in, copy_sem.at[1, i]),
        ))
        swaps.append((
            send(left_in.at[i], left.at[i, 1], core_send.at[0, i], core_recv.at[0, i], twin),
            send(theirs, place_out, core_send.at[1, i], core_recv.at[1, i], twin),
        ))
        offset += width
    for copy in local[0] + swaps[0]:
        copy.start()

    def send_vector(step):
        peer = (mine + step) % GROUP
        start = pl.multiple_of((peer // CORES) * 128, 128)
        return send(
            vector_in.at[:, pl.ds(start, 128)], vectors.at[mine],
            vector_send.at[step], vector_recv.at[mine], (section, first + peer),
        )

    @pl.loop(1, GROUP)
    def _(step):
        send_vector(step).start()

    def line_in_of(i, p):
        return send(parts.at[p, pl.ds(1, 3)], line_in.at[i], line_in_send.at[i], line_in_recv.at[i], inner)

    def line_across_of(i, p):
        return send(parts.at[p, pl.ds(2, 2)], line_across.at[i],
                    line_across_send.at[i], line_across_recv.at[i], across)

    def line_out_of(i, p):
        return send(parts.at[p, 0], line_in.at[i, 0], line_out_send.at[i], line_out_recv.at[i], end)

    def line_beside_of(i, p):
        return send(parts.at[p, own, other_y], line_beside.at[i],
                    line_beside_send.at[i], line_beside_recv.at[i], beside)

    def pair_beside_of(i, p):
        return send(parts.at[p, :, other_y], pair_beside.at[i],
                    pair_beside_send.at[i], pair_beside_recv.at[i], beside)

    def pair_in_of(i, p):
        return send(parts.at[p, pl.ds(1, 3), y], pair_in.at[i], pair_in_send.at[i], pair_in_recv.at[i], inner)

    def pair_across_of(i, p):
        return send(parts.at[p, pl.ds(2, 2), y], pair_across.at[i],
                    pair_across_send.at[i], pair_across_recv.at[i], across)

    def pair_out_of(i, p):
        return send(parts.at[p, 0, y], pair_in.at[i, 0], pair_out_send.at[i], pair_out_recv.at[i], end)

    def fin_of(p):
        return send(fin.at[p], out.at[core, :, pl.ds(pl.multiple_of(p * PANEL, PANEL), PANEL)],
                    fin_send.at[p], fin_recv.at[p], twin)

    def line_panel(i):
        return 5 * i + 1

    def pair_panel(i):
        return i + (i + 3) // 4

    def add(target, *refs):
        total = target[...].astype(F32)
        for ref in refs:
            total = total + ref[...].astype(F32)
        target[...] = total.astype(BF16)

    starts = [0]
    for ref in inputs:
        starts.append(starts[-1] + ref.shape[1] // 2 // PANEL)

    @pl.loop(0, panels)
    def _(p):
        which = 0
        for i, start in enumerate(starts[:-1]):
            which = which + (0 if i == 0 else (p >= start).astype(jnp.int32))

            @pl.when(p == start)
            def _(i=i):
                for copy in local[i]:
                    copy.wait()
                for copy in swaps[i]:
                    copy.wait_recv()
                if i + 1 < len(inputs):
                    for copy in local[i + 1] + swaps[i + 1]:
                        copy.start()

        columns = pl.ds(pl.multiple_of(p * PANEL, PANEL), PANEL)
        total = None
        for source in range(CORES):
            term = lax.dot_general(
                left[which, source], right[source, :, columns], (((0,), (0,)), ((), ())),
                preferred_element_type=F32,
            )
            total = term if total is None else total + term
        total = total.astype(BF16).reshape(parts.shape[1:])
        for zz in range(LINE):
            parts[p, numbered(zz)] = total[zz]
        is_line = p % 5 == 1

        @pl.when(jnp.logical_not(is_line) & (p < pair_panel(AHEAD)))
        def _():
            pair_beside_of(p - (p + 3) // 5, p).start()

        @pl.when((p == line_panel(0)) & is_end)
        def _():
            line_in_of(0, p).start()

    def finish(p, *refs):
        for kept in (True, False):
            which = core if kept else other_core
            rows_of = pl.ds(pl.multiple_of(which * half_rows, half_rows), half_rows)
            total = parts[p, own, y, rows_of].astype(F32)
            for ref in refs:
                total = total + ref[rows_of].astype(F32)
            if kept:
                out[core, :, pl.ds(pl.multiple_of(p * PANEL, PANEL), PANEL)] = total
            else:
                fin[p] = total
                fin_of(p).start()

    def stages(count, panel, in_of, across_of, out_of, inward, acrossward, pick):
        def relay_in(i):
            @pl.when((i >= 0) & (i < count) & jnp.logical_not(is_end))
            def _():
                p = panel(i)
                in_of(i, p).wait_recv()
                add(pick(parts.at[p, pl.ds(2, 2)]), inward.at[i, pl.ds(1, 2)])
                across_of(i, p).start()

        def relay_out(i):
            @pl.when((i >= 0) & (i < count) & jnp.logical_not(is_end))
            def _():
                p = panel(i)
                across_of(i, p).wait_recv()
                add(pick(parts.at[p, 0]), acrossward.at[i, 1])
                out_of(i, p).start()

        return relay_in, relay_out

    def whole(ref):
        return ref

    def half_of(ref):
        return ref.at[:, y] if len(ref.shape) == 4 else ref.at[y]

    line_relay_in, line_relay_out = stages(
        lines, line_panel, line_in_of, line_across_of, line_out_of, line_in, line_across, whole)
    pair_relay_in, pair_relay_out = stages(
        pairs, pair_panel, pair_in_of, pair_across_of, pair_out_of, pair_in, pair_across, half_of)

    def pair_start(i):
        @pl.when(i < pairs)
        def _():
            p = pair_panel(i)
            pair_beside_of(i, p).wait()

            @pl.when(i + AHEAD < pairs)
            def _():
                pair_beside_of(i + AHEAD, pair_panel(i + AHEAD)).start()

            add(parts.at[p, pl.ds(2, 2), y], pair_beside.at[i, pl.ds(2, 2)])
            add(parts.at[p, 1 - own, y], pair_beside.at[i, 1 - own])

            @pl.when(is_end)
            def _():
                pair_in_of(i, p).start()

    def pair_finish(i):
        @pl.when((i >= 0) & (i < pairs))
        def _():
            p = pair_panel(i)

            @pl.when(is_end)
            def _():
                pair_out_of(i, p).wait_recv()
                finish(p, pair_beside.at[i, 0], pair_in.at[i, 0])

            @pl.when(jnp.logical_not(is_end))
            def _():
                finish(p, pair_beside.at[i, 1], pair_in.at[i, 0], pair_across.at[i, 0])

    def line_cross(i):
        @pl.when((i >= 0) & (i < lines))
        def _():
            p = line_panel(i)

            @pl.when(is_end)
            def _():
                line_out_of(i, p).wait_recv()
                add(parts.at[p, 0, other_y], line_in.at[i, 0, other_y])

            @pl.when(jnp.logical_not(is_end))
            def _():
                add(parts.at[p, 1, other_y], line_in.at[i, 0, other_y], line_across.at[i, 0, other_y])

            line_beside_of(i, p).start()

    def line_finish(i):
        @pl.when((i >= 0) & (i < lines))
        def _():
            p = line_panel(i)
            line_beside_of(i, p).wait_recv()

            @pl.when(is_end)
            def _():
                finish(p, line_in.at[i, 0, y], line_beside.at[i])

            @pl.when(jnp.logical_not(is_end))
            def _():
                finish(p, line_in.at[i, 0, y], line_across.at[i, 0, y], line_beside.at[i])

    @pl.loop(0, pairs + 3)
    def _(t):
        pair_start(t)
        pair_relay_in(t - 1)
        pair_relay_out(t - 2)
        pair_finish(t - 3)
        i, phase = t // 4, t % 4

        @pl.when(phase == 1)
        def _():
            line_relay_in(i)
            line_finish(i - 1)

        @pl.when(phase == 2)
        def _():
            line_relay_out(i)

        @pl.when(phase == 3)
        def _():
            line_cross(i)

            @pl.when((i + 1 < lines) & is_end)
            def _():
                line_in_of(i + 1, line_panel(i + 1)).start()

    own_start = pl.multiple_of((mine // CORES) * 128, 128)
    vector_total = vector_in[:, pl.ds(own_start, 128)]
    for step in range(1, GROUP):
        sender = (mine + step) % GROUP
        send(vector_in.at[:, pl.ds(0, 128)], vectors.at[sender], vector_send.at[step],
             vector_recv.at[sender], twin).wait_recv()
        vector_total = vector_total + vectors[sender]
    vector_out[...] = vector_total

    for pair in swaps:
        for copy in pair:
            copy.wait_send()

    @pl.loop(1, GROUP)
    def _(step):
        send_vector(step).wait_send()

    @pl.loop(0, lines)
    def _(i):
        p = line_panel(i)
        line_beside_of(i, p).wait_send()

        @pl.when(is_end)
        def _():
            line_in_of(i, p).wait_send()

        @pl.when(jnp.logical_not(is_end))
        def _():
            line_across_of(i, p).wait_send()
            line_out_of(i, p).wait_send()

    @pl.loop(0, pairs)
    def _(i):
        p = pair_panel(i)

        @pl.when(is_end)
        def _():
            pair_in_of(i, p).wait_send()

        @pl.when(jnp.logical_not(is_end))
        def _():
            pair_across_of(i, p).wait_send()
            pair_out_of(i, p).wait_send()

    @pl.loop(0, panels)
    def _(p):
        fin_of(p).wait()


def reduced(lefts, rights, vectors):
    left = jnp.stack(lefts)
    rows, width = lefts[0].shape
    columns = sum(member.shape[1] for member in rights) // CORES
    panels = columns // PANEL
    lines = (panels + 3) // 5
    pairs = panels - lines
    chunk = width // (LINE * PAIR)
    half = chunk // 2
    dma = pltpu.SemaphoreType.DMA
    anywhere = pl.BlockSpec(memory_space=pl.ANY)
    in_vmem = pl.BlockSpec(memory_space=pltpu.VMEM)
    scratch = [
        pltpu.VMEM((4, CORES, rows, width), BF16),
        pltpu.VMEM((CORES, rows, columns), BF16),
        pltpu.VMEM((panels, LINE, PAIR, chunk, PANEL), BF16),
        pltpu.VMEM((panels, half, PANEL), F32),
        pltpu.VMEM((lines, 3, PAIR, chunk, PANEL), BF16),
        pltpu.VMEM((lines, 2, PAIR, chunk, PANEL), BF16),
        pltpu.VMEM((lines, chunk, PANEL), BF16),
        pltpu.VMEM((pairs, LINE, chunk, PANEL), BF16),
        pltpu.VMEM((pairs, 3, chunk, PANEL), BF16),
        pltpu.VMEM((pairs, 2, chunk, PANEL), BF16),
        pltpu.VMEM((GROUP, 8, chunk), F32),
        dma((2, 4)), dma((2, 4)), dma((2, 4)), dma((panels,)), dma((panels,)),
    ] + [dma((lines,))] * 8 + [dma((pairs,))] * 8 + [dma((GROUP,)), dma((GROUP,))]
    return pl.pallas_call(
        reduce_kernel,
        out_shape=(
            jax.ShapeDtypeStruct((CORES, half, columns), F32),
            jax.ShapeDtypeStruct((8, chunk), F32),
        ),
        in_specs=[anywhere] * 5 + [in_vmem],
        out_specs=(in_vmem, in_vmem),
        scratch_shapes=scratch,
        compiler_params=pltpu.CompilerParams(
            collective_id=1, has_side_effects=True, vmem_limit_bytes=56 * 2**20
        ),
        name="reduce_gradients",
    )(left, *rights, vectors)


def on_device(tokens, cotangent, norm_gains, norm_biases, w_qkv, w_out, w_up, w_down):
    weights = (norm_gains[0], norm_biases[0], w_qkv[0], w_out[0], w_up[0], w_down[0])
    section_index = lax.axis_index("section")
    is_first = section_index == 0
    width = tokens.shape[1]
    row_count = tokens.shape[0] // MICRO
    pieces = tokens.reshape(MICRO, row_count, width)
    cot_pieces = cotangent.reshape(MICRO, row_count, width)
    outgoing = jnp.zeros((row_count, width), jnp.bfloat16)
    caches = []
    produced = []
    for moment in range(MICRO + 1):
        arrived = passed_along(outgoing, "section", 1)
        own_piece = pieces[min(moment, MICRO - 1)]
        inputs = jnp.where(is_first, own_piece, arrived)
        outgoing, cache = forward(inputs, weights)
        caches.append(cache)
        produced.append(outgoing)
    mixed = lax.dynamic_slice_in_dim(jnp.stack(produced), section_index, MICRO, 0)
    mixed = mixed.reshape(1, MICRO * row_count, width)
    returning = jnp.zeros((row_count, width), jnp.bfloat16)
    returned, all_vectors, all_lefts, all_rights = [], [], [], []
    for moment in range(MICRO + 1):
        arrived = passed_along(returning, "section", -1)
        target = cot_pieces[max(MICRO - 1 - moment, 0)]
        incoming = jnp.where(is_first, arrived, target)
        returning, vectors, lefts, rights = backward(incoming, caches[MICRO - moment], weights)
        returned.append(returning)
        all_vectors.append(vectors)
        all_lefts.append(lefts)
        all_rights.append(rights)

    def chosen(members):
        stacked = jnp.stack(members[::-1])
        kept = lax.dynamic_slice_in_dim(stacked, section_index, MICRO, 0)
        return kept.reshape((MICRO * stacked.shape[1],) + stacked.shape[2:])

    lefts = [chosen(members) for members in zip(*all_lefts)]
    rights = [chosen(members) for members in zip(*all_rights)]
    vectors = [
        lax.dynamic_slice_in_dim(jnp.stack(members[::-1]), section_index, MICRO, 0).sum(0)
        for members in zip(*all_vectors)
    ]
    grad_inputs = chosen(returned)[None]
    return (mixed, grad_inputs) + shares(lefts, rights, vectors)


def shares(lefts, rights, vectors):
    groups = lax.axis_size("dp") // GROUP
    width = lefts[0].shape[1]
    if groups > 1:
        def ordered(member):
            split = member.reshape(member.shape[:-1] + (groups, LINE * PAIR, CORES, -1))
            moved = jnp.moveaxis(split, -4, -2)
            return moved.reshape(member.shape)

        lefts = [ordered(member) for member in lefts]
        vectors = [ordered(member) for member in vectors]
    vectors = jnp.concatenate([jnp.stack(vectors), jnp.zeros((4, width), F32)])
    block, vector_block = reduced(lefts, rights, vectors)
    core = lax.axis_index("dp") % CORES
    vector_block = lax.dynamic_slice_in_dim(vector_block[:4], core * block.shape[1], block.shape[1], 1)
    pieces = []
    offset = 0
    for member in rights:
        half = member.shape[1] // CORES
        part = block[:, :, offset : offset + half]
        pieces.append(jnp.concatenate([part[0], part[1]], axis=1))
        offset += half
    vector_block = vector_block.T
    if groups > 1:
        same = [[g * GROUP + j for g in range(groups)] for j in range(GROUP)]

        def summed(member):
            return lax.psum_scatter(
                member, "dp", scatter_dimension=0, axis_index_groups=same, tiled=True
            )

        pieces = [summed(member) for member in pieces]
        vector_block = summed(vector_block)
    down, up, out, qkv = pieces
    vector_block = vector_block.T
    return (
        qkv[None], out.T[None], up[None], down.T[None],
        vector_block[None, 0:2], vector_block[None, 2:4],
    )


def solution(mesh):
    placed = (P("dp", None),) * 2 + (P("section", None, None),) * 6
    return jax.shard_map(
        on_device,
        mesh=mesh,
        in_specs=placed,
        out_specs=(
            P("section", "dp", None),
            P("section", "dp", None),
            P("section", "dp", None),
            P("section", None, "dp"),
            P("section", "dp", None),
            P("section", None, "dp"),
            P("section", None, "dp"),
            P("section", None, "dp"),
        ),
        check_vma=False,
    )
```

```python
import math

import jax
import jax.numpy as jnp
from jax import lax
from jax.experimental import pallas as pl
from jax.experimental.pallas import tpu as pltpu
from jax.sharding import PartitionSpec as P

HEADS = 8
HEAD_DIM = 128
ITEM_LEN = 15
MICRO = 2
EPSILON = 1e-05

LINE, PAIR, CORES = 4, 2, 2
GROUP = LINE * PAIR * CORES
PANEL = 256
AHEAD = 4
RING = 4
MESH = pl.DeviceIdType.MESH
BF16, F32 = jnp.bfloat16, jnp.float32
DOWN, UP, OUT, QKV = range(4)


def dot(left, right):
    return jnp.dot(left, right, preferred_element_type=F32)


def dot_nt(left, right):
    return lax.dot_general(left, right, (((1,), (1,)), ((), ())), preferred_element_type=F32)


def dot_tn(left, right):
    return lax.dot_general(left, right, (((0,), (0,)), ((), ())), preferred_element_type=F32)


def normalized(values):
    centered = values - jnp.mean(values, axis=-1, keepdims=True)
    scale = lax.rsqrt(jnp.mean(centered * centered, axis=-1, keepdims=True) + EPSILON)
    return centered * scale, scale


def normalize_back(grad, unit, scale, gain):
    scaled = grad * gain
    along = jnp.mean(scaled * unit, axis=-1, keepdims=True)
    return scale * (scaled - jnp.mean(scaled, axis=-1, keepdims=True) - unit * along)


def gelu_parts(u):
    square = u * u
    inner = jnp.tanh(0.7978845608 * u * (1.0 + 0.044715 * square))
    return square, inner


def gelu(u):
    unused, inner = gelu_parts(u)
    return 0.5 * u * (1.0 + inner)


def gelu_slope(u):
    square, inner = gelu_parts(u)
    steep = 0.7978845608 * (1.0 + 3 * 0.044715 * square)
    return 0.5 * (1.0 + inner) + 0.5 * u * (1.0 - inner * inner) * steep


def layer_kernel(
    tokens_in, cotangent_in, gains, biases, w_qkv_in, w_out_in, w_up_in, w_down_in,
    mixed_out, grads_out, out, vector_out, buf, sem,
):
    h, e, result = buf["h"], buf["e"], buf["result"]
    w_qkv, w_out, w_up, w_down = buf["w_qkv"], buf["w_out"], buf["w_up"], buf["w_down"]
    left, e_half, right, twin_right = buf["left"], buf["e_half"], buf["right"], buf["twin_right"]
    act_beside, proj, middle, up = buf["act_beside"], buf["proj"], buf["middle"], buf["up"]
    probs, bias, dctx, vector = buf["probs"], buf["bias"], buf["dctx"], buf["vector"]
    parts, acc, fin = buf["parts"], buf["acc"], buf["fin"]
    pair_beside, pair_in, pair_across = buf["pair_beside"], buf["pair_in"], buf["pair_across"]
    vectors = buf["vectors"]

    all_rows, width = h.shape
    rows = all_rows // MICRO
    hidden = w_up.shape[1]
    chunk, half_chunk = acc.shape[2], acc.shape[2] // 2
    widths = (hidden, hidden, width, 3 * width)
    columns_at = (0, hidden, 2 * hidden, 2 * hidden + width)
    starts = [0]
    for member in widths:
        starts.append(starts[-1] + member // CORES // PANEL)
    panels, direct = starts[-1], starts[1]
    halves = [member // CORES for member in widths]
    twin_at = [start * PANEL for start in starts]

    section = lax.axis_index("section")
    place = lax.axis_index("dp")
    first = (place // GROUP) * GROUP
    mine = place - first
    z, y, core = mine // (PAIR * CORES), (mine // CORES) % PAIR, mine % CORES
    other_y, other_core = 1 - y, 1 - core
    far_side = z // 2
    is_end = (z == 0) | (z == LINE - 1)
    is_inner = jnp.logical_not(is_end)
    own = jnp.where(is_end, 0, 1)

    def numbered(zz):
        return zz + far_side * (LINE - 1 - 2 * zz)

    def device(zz, yy, cc):
        return (section, first + (zz * PAIR + yy) * CORES + cc)

    inner, end, across = (device(numbered(zz), y, core) for zz in (1, 0, 2))
    beside, twin = device(z, other_y, core), device(z, y, other_core)
    partner = (1 - section, place)
    leads = section == 0

    def send(source, target, key, index, to):
        return pltpu.make_async_remote_copy(
            src_ref=source, dst_ref=target, send_sem=sem[key + "_send"].at[index],
            recv_sem=sem[key + "_recv"].at[index], device_id=to, device_id_type=MESH,
        )

    def fetch(source, target, index):
        return pltpu.make_async_copy(source, target, sem["fetch"].at[index])

    def rows_of(m):
        return pl.ds(pl.multiple_of(m * rows, rows), rows)

    loads = [
        fetch(w_qkv_in, w_qkv, 0), fetch(w_out_in, w_out, 1), fetch(w_up_in, w_up, 2), fetch(w_down_in, w_down, 3),
    ]

    @pl.when(leads)
    def _():
        fetch(tokens_in, h, 4).start()

    @pl.when(jnp.logical_not(leads))
    def _():
        fetch(cotangent_in, e, 4).start()

    loads[0].start()
    barrier = pltpu.get_barrier_semaphore()
    pl.semaphore_signal(barrier, inc=1, device_id=partner, device_id_type=MESH)
    for step in range(1, GROUP):
        peer = (section, first + (mine + step) % GROUP)
        pl.semaphore_signal(barrier, inc=1, device_id=peer, device_id_type=MESH)

    row_ids = lax.broadcasted_iota(jnp.int32, (rows, rows), 0)
    col_ids = lax.broadcasted_iota(jnp.int32, (rows, rows), 1)
    seen = (row_ids // ITEM_LEN == col_ids // ITEM_LEN) & (col_ids <= row_ids)
    bias[...] = jnp.where(seen, 0.0, -1e30)
    vector[...] = jnp.zeros_like(vector)
    scale = 1.0 / math.sqrt(HEAD_DIM)

    pl.semaphore_wait(barrier, GROUP)
    fetch(tokens_in, h, 4).wait()


    def x_forward(m):
        return send(result.at[rows_of(m)], h.at[rows_of(m)], "x_forward", m, partner)

    def x_back(m):
        return send(h.at[rows_of(m)], e.at[rows_of(m)], "x_back", m, partner)

    def mixed_store(m):
        return pltpu.make_async_copy(result.at[rows_of(m)], mixed_out.at[rows_of(m)], sem["store"].at[0, m])

    def grads_store(m):
        return pltpu.make_async_copy(h.at[rows_of(m)], grads_out.at[rows_of(m)], sem["store"].at[1, m])

    def twin_left(which, m):
        return send(left.at[which - 1, 0, rows_of(m)], left.at[which - 1, 1, rows_of(m)],
                    "twin_left", (which - 1, m), twin)

    def twin_right_of(which, m):
        start = pl.multiple_of(columns_at[which] + other_core * halves[which], 128)
        return send(right.at[rows_of(m), pl.ds(start, halves[which])],
                    twin_right.at[rows_of(m), pl.ds(twin_at[which], halves[which])],
                    "twin_right", (which, m), twin)

    def act_beside_of(source, m):
        if source == 0:
            start = pl.multiple_of(core * halves[DOWN], 128)
            held = right.at[rows_of(m), pl.ds(start, halves[DOWN])]
        else:
            held = twin_right.at[rows_of(m), pl.ds(0, halves[DOWN])]
        return send(held, act_beside.at[source, rows_of(m)], "act_beside", (source, m), beside)

    def e_twin(m):
        return send(e_half.at[0, rows_of(m)], e_half.at[1, rows_of(m)], "e_half", (0, m), twin)

    def e_beside(m):
        return send(result.at[rows_of(m), pl.ds(0, width // 2)], e_half.at[2, rows_of(m)], "e_half", (1, m), beside)

    def e_onward(m):
        return send(e_half.at[2, rows_of(m)], e_half.at[3, rows_of(m)], "e_half", (2, m), twin)


    def once(m, load, following=()):
        @pl.when(m == 0)
        def _():
            loads[load].wait()
            for other in following:
                loads[other].start()

    def forward(m):
        at = rows_of(m)
        unit, unused = normalized(h[at].astype(F32))
        left[QKV - 1, 0, at] = (unit * gains[0:1] + biases[0:1]).astype(BF16)
        once(m, 0, (1, 2, 3))
        for part in range(3):
            cols = slice(part * width, (part + 1) * width)
            proj[at, cols] = dot(left[QKV - 1, 0, at], w_qkv[:, cols]).astype(BF16)
        twin_left(QKV, m).start()

        @pl.loop(0, HEADS // 2)
        def _(pair):
            for member in range(2):
                head = pair * 2 + member
                q, k, v = (
                    proj[at, pl.ds(pl.multiple_of(part * width + head * HEAD_DIM, HEAD_DIM), HEAD_DIM)]
                    for part in range(3)
                )
                scores = dot_nt(q, k) * scale + bias[...]
                weight = jnp.exp(scores - jnp.max(scores, axis=-1, keepdims=True))
                weight = weight / jnp.sum(weight, axis=-1, keepdims=True)
                weight = weight.astype(BF16)
                probs[m * HEADS + head] = weight
                cols = pl.ds(pl.multiple_of(columns_at[OUT] + head * HEAD_DIM, HEAD_DIM), HEAD_DIM)
                right[at, cols] = dot(weight, v).astype(BF16)

        once(m, 1)
        twin_right_of(OUT, m).start()
        attended = dot(right[at, columns_at[OUT] : columns_at[OUT] + width], w_out[...])
        middle[at] = h[at].astype(F32) + attended
        unit, unused = normalized(middle[at])
        left[UP - 1, 0, at] = (unit * gains[1:2] + biases[1:2]).astype(BF16)
        twin_left(UP, m).start()
        once(m, 2)
        for part in range(2):
            cols = slice(part * hidden // 2, (part + 1) * hidden // 2)
            upward = dot(left[UP - 1, 0, at], w_up[:, cols])
            up[at, cols] = upward.astype(BF16)
            right[at, cols] = gelu(upward).astype(BF16)
        twin_right_of(DOWN, m).start()
        act_beside_of(0, m).start()
        once(m, 3)
        result[at] = (middle[at] + dot(right[at, :hidden], w_down[...])).astype(BF16)
        mixed_store(m).start()

        @pl.when(leads)
        def _():
            x_forward(m).start()

        twin_right_of(DOWN, m).wait_recv()
        act_beside_of(1, m).start()

    def backward(m, hook):
        at = rows_of(m)
        mixed_store(m).wait()

        @pl.when(leads)
        def _():
            x_forward(m).wait_send()

        for zz in range(LINE):
            cols = pl.ds(zz * chunk, chunk)
            e_half[0, at, cols] = e[at, pl.ds(pl.multiple_of((zz * PAIR + y) * chunk, chunk), chunk)]
            result[at, cols] = e[at, pl.ds(pl.multiple_of((zz * PAIR + other_y) * chunk, chunk), chunk)]
        e_beside(m).start()
        e_twin(m).start()
        for part in range(2):
            cols = slice(part * hidden // 2, (part + 1) * hidden // 2)
            passed = dot_nt(e[at], w_down[cols])
            slope = gelu_slope(up[at, cols].astype(F32))
            here = slice(columns_at[UP] + cols.start, columns_at[UP] + cols.stop)
            right[at, here] = (passed * slope).astype(BF16)
        twin_right_of(UP, m).start()
        grad = dot_nt(right[at, columns_at[UP] : columns_at[UP] + hidden], w_up[...])
        unit, size = normalized(middle[at])
        vector[1:2] += jnp.sum(grad * unit, axis=0, keepdims=True)
        vector[3:4] += jnp.sum(grad, axis=0, keepdims=True)
        middle[at] = e[at].astype(F32) + normalize_back(grad, unit, size, gains[1:2])
        left[OUT - 1, 0, at] = middle[at].astype(BF16)
        twin_left(OUT, m).start()
        dctx[...] = dot_nt(left[OUT - 1, 0, at], w_out[...]).astype(BF16)
        hook(m)

        @pl.loop(0, HEADS // 2)
        def _(pair):
            for member in range(2):
                head = pair * 2 + member
                q, k, v = (
                    proj[at, pl.ds(pl.multiple_of(part * width + head * HEAD_DIM, HEAD_DIM), HEAD_DIM)]
                    for part in range(3)
                )
                grad_ctx = dctx[:, pl.ds(pl.multiple_of(head * HEAD_DIM, HEAD_DIM), HEAD_DIM)]
                weight = probs[m * HEADS + head]
                grad_weight = dot_nt(grad_ctx, v)
                grad_v = dot_tn(weight, grad_ctx)
                weight = weight.astype(F32)
                total = jnp.sum(weight * grad_weight, axis=-1, keepdims=True)
                grad_scores = (weight * (grad_weight - total)).astype(BF16)
                grad_q = dot(grad_scores, k) * scale
                grad_k = dot_tn(grad_scores, q) * scale
                for part, value in enumerate((grad_q, grad_k, grad_v)):
                    start = columns_at[QKV] + part * width + head * HEAD_DIM
                    right[at, pl.ds(pl.multiple_of(start, HEAD_DIM), HEAD_DIM)] = value.astype(BF16)

        twin_right_of(QKV, m).start()
        grad = dot_nt(right[at, columns_at[QKV] : columns_at[QKV] + 3 * width], w_qkv[...])
        unit, size = normalized(h[at].astype(F32))
        vector[0:1] += jnp.sum(grad * unit, axis=0, keepdims=True)
        vector[2:3] += jnp.sum(grad, axis=0, keepdims=True)
        h[at] = (middle[at] + normalize_back(grad, unit, size, gains[0:1])).astype(BF16)
        grads_store(m).start()

        @pl.when(jnp.logical_not(leads))
        def _():
            x_back(m).start()


    def beside_of(p):
        i = p - direct
        return send(parts.at[i % AHEAD, :, other_y], pair_beside.at[i % (2 * AHEAD)], "pair_beside", i, beside)

    def in_of(p):
        return send(acc.at[p % RING, pl.ds(1, 3)], pair_in.at[p % RING], "pair_in", p, inner)

    def across_of(p):
        return send(acc.at[p % RING, pl.ds(2, 2)], pair_across.at[p % RING], "pair_across", p, across)

    def out_of(p):
        return send(acc.at[p % RING, 0], pair_in.at[p % RING, 0], "pair_out", p, end)

    def fin_of(p):
        return send(fin.at[p % RING], out.at[core, :, pl.ds(pl.multiple_of(p * PANEL, PANEL), PANEL)], "fin", p, twin)

    def add(target, *refs):
        total = target[...].astype(F32)
        for ref in refs:
            total = total + ref[...].astype(F32)
        target[...] = total.astype(BF16)

    def own_columns(p):
        place_of = p * PANEL + core * halves[0]
        for i in (1, 2, 3):
            shift = (columns_at[i] - twin_at[i] + core * halves[i]) - (
                columns_at[i - 1] - twin_at[i - 1] + core * halves[i - 1])
            place_of = place_of + jnp.where(p >= starts[i], shift, 0)
        return pl.ds(pl.multiple_of(place_of, 128), PANEL)

    def twin_columns(p):
        return pl.ds(pl.multiple_of(p * PANEL, PANEL), PANEL)

    def wait_for(which):
        for m in range(MICRO):
            twin_left(which, m).wait_recv()
            twin_right_of(which, m).wait_recv()

    def start_panel(p):
        which = 0
        for i in (OUT, QKV):
            which = which + (p >= starts[i]).astype(jnp.int32)

            @pl.when(p == starts[i])
            def _(i=i):
                wait_for(i)

        total = dot_tn(left[which, 0], right[:, own_columns(p)]) + dot_tn(left[which, 1], twin_right[:, twin_columns(p)])
        total = total.astype(BF16).reshape(parts.shape[1:])
        for zz in range(LINE):
            parts[(p - direct) % AHEAD, numbered(zz)] = total[zz]
        beside_of(p).start()

    def early():
        wait_for(UP)

        @pl.loop(direct, direct + AHEAD)
        def _(p):
            start_panel(p)

        for m in range(MICRO):
            e_beside(m).wait_recv()
            e_onward(m).start()
        for m in range(MICRO):
            e_twin(m).wait_recv()
            act_beside_of(0, m).wait_recv()
            act_beside_of(1, m).wait_recv()
            e_onward(m).wait_recv()

        @pl.loop(0, direct)
        def _(p):
            total = dot_tn(e_half[0], right[:, own_columns(p)]) + dot_tn(e_half[1], twin_right[:, twin_columns(p)])
            for source in range(2):
                total = total + dot_tn(e_half[2 + source], act_beside[source, :, twin_columns(p)])
            total = total.astype(BF16).reshape(acc.shape[1:])
            for zz in range(LINE):
                acc[p % RING, numbered(zz)] = total[zz]

            @pl.when(is_end & (p < 2))
            def _():
                in_of(p).start()

    def proceed(t):
        @pl.when((t < direct - 2) & is_end)
        def _():
            in_of(t + 2).start()

        @pl.when((t >= direct) & (t < panels))
        def _():
            i = t - direct
            beside_of(t).wait()
            for d in range(LINE):
                total = parts[i % AHEAD, d, y].astype(F32) + pair_beside[i % (2 * AHEAD), d].astype(F32)
                acc[t % RING, d] = total.astype(BF16)

            @pl.when(is_end)
            def _():
                in_of(t).start()

            @pl.when(t + AHEAD < panels)
            def _():
                start_panel(t + AHEAD)

        p = t - 1

        @pl.when((p >= 0) & (p < panels) & is_inner)
        def _():
            in_of(p).wait_recv()
            add(acc.at[p % RING, pl.ds(2, 2)], pair_in.at[p % RING, pl.ds(1, 2)])
            across_of(p).start()
            add(acc.at[p % RING, 1], pair_in.at[p % RING, 0])

        q = t - 2

        @pl.when((q >= 0) & (q < panels) & is_inner)
        def _():
            across_of(q).wait_recv()
            add(acc.at[q % RING, 0], pair_across.at[q % RING, 1])
            out_of(q).start()
            add(acc.at[q % RING, 1], pair_across.at[q % RING, 0])

        r = t - 3

        @pl.when(r >= 0)
        def _():
            @pl.when(is_end)
            def _():
                out_of(r).wait_recv()
                add(acc.at[r % RING, 0], pair_in.at[r % RING, 0])
                in_of(r).wait_send()

            @pl.when(is_inner)
            def _():
                across_of(r).wait_send()
                out_of(r).wait_send()

            def block(which):
                return acc[r % RING, own, pl.ds(pl.multiple_of(which * half_chunk, half_chunk), half_chunk)].astype(F32)

            @pl.when(r >= RING)
            def _():
                fin_of(r - RING).wait_send()

            fin[r % RING] = block(other_core)
            fin_of(r).start()
            out[core, :, twin_columns(r)] = block(core)


    def hook(m):
        @pl.when((m == MICRO - 1) & leads)
        def _():
            early()

    @pl.loop(0, 2 * MICRO)
    def _(step):
        m = step % MICRO

        @pl.when(step < MICRO)
        def _():
            @pl.when(jnp.logical_not(leads))
            def _():
                x_forward(m).wait_recv()

            forward(m)

        @pl.when(leads == (step >= MICRO))
        def _():
            @pl.when(leads)
            def _():
                x_back(m).wait_recv()

            backward(m, hook)

    def send_vector(step):
        peer = (mine + step) % GROUP
        start = pl.multiple_of((peer // CORES) * chunk, chunk)
        return pltpu.make_async_remote_copy(
            src_ref=vector.at[:, pl.ds(start, chunk)], dst_ref=vectors.at[mine],
            send_sem=sem["vector_send"].at[step], recv_sem=sem["vector_recv"].at[mine],
            device_id=(section, first + peer), device_id_type=MESH,
        )

    @pl.loop(1, GROUP)
    def _(step):
        send_vector(step).start()

    @pl.when(jnp.logical_not(leads))
    def _():
        early()

    @pl.loop(0, panels + 3)
    def _(t):
        proceed(t)

    vector_total = vector[:, pl.ds(pl.multiple_of((mine // CORES) * chunk, chunk), chunk)]
    for step in range(1, GROUP):
        sender = (mine + step) % GROUP
        pltpu.make_async_remote_copy(
            src_ref=vector.at[:, pl.ds(0, chunk)], dst_ref=vectors.at[sender],
            send_sem=sem["vector_send"].at[step], recv_sem=sem["vector_recv"].at[sender],
            device_id=twin, device_id_type=MESH,
        ).wait_recv()
        vector_total = vector_total + vectors[sender]
    vector_out[...] = vector_total

    @pl.loop(1, GROUP)
    def _(step):
        send_vector(step).wait_send()

    for m in range(MICRO):
        for which in (UP, OUT, QKV):
            twin_left(which, m).wait_send()
        for which in range(4):
            twin_right_of(which, m).wait_send()
        for source in range(2):
            act_beside_of(source, m).wait_send()
        e_twin(m).wait_send()
        e_beside(m).wait_send()
        e_onward(m).wait_send()
        grads_store(m).wait()

        @pl.when(jnp.logical_not(leads))
        def _(m=m):
            x_back(m).wait_send()

    @pl.loop(0, panels)
    def _(p):
        fin_of(p).wait_recv()

    @pl.loop(panels - RING, panels)
    def _(p):
        fin_of(p).wait_send()


def layers(tokens, cotangent, gains, biases, w_qkv, w_out, w_up, w_down):
    all_rows, width = tokens.shape
    hidden = w_up.shape[1]
    rows = all_rows // MICRO
    columns = 2 * hidden + 4 * width
    panels = columns // CORES // PANEL
    direct = hidden // CORES // PANEL
    pairs = panels - direct
    chunk = width // (LINE * PAIR)
    dma = pltpu.SemaphoreType.DMA
    shapes = {
        "h": ((all_rows, width), BF16),
        "e": ((all_rows, width), BF16),
        "result": ((all_rows, width), BF16),
        "w_qkv": (w_qkv.shape, BF16),
        "w_out": (w_out.shape, BF16),
        "w_up": (w_up.shape, BF16),
        "w_down": (w_down.shape, BF16),
        "left": ((3, CORES, all_rows, width), BF16),
        "e_half": ((4, all_rows, width // 2), BF16),
        "right": ((all_rows, columns), BF16),
        "twin_right": ((all_rows, columns // CORES), BF16),
        "act_beside": ((2, all_rows, hidden // CORES), BF16),
        "proj": ((all_rows, 3 * width), BF16),
        "middle": ((all_rows, width), F32),
        "up": ((all_rows, hidden), BF16),
        "probs": ((MICRO * HEADS, rows, rows), BF16),
        "bias": ((rows, rows), F32),
        "dctx": ((rows, width), BF16),
        "vector": ((8, width), F32),
        "parts": ((AHEAD, LINE, PAIR, chunk, PANEL), BF16),
        "acc": ((RING, LINE, chunk, PANEL), BF16),
        "fin": ((RING, chunk // 2, PANEL), F32),
        "pair_beside": ((2 * AHEAD, LINE, chunk, PANEL), BF16),
        "pair_in": ((RING, 3, chunk, PANEL), BF16),
        "pair_across": ((RING, 2, chunk, PANEL), BF16),
        "vectors": ((GROUP, 8, chunk), F32),
    }
    exchanges = {
        "x_forward": (MICRO,), "x_back": (MICRO,), "twin_left": (3, MICRO), "twin_right": (4, MICRO),
        "act_beside": (2, MICRO), "e_half": (3, MICRO), "pair_beside": (pairs,), "pair_in": (panels,),
        "pair_across": (panels,), "pair_out": (panels,), "fin": (panels,), "vector": (GROUP,),
    }
    semaphores = {"fetch": dma((5,)), "store": dma((2, MICRO))}
    for key, count in exchanges.items():
        semaphores[key + "_send"] = dma(count)
        semaphores[key + "_recv"] = dma(count)
    anywhere = pl.BlockSpec(memory_space=pl.ANY)
    in_vmem = pl.BlockSpec(memory_space=pltpu.VMEM)
    return pl.pallas_call(
        layer_kernel,
        out_shape=(
            jax.ShapeDtypeStruct((all_rows, width), BF16),
            jax.ShapeDtypeStruct((all_rows, width), BF16),
            jax.ShapeDtypeStruct((CORES, chunk // 2, columns // CORES), F32),
            jax.ShapeDtypeStruct((8, chunk), F32),
        ),
        in_specs=[anywhere] * 2 + [in_vmem] * 2 + [anywhere] * 4,
        out_specs=(anywhere, anywhere, in_vmem, in_vmem),
        scratch_shapes=[{key: pltpu.VMEM(*shape) for key, shape in shapes.items()}, semaphores],
        compiler_params=pltpu.CompilerParams(
            collective_id=1, has_side_effects=True, vmem_limit_bytes=64 * 2**20
        ),
        name="relay_layers",
    )(tokens, cotangent, gains, biases, w_qkv, w_out, w_up, w_down)


def reordered(member, axis, groups, back=False):
    shape = member.shape
    row = shape[axis] // (groups * GROUP)
    split = (GROUP, groups, row) if back else (groups, GROUP, row)
    apart = member.reshape(shape[:axis] + split + shape[axis + 1 :])
    return jnp.swapaxes(apart, axis, axis + 1).reshape(shape)


def on_device(tokens, cotangent, norm_gains, norm_biases, w_qkv, w_out, w_up, w_down):
    hidden, width = w_up.shape[2], tokens.shape[1]
    operands = (tokens, cotangent, norm_gains[0], norm_biases[0], w_qkv[0], w_out[0], w_up[0], w_down[0])
    groups = lax.axis_size("dp") // GROUP
    if groups > 1:
        axes = (1, 1, 1, 1, 0, 1, 0, 1)
        operands = tuple(reordered(member, axis, groups) for member, axis in zip(operands, axes))
    mixed, grads, block, vector_block = layers(*operands)
    core = lax.axis_index("dp") % CORES
    share = block.shape[1]
    vector_block = lax.dynamic_slice_in_dim(vector_block[:4], core * share, share, 1)
    pieces = []
    offset = 0
    for member in (hidden, hidden, width, 3 * width):
        half = member // CORES
        part = block[:, :, offset : offset + half]
        pieces.append(jnp.concatenate([part[0], part[1]], axis=1))
        offset += half
    if groups > 1:
        mixed, grads = (reordered(member, 1, groups, back=True) for member in (mixed, grads))
        same = [[g * GROUP + j for g in range(groups)] for j in range(GROUP)]

        def summed(member):
            return lax.psum_scatter(member, "dp", scatter_dimension=0, axis_index_groups=same, tiled=True)

        pieces = [summed(member) for member in pieces]
        vector_block = summed(vector_block.T).T
    down, up, out, qkv = pieces
    return (
        mixed[None], grads[None], qkv[None], out.T[None], up[None], down.T[None],
        vector_block[None, 0:2], vector_block[None, 2:4],
    )


def solution(mesh):
    placed = (P("dp", None),) * 2 + (P("section", None, None),) * 6
    return jax.shard_map(
        on_device,
        mesh=mesh,
        in_specs=placed,
        out_specs=(
            P("section", "dp", None),
            P("section", "dp", None),
            P("section", "dp", None),
            P("section", None, "dp"),
            P("section", "dp", None),
            P("section", None, "dp"),
            P("section", None, "dp"),
            P("section", None, "dp"),
        ),
        check_vma=False,
    )
```

```python
import math

import jax
import jax.numpy as jnp
from jax import lax
from jax.experimental import pallas as pl
from jax.experimental.pallas import tpu as pltpu
from jax.sharding import PartitionSpec as P

HEADS = 8
HEAD_DIM = 128
ITEM_LEN = 15
MICRO = 2
EPSILON = 1e-05

LINE, PAIR, CORES = 4, 2, 2
GROUP = LINE * PAIR * CORES
PANEL = 256
AHEAD = 4
RING = 4
MESH = pl.DeviceIdType.MESH
BF16, F32 = jnp.bfloat16, jnp.float32
DOWN, UP, OUT, QKV = range(4)


def dot(left, right):
    return jnp.dot(left, right, preferred_element_type=F32)


def dot_nt(left, right):
    return lax.dot_general(left, right, (((1,), (1,)), ((), ())), preferred_element_type=F32)


def dot_tn(left, right):
    return lax.dot_general(left, right, (((0,), (0,)), ((), ())), preferred_element_type=F32)


def normalized(values):
    centered = values - jnp.mean(values, axis=-1, keepdims=True)
    scale = lax.rsqrt(jnp.mean(centered * centered, axis=-1, keepdims=True) + EPSILON)
    return centered * scale, scale


def normalize_back(grad, unit, scale, gain):
    scaled = grad * gain
    along = jnp.mean(scaled * unit, axis=-1, keepdims=True)
    return scale * (scaled - jnp.mean(scaled, axis=-1, keepdims=True) - unit * along)


def gelu_and_slope(u):
    square = u * u
    inner = jnp.tanh(u * (0.7978845608 + 0.7978845608 * 0.044715 * square))
    part = 0.5 + 0.5 * inner
    steep = 0.5 * 0.7978845608 + 1.5 * 0.7978845608 * 0.044715 * square
    return u * part, part + u * (1.0 - inner * inner) * steep


def layer_kernel(
    tokens_in, cotangent_in, gains, biases, w_qkv_in, w_out_in, w_up_in, w_down_in,
    mixed_out, grads_out, out, vector_out, buf, sem,
):
    h, e, e_other, result = buf["h"], buf["e"], buf["e_other"], buf["result"]
    w_qkv, w_out, w_up, w_down = buf["w_qkv"], buf["w_out"], buf["w_up"], buf["w_down"]
    left, e_half, right, twin_right = buf["left"], buf["e_half"], buf["right"], buf["twin_right"]
    act_beside, proj, middle, slopes = buf["act_beside"], buf["proj"], buf["middle"], buf["slopes"]
    probs, bias, dctx, vector = buf["probs"], buf["bias"], buf["dctx"], buf["vector"]
    parts, acc, fin = buf["parts"], buf["acc"], buf["fin"]
    pair_beside, pair_in, pair_across = buf["pair_beside"], buf["pair_in"], buf["pair_across"]
    vectors = buf["vectors"]

    all_rows, width = h.shape
    rows = all_rows // MICRO
    front = (rows // 2 + 15) // 16 * 16
    hidden = w_up.shape[1]
    chunk, half_chunk = acc.shape[2], acc.shape[2] // 2
    widths = (hidden, hidden, width, 3 * width)
    columns_at = (0, hidden, 2 * hidden, 2 * hidden + width)
    starts = [0]
    for member in widths:
        starts.append(starts[-1] + member // CORES // PANEL)
    panels, direct = starts[-1], starts[1]
    halves = [member // CORES for member in widths]
    twin_at = [start * PANEL for start in starts]

    section = lax.axis_index("section")
    place = lax.axis_index("dp")
    first = (place // GROUP) * GROUP
    mine = place - first
    z, y, core = mine // (PAIR * CORES), (mine // CORES) % PAIR, mine % CORES
    other_y, other_core = 1 - y, 1 - core
    far_side = z // 2
    is_end = (z == 0) | (z == LINE - 1)
    is_inner = jnp.logical_not(is_end)
    own = jnp.where(is_end, 0, 1)

    def numbered(zz):
        return zz + far_side * (LINE - 1 - 2 * zz)

    def device(zz, yy, cc):
        return (section, first + (zz * PAIR + yy) * CORES + cc)

    inner, end, across = (device(numbered(zz), y, core) for zz in (1, 0, 2))
    beside, twin = device(z, other_y, core), device(z, y, other_core)
    partner = (1 - section, place)
    leads = section == 0

    def send(source, target, key, index, to):
        return pltpu.make_async_remote_copy(
            src_ref=source, dst_ref=target, send_sem=sem[key + "_send"].at[index],
            recv_sem=sem[key + "_recv"].at[index], device_id=to, device_id_type=MESH,
        )

    def fetch(source, target, index):
        return pltpu.make_async_copy(source, target, sem["fetch"].at[index])

    def rows_of(m):
        return pl.ds(pl.multiple_of(m * rows, rows), rows)

    loads = [fetch(w_out_in, w_out, 0), fetch(w_up_in, w_up, 1), fetch(w_down_in, w_down, 2)]
    loads_qkv = [
        fetch(w_qkv_in.at[:, pl.ds(part * width, width)], w_qkv.at[:, pl.ds(part * width, width)], 3 + part)
        for part in range(3)
    ]
    load_rows = fetch(tokens_in, h, 6)

    @pl.when(leads)
    def _():
        load_rows.start()

    @pl.when(jnp.logical_not(leads))
    def _():
        fetch(cotangent_in, e, 6).start()

    for load in loads_qkv:
        load.start()
    barrier = pltpu.get_barrier_semaphore()
    pl.semaphore_signal(barrier, inc=1, device_id=partner, device_id_type=MESH)
    for step in range(1, GROUP):
        peer = (section, first + (mine + step) % GROUP)
        pl.semaphore_signal(barrier, inc=1, device_id=peer, device_id_type=MESH)

    row_ids = lax.broadcasted_iota(jnp.int32, (rows, rows), 0)
    col_ids = lax.broadcasted_iota(jnp.int32, (rows, rows), 1)
    seen = (row_ids // ITEM_LEN == col_ids // ITEM_LEN) & (col_ids <= row_ids)
    bias[...] = jnp.where(seen, 0.0, -1e30)
    vector[...] = jnp.zeros_like(vector)
    proj[front:rows, width:] = jnp.zeros((rows - front, 2 * width), BF16)
    scale = 1.0 / math.sqrt(HEAD_DIM)


    spans = ((0, front), (front, rows), (rows, 2 * rows))

    def x_forward(i):
        at = pl.ds(spans[i][0], spans[i][1] - spans[i][0])
        return send(result.at[at], h.at[at], "x_forward", i, partner)

    def x_back(m):
        return send(h.at[rows_of(m)], e.at[rows_of(m)], "x_back", m, partner)

    def mixed_store(m):
        return pltpu.make_async_copy(result.at[rows_of(m)], mixed_out.at[rows_of(m)], sem["store"].at[0, m])

    def grads_store(m):
        return pltpu.make_async_copy(h.at[rows_of(m)], grads_out.at[rows_of(m)], sem["store"].at[1, m])

    def twin_left(which, m):
        return send(left.at[which - 1, 0, rows_of(m)], left.at[which - 1, 1, rows_of(m)],
                    "twin_left", (which - 1, m), twin)

    def twin_right_of(which, m):
        start = pl.multiple_of(columns_at[which] + other_core * halves[which], 128)
        return send(right.at[rows_of(m), pl.ds(start, halves[which])],
                    twin_right.at[rows_of(m), pl.ds(twin_at[which], halves[which])],
                    "twin_right", (which, m), twin)

    def act_beside_of(source, m):
        if source == 0:
            start = pl.multiple_of(core * halves[DOWN], 128)
            held = right.at[rows_of(m), pl.ds(start, halves[DOWN])]
        else:
            held = twin_right.at[rows_of(m), pl.ds(0, halves[DOWN])]
        return send(held, act_beside.at[source, rows_of(m)], "act_beside", (source, m), beside)

    def e_twin(m):
        return send(e_half.at[0, rows_of(m)], e_half.at[1, rows_of(m)], "e_half", (0, m), twin)

    def e_beside(m):
        return send(e_other.at[rows_of(m)], e_half.at[2, rows_of(m)], "e_half", (1, m), beside)

    def e_onward(m):
        return send(e_half.at[2, rows_of(m)], e_half.at[3, rows_of(m)], "e_half", (2, m), twin)


    def attend(i, load=False):
        low, high = spans[i]
        at, m = slice(low, high), low // rows
        whole = slice(m * rows, (m + 1) * rows)
        unit, unused = normalized(h[at].astype(F32))
        left[QKV - 1, 0, at] = (unit * gains[0:1] + biases[0:1]).astype(BF16)
        for part in range(3):
            cols = slice(part * width, (part + 1) * width)
            if load:
                loads_qkv[part].wait()
                loads[part].start()
            proj[at, cols] = dot(left[QKV - 1, 0, at], w_qkv[:, cols]).astype(BF16)
        for head in range(HEADS):
            q, k, v = (proj[whole, part * width + head * HEAD_DIM : part * width + (head + 1) * HEAD_DIM] for part in range(3))
            scores = dot_nt(q, k) * scale + bias[...]
            weight = jnp.exp(scores - jnp.max(scores, axis=-1, keepdims=True))
            weight = weight / jnp.sum(weight, axis=-1, keepdims=True)
            weight = weight.astype(BF16)
            probs[m * HEADS + head] = weight
            cols = slice(columns_at[OUT] + head * HEAD_DIM, columns_at[OUT] + (head + 1) * HEAD_DIM)
            right[whole, cols] = dot(weight, v).astype(BF16)

    def forward(i, load=False):
        at = slice(*spans[i])
        if load:
            loads[0].wait()
        attended = dot(right[at, columns_at[OUT] : columns_at[OUT] + width], w_out[...])
        middle[at] = h[at].astype(F32) + attended
        unit, unused = normalized(middle[at])
        left[UP - 1, 0, at] = (unit * gains[1:2] + biases[1:2]).astype(BF16)
        if load:
            loads[1].wait()
        for part in range(2):
            cols = slice(part * hidden // 2, (part + 1) * hidden // 2)
            upward = dot(left[UP - 1, 0, at], w_up[:, cols])
            active, slope = gelu_and_slope(upward)
            slopes[at, cols] = slope.astype(BF16)
            right[at, cols] = active.astype(BF16)
        if load:
            loads[2].wait()
        result[at] = (middle[at] + dot(right[at, :hidden], w_down[...])).astype(BF16)

        @pl.when(leads)
        def _():
            x_forward(i).start()

    def share(m):
        mixed_store(m).start()
        twin_right_of(DOWN, m).start()
        act_beside_of(0, m).start()
        twin_right_of(OUT, m).start()
        twin_left(QKV, m).start()
        twin_left(UP, m).start()

    def share_on(m):
        twin_right_of(DOWN, m).wait_recv()
        act_beside_of(1, m).start()

    def spread(m):
        at = rows_of(m)
        for zz in range(LINE):
            cols = pl.ds(zz * chunk, chunk)
            e_half[0, at, cols] = e[at, pl.ds(pl.multiple_of((zz * PAIR + y) * chunk, chunk), chunk)]
            e_other[at, cols] = e[at, pl.ds(pl.multiple_of((zz * PAIR + other_y) * chunk, chunk), chunk)]
        e_beside(m).start()
        e_twin(m).start()

    def backward(m, hook):
        at = rows_of(m)

        @pl.when(leads)
        def _():
            spread(m)

        for part in range(2):
            cols = slice(part * hidden // 2, (part + 1) * hidden // 2)
            passed = dot_nt(e[at], w_down[cols])
            slope = slopes[at, cols].astype(F32)
            here = slice(columns_at[UP] + cols.start, columns_at[UP] + cols.stop)
            right[at, here] = (passed * slope).astype(BF16)
        twin_right_of(UP, m).start()

        @pl.when(jnp.logical_not(leads))
        def _():
            share_on(m)

        grad = dot_nt(right[at, columns_at[UP] : columns_at[UP] + hidden], w_up[...])
        unit, size = normalized(middle[at])
        vector[1:2] += jnp.sum(grad * unit, axis=0, keepdims=True)
        vector[3:4] += jnp.sum(grad, axis=0, keepdims=True)
        middle[at] = e[at].astype(F32) + normalize_back(grad, unit, size, gains[1:2])
        left[OUT - 1, 0, at] = middle[at].astype(BF16)
        twin_left(OUT, m).start()
        dctx[...] = dot_nt(left[OUT - 1, 0, at], w_out[...]).astype(BF16)
        hook(m)

        for head in range(HEADS):
            q, k, v = (proj[at, part * width + head * HEAD_DIM : part * width + (head + 1) * HEAD_DIM] for part in range(3))
            grad_ctx = dctx[:, head * HEAD_DIM : (head + 1) * HEAD_DIM]
            weight = probs[m * HEADS + head]
            grad_weight = dot_nt(grad_ctx, v)
            grad_v = dot_tn(weight, grad_ctx)
            weight = weight.astype(F32)
            total = jnp.sum(weight * grad_weight, axis=-1, keepdims=True)
            grad_scores = (weight * (grad_weight - total)).astype(BF16)
            grad_q = dot(grad_scores, k) * scale
            grad_k = dot_tn(grad_scores, q) * scale
            for part, value in enumerate((grad_q, grad_k, grad_v)):
                start = columns_at[QKV] + part * width + head * HEAD_DIM
                right[at, start : start + HEAD_DIM] = value.astype(BF16)

        twin_right_of(QKV, m).start()
        grad = dot_nt(right[at, columns_at[QKV] : columns_at[QKV] + 3 * width], w_qkv[...])
        unit, size = normalized(h[at].astype(F32))
        vector[0:1] += jnp.sum(grad * unit, axis=0, keepdims=True)
        vector[2:3] += jnp.sum(grad, axis=0, keepdims=True)
        h[at] = (middle[at] + normalize_back(grad, unit, size, gains[0:1])).astype(BF16)
        grads_store(m).start()

        @pl.when(jnp.logical_not(leads))
        def _():
            x_back(m).start()


    def beside_of(p):
        i = p - direct
        return send(parts.at[i % AHEAD, :, other_y], pair_beside.at[i % (2 * AHEAD)], "pair_beside", i, beside)

    def in_of(p):
        return send(acc.at[p % RING, pl.ds(1, 3)], pair_in.at[p % RING], "pair_in", p, inner)

    def across_of(p):
        return send(acc.at[p % RING, pl.ds(2, 2)], pair_across.at[p % RING], "pair_across", p, across)

    def out_of(p):
        return send(acc.at[p % RING, 0], pair_in.at[p % RING, 0], "pair_out", p, end)

    def fin_of(p):
        return send(fin.at[p % RING], out.at[core, :, pl.ds(pl.multiple_of(p * PANEL, PANEL), PANEL)], "fin", p, twin)

    def add(target, *refs):
        total = target[...].astype(F32)
        for ref in refs:
            total = total + ref[...].astype(F32)
        target[...] = total.astype(BF16)

    def own_columns(p):
        place_of = p * PANEL + core * halves[0]
        for i in (1, 2, 3):
            shift = (columns_at[i] - twin_at[i] + core * halves[i]) - (
                columns_at[i - 1] - twin_at[i - 1] + core * halves[i - 1])
            place_of = place_of + jnp.where(p >= starts[i], shift, 0)
        return pl.ds(pl.multiple_of(place_of, 128), PANEL)

    def twin_columns(p):
        return pl.ds(pl.multiple_of(p * PANEL, PANEL), PANEL)

    def wait_for(which):
        for m in range(MICRO):
            twin_left(which, m).wait_recv()
            twin_right_of(which, m).wait_recv()

    def start_panel(p):
        which = 0
        for i in (OUT, QKV):
            which = which + (p >= starts[i]).astype(jnp.int32)

            @pl.when(p == starts[i])
            def _(i=i):
                wait_for(i)

        total = dot_tn(left[which, 0], right[:, own_columns(p)]) + dot_tn(left[which, 1], twin_right[:, twin_columns(p)])
        total = total.astype(BF16).reshape(parts.shape[1:])
        for zz in range(LINE):
            parts[(p - direct) % AHEAD, numbered(zz)] = total[zz]
        beside_of(p).start()

    def early_up():
        wait_for(UP)

        @pl.loop(direct, direct + AHEAD)
        def _(p):
            start_panel(p)

    def early_down():
        for m in range(MICRO):
            e_beside(m).wait_recv()
            e_onward(m).start()
        for m in range(MICRO):
            e_twin(m).wait_recv()
            act_beside_of(0, m).wait_recv()
            act_beside_of(1, m).wait_recv()
            e_onward(m).wait_recv()

        @pl.loop(0, direct)
        def _(p):
            total = dot_tn(e_half[0], right[:, own_columns(p)]) + dot_tn(e_half[1], twin_right[:, twin_columns(p)])
            for source in range(2):
                total = total + dot_tn(e_half[2 + source], act_beside[source, :, twin_columns(p)])
            total = total.astype(BF16).reshape(acc.shape[1:])
            for zz in range(LINE):
                acc[p % RING, numbered(zz)] = total[zz]

            @pl.when(is_end & (p < 2))
            def _():
                in_of(p).start()

    def proceed(t):
        @pl.when((t < direct - 2) & is_end)
        def _():
            in_of(t + 2).start()

        @pl.when((t >= direct) & (t < panels))
        def _():
            i = t - direct
            beside_of(t).wait()
            for d in range(LINE):
                total = parts[i % AHEAD, d, y].astype(F32) + pair_beside[i % (2 * AHEAD), d].astype(F32)
                acc[t % RING, d] = total.astype(BF16)

            @pl.when(is_end)
            def _():
                in_of(t).start()

            @pl.when(t + AHEAD < panels)
            def _():
                start_panel(t + AHEAD)

        p = t - 1

        @pl.when((p >= 0) & (p < panels) & is_inner)
        def _():
            in_of(p).wait_recv()
            add(acc.at[p % RING, pl.ds(2, 2)], pair_in.at[p % RING, pl.ds(1, 2)])
            across_of(p).start()
            add(acc.at[p % RING, 1], pair_in.at[p % RING, 0])

        q = t - 2

        @pl.when((q >= 0) & (q < panels) & is_inner)
        def _():
            across_of(q).wait_recv()
            add(acc.at[q % RING, 0], pair_across.at[q % RING, 1])
            out_of(q).start()
            add(acc.at[q % RING, 1], pair_across.at[q % RING, 0])

        r = t - 3

        @pl.when(r >= 0)
        def _():
            @pl.when(is_end)
            def _():
                out_of(r).wait_recv()
                add(acc.at[r % RING, 0], pair_in.at[r % RING, 0])
                in_of(r).wait_send()

            @pl.when(is_inner)
            def _():
                across_of(r).wait_send()
                out_of(r).wait_send()

            def block(which):
                return acc[r % RING, own, pl.ds(pl.multiple_of(which * half_chunk, half_chunk), half_chunk)].astype(F32)

            @pl.when(r >= RING)
            def _():
                fin_of(r - RING).wait_send()

            fin[r % RING] = block(other_core)
            fin_of(r).start()
            out[core, :, twin_columns(r)] = block(core)


    def hook(m):
        @pl.when((m == MICRO - 1) & leads)
        def _():
            early_up()
            early_down()

    @pl.when(leads)
    def _():
        load_rows.wait()
        attend(0, load=True)

    pl.semaphore_wait(barrier, GROUP)

    @pl.when(jnp.logical_not(leads))
    def _():
        load_rows.wait()
        for m in range(MICRO):
            spread(m)
        x_forward(0).wait_recv()
        attend(0, load=True)

    forward(0, load=True)

    @pl.when(jnp.logical_not(leads))
    def _():
        x_forward(1).wait_recv()

    attend(1)
    forward(1)
    share(0)

    @pl.when(leads)
    def _():
        share_on(0)

    @pl.loop(0, MICRO + 1)
    def _(step):
        @pl.when(step == section)
        def _():
            @pl.when(jnp.logical_not(leads))
            def _():
                x_forward(2).wait_recv()

            attend(2)
            forward(2)
            share(1)

            @pl.when(leads)
            def _():
                share_on(1)

        @pl.when(step != section)
        def _():
            m = step // 2

            @pl.when(leads)
            def _():
                x_back(m).wait_recv()

            backward(m, hook)

    def send_vector(step):
        peer = (mine + step) % GROUP
        start = pl.multiple_of((peer // CORES) * chunk, chunk)
        return pltpu.make_async_remote_copy(
            src_ref=vector.at[:, pl.ds(start, chunk)], dst_ref=vectors.at[mine],
            send_sem=sem["vector_send"].at[step], recv_sem=sem["vector_recv"].at[mine],
            device_id=(section, first + peer), device_id_type=MESH,
        )

    @pl.loop(1, GROUP)
    def _(step):
        send_vector(step).start()

    @pl.when(jnp.logical_not(leads))
    def _():
        early_down()
        early_up()

    @pl.loop(0, panels + 3)
    def _(t):
        proceed(t)

    vector_total = vector[:, pl.ds(pl.multiple_of((mine // CORES) * chunk, chunk), chunk)]
    for step in range(1, GROUP):
        sender = (mine + step) % GROUP
        pltpu.make_async_remote_copy(
            src_ref=vector.at[:, pl.ds(0, chunk)], dst_ref=vectors.at[sender],
            send_sem=sem["vector_send"].at[step], recv_sem=sem["vector_recv"].at[sender],
            device_id=twin, device_id_type=MESH,
        ).wait_recv()
        vector_total = vector_total + vectors[sender]
    vector_out[...] = vector_total

    @pl.loop(1, GROUP)
    def _(step):
        send_vector(step).wait_send()

    for m in range(MICRO):
        for which in (UP, OUT, QKV):
            twin_left(which, m).wait_send()
        for which in range(4):
            twin_right_of(which, m).wait_send()
        for source in range(2):
            act_beside_of(source, m).wait_send()
        e_twin(m).wait_send()
        e_beside(m).wait_send()
        e_onward(m).wait_send()
        grads_store(m).wait()
        mixed_store(m).wait()

        @pl.when(jnp.logical_not(leads))
        def _(m=m):
            x_back(m).wait_send()

    @pl.when(leads)
    def _():
        for i in range(len(spans)):
            x_forward(i).wait_send()

    @pl.loop(0, panels)
    def _(p):
        fin_of(p).wait_recv()

    @pl.loop(panels - RING, panels)
    def _(p):
        fin_of(p).wait_send()


def layers(tokens, cotangent, gains, biases, w_qkv, w_out, w_up, w_down):
    all_rows, width = tokens.shape
    hidden = w_up.shape[1]
    rows = all_rows // MICRO
    columns = 2 * hidden + 4 * width
    panels = columns // CORES // PANEL
    direct = hidden // CORES // PANEL
    pairs = panels - direct
    chunk = width // (LINE * PAIR)
    dma = pltpu.SemaphoreType.DMA
    shapes = {
        "h": ((all_rows, width), BF16),
        "e": ((all_rows, width), BF16),
        "e_other": ((all_rows, width // 2), BF16),
        "result": ((all_rows, width), BF16),
        "w_qkv": (w_qkv.shape, BF16),
        "w_out": (w_out.shape, BF16),
        "w_up": (w_up.shape, BF16),
        "w_down": (w_down.shape, BF16),
        "left": ((3, CORES, all_rows, width), BF16),
        "e_half": ((4, all_rows, width // 2), BF16),
        "right": ((all_rows, columns), BF16),
        "twin_right": ((all_rows, columns // CORES), BF16),
        "act_beside": ((2, all_rows, hidden // CORES), BF16),
        "proj": ((all_rows, 3 * width), BF16),
        "middle": ((all_rows, width), F32),
        "slopes": ((all_rows, hidden), BF16),
        "probs": ((MICRO * HEADS, rows, rows), BF16),
        "bias": ((rows, rows), F32),
        "dctx": ((rows, width), BF16),
        "vector": ((8, width), F32),
        "parts": ((AHEAD, LINE, PAIR, chunk, PANEL), BF16),
        "acc": ((RING, LINE, chunk, PANEL), BF16),
        "fin": ((RING, chunk // 2, PANEL), F32),
        "pair_beside": ((2 * AHEAD, LINE, chunk, PANEL), BF16),
        "pair_in": ((RING, 3, chunk, PANEL), BF16),
        "pair_across": ((RING, 2, chunk, PANEL), BF16),
        "vectors": ((GROUP, 8, chunk), F32),
    }
    exchanges = {
        "x_forward": (3,), "x_back": (MICRO,), "twin_left": (3, MICRO), "twin_right": (4, MICRO),
        "act_beside": (2, MICRO), "e_half": (3, MICRO), "pair_beside": (pairs,), "pair_in": (panels,),
        "pair_across": (panels,), "pair_out": (panels,), "fin": (panels,), "vector": (GROUP,),
    }
    semaphores = {"fetch": dma((7,)), "store": dma((2, MICRO))}
    for key, count in exchanges.items():
        semaphores[key + "_send"] = dma(count)
        semaphores[key + "_recv"] = dma(count)
    anywhere = pl.BlockSpec(memory_space=pl.ANY)
    in_vmem = pl.BlockSpec(memory_space=pltpu.VMEM)
    return pl.pallas_call(
        layer_kernel,
        out_shape=(
            jax.ShapeDtypeStruct((all_rows, width), BF16),
            jax.ShapeDtypeStruct((all_rows, width), BF16),
            jax.ShapeDtypeStruct((CORES, chunk // 2, columns // CORES), F32),
            jax.ShapeDtypeStruct((8, chunk), F32),
        ),
        in_specs=[anywhere] * 2 + [in_vmem] * 2 + [anywhere] * 4,
        out_specs=(anywhere, anywhere, in_vmem, in_vmem),
        scratch_shapes=[{key: pltpu.VMEM(*shape) for key, shape in shapes.items()}, semaphores],
        compiler_params=pltpu.CompilerParams(
            collective_id=1, has_side_effects=True, vmem_limit_bytes=64 * 2**20
        ),
        name="relay_layers",
    )(tokens, cotangent, gains, biases, w_qkv, w_out, w_up, w_down)


def results_kernel(
    mixed_in, grads_in, block_in, vectors_in, mixed, grads, down, up, out, qkv, gains, biases,
    rows, block, vectors, shares, sem,
):
    started = []

    def copy(source, target):
        started.append(pltpu.make_async_copy(source, target, sem.at[len(started)]))
        started[-1].start()
        return started[-1]

    fetches = [copy(block_in.at[core], block.at[core]) for core in range(CORES)]
    fetches.append(copy(vectors_in, vectors))
    fetches += [copy(ref, rows.at[i]) for i, ref in enumerate((mixed_in, grads_in))]
    stores = []
    for core in range(CORES):
        fetches[core].wait()
        offset = 0
        for ref in (down, up, out, qkv):
            half = ref.shape[1] // CORES
            stores.append(copy(block.at[core, :, pl.ds(offset, half)], ref.at[:, pl.ds(core * half, half)]))
            offset += half
    fetches[CORES].wait()
    share = gains.shape[1]
    mine = lax.axis_index("dp") % CORES
    for core in range(CORES):
        @pl.when(mine == core)
        def _(core=core):
            here = slice(core * share, (core + 1) * share)
            shares[0] = vectors[0:2, here]
            shares[1] = vectors[2:4, here]

    stores += [copy(shares.at[i], ref) for i, ref in enumerate((gains, biases))]
    for i, ref in enumerate((mixed, grads)):
        fetches[CORES + 1 + i].wait()
        stores.append(copy(rows.at[i], ref))
    for store in stores:
        store.wait()


def results(mixed, grads, block, vectors, hidden):
    width, share = mixed.shape[1], block.shape[1]
    anywhere = pl.BlockSpec(memory_space=pl.ANY)
    shapes = ((share, hidden), (share, hidden), (share, width), (share, 3 * width), (2, share), (2, share))
    mixed, grads, down, up, out, qkv, gains, biases = pl.pallas_call(
        results_kernel,
        out_shape=(jax.ShapeDtypeStruct(mixed.shape, BF16), jax.ShapeDtypeStruct(grads.shape, BF16))
        + tuple(jax.ShapeDtypeStruct(shape, F32) for shape in shapes),
        in_specs=[anywhere] * 4,
        out_specs=(anywhere,) * 8,
        scratch_shapes=[
            pltpu.VMEM((2,) + mixed.shape, BF16), pltpu.VMEM(block.shape, F32), pltpu.VMEM(vectors.shape, F32),
            pltpu.VMEM((2, 2, share), F32), pltpu.SemaphoreType.DMA((CORES + 3 + 4 * CORES + 4,)),
        ],
        compiler_params=pltpu.CompilerParams(vmem_limit_bytes=64 * 2**20),
        name="place_results",
    )(mixed, grads, block, vectors)
    return mixed, grads, qkv, out.T, up, down.T, gains, biases


def reordered(member, axis, groups, back=False):
    shape = member.shape
    row = shape[axis] // (groups * GROUP)
    split = (GROUP, groups, row) if back else (groups, GROUP, row)
    apart = member.reshape(shape[:axis] + split + shape[axis + 1 :])
    return jnp.swapaxes(apart, axis, axis + 1).reshape(shape)


def on_device(tokens, cotangent, norm_gains, norm_biases, w_qkv, w_out, w_up, w_down):
    hidden, width = w_up.shape[2], tokens.shape[1]
    operands = (tokens, cotangent, norm_gains[0], norm_biases[0], w_qkv[0], w_out[0], w_up[0], w_down[0])
    groups = lax.axis_size("dp") // GROUP
    if groups > 1:
        axes = (1, 1, 1, 1, 0, 1, 0, 1)
        operands = tuple(reordered(member, axis, groups) for member, axis in zip(operands, axes))
    mixed, grads, block, vector_block = layers(*operands)
    if groups == 1:
        return tuple(member[None] for member in results(mixed, grads, block, vector_block, hidden))
    core = lax.axis_index("dp") % CORES
    share = block.shape[1]
    vector_block = lax.dynamic_slice_in_dim(vector_block[:4], core * share, share, 1)
    pieces = []
    offset = 0
    for member in (hidden, hidden, width, 3 * width):
        half = member // CORES
        part = block[:, :, offset : offset + half]
        pieces.append(jnp.concatenate([part[0], part[1]], axis=1))
        offset += half
    mixed, grads = (reordered(member, 1, groups, back=True) for member in (mixed, grads))
    same = [[g * GROUP + j for g in range(groups)] for j in range(GROUP)]

    def summed(member):
        return lax.psum_scatter(member, "dp", scatter_dimension=0, axis_index_groups=same, tiled=True)

    pieces = [summed(member) for member in pieces]
    vector_block = summed(vector_block.T).T
    down, up, out, qkv = pieces
    return (
        mixed[None], grads[None], qkv[None], out.T[None], up[None], down.T[None],
        vector_block[None, 0:2], vector_block[None, 2:4],
    )


def solution(mesh):
    placed = (P("dp", None),) * 2 + (P("section", None, None),) * 6
    return jax.shard_map(
        on_device,
        mesh=mesh,
        in_specs=placed,
        out_specs=(
            P("section", "dp", None),
            P("section", "dp", None),
            P("section", "dp", None),
            P("section", None, "dp"),
            P("section", "dp", None),
            P("section", None, "dp"),
            P("section", None, "dp"),
            P("section", None, "dp"),
        ),
        check_vma=False,
    )
```

```python
import math

import jax
import jax.numpy as jnp
from jax import lax
from jax.experimental import pallas as pl
from jax.experimental.pallas import tpu as pltpu
from jax.sharding import PartitionSpec as P

HEADS = 8
HEAD_DIM = 128
ITEM_LEN = 15
MICRO = 2
EPSILON = 1e-05

LINE, PAIR, CORES = 4, 2, 2
GROUP = LINE * PAIR * CORES
PANEL = 256
STRIPS = 2
AHEAD = 8
LAG = 2
BEFORE_HEADS, BEFORE_LAST = 4, 5
RING = 8
FIRST = 4
LEAVING = 8
MESH = pl.DeviceIdType.MESH
BF16, F32 = jnp.bfloat16, jnp.float32
DOWN, UP, OUT, QKV = range(4)


def dot(left, right):
    return jnp.dot(left, right, preferred_element_type=F32)


def dot_nt(left, right):
    return lax.dot_general(left, right, (((1,), (1,)), ((), ())), preferred_element_type=F32)


def dot_tn(left, right):
    return lax.dot_general(left, right, (((0,), (0,)), ((), ())), preferred_element_type=F32)


def normalized(values):
    centered = values - jnp.mean(values, axis=-1, keepdims=True)
    scale = lax.rsqrt(jnp.mean(centered * centered, axis=-1, keepdims=True) + EPSILON)
    return centered * scale, scale


def normalize_back(grad, unit, scale, gain):
    scaled = grad * gain
    along = jnp.mean(scaled * unit, axis=-1, keepdims=True)
    return scale * (scaled - jnp.mean(scaled, axis=-1, keepdims=True) - unit * along)


def gelu_and_slope(u):
    square = u * u
    inner = jnp.tanh(u * (0.7978845608 + 0.7978845608 * 0.044715 * square))
    part = 0.5 + 0.5 * inner
    steep = 0.5 * 0.7978845608 + 1.5 * 0.7978845608 * 0.044715 * square
    return u * part, part + u * (1.0 - inner * inner) * steep


def layer_kernel(
    tokens_in, cotangent_in, gains, biases, w_qkv_in, w_out_in, w_up_in, w_down_in,
    mixed_out, grads_out, out, vector_out, buf, sem,
):
    h, e, e_other, result = buf["h"], buf["e"], buf["e_other"], buf["result"]
    w_qkv, w_out, w_up, w_down = buf["w_qkv"], buf["w_out"], buf["w_up"], buf["w_down"]
    left, e_half, right, twin_right = buf["left"], buf["e_half"], buf["right"], buf["twin_right"]
    act_beside, proj, middle, slopes = buf["act_beside"], buf["proj"], buf["middle"], buf["slopes"]
    probs, bias, dctx, vector = buf["probs"], buf["bias"], buf["dctx"], buf["vector"]
    parts, acc, fin = buf["parts"], buf["acc"], buf["fin"]
    pair_beside, pair_in, pair_across = buf["pair_beside"], buf["pair_in"], buf["pair_across"]
    vectors = buf["vectors"]

    all_rows, width = h.shape
    rows = all_rows // MICRO
    front = (rows // 2 + 15) // 16 * 16
    hidden = w_up.shape[1]
    chunk, half_chunk = acc.shape[2], acc.shape[2] // 2
    widths = (hidden, hidden, width, 3 * width)
    columns_at = (0, hidden, 2 * hidden, 2 * hidden + width)
    starts = [0]
    for member in widths:
        starts.append(starts[-1] + member // CORES // PANEL)
    strip = PANEL // STRIPS
    strips, direct = starts[-1] * STRIPS, starts[1] * STRIPS
    halves = [member // CORES for member in widths]
    twin_at = [start * PANEL for start in starts]

    section = lax.axis_index("section")
    place = lax.axis_index("dp")
    first = (place // GROUP) * GROUP
    mine = place - first
    z, y, core = mine // (PAIR * CORES), (mine // CORES) % PAIR, mine % CORES
    other_y, other_core = 1 - y, 1 - core
    far_side = z // 2
    is_end = (z == 0) | (z == LINE - 1)
    is_inner = jnp.logical_not(is_end)
    own = jnp.where(is_end, 0, 1)

    def numbered(zz):
        return zz + far_side * (LINE - 1 - 2 * zz)

    def device(zz, yy, cc):
        return (section, first + (zz * PAIR + yy) * CORES + cc)

    inner, end, across = (device(numbered(zz), y, core) for zz in (1, 0, 2))
    beside, twin = device(z, other_y, core), device(z, y, other_core)
    partner = (1 - section, place)
    leads = section == 0

    def send(source, target, key, index, to, landing=None):
        return pltpu.make_async_remote_copy(
            src_ref=source, dst_ref=target, send_sem=sem[key + "_send"].at[index],
            recv_sem=sem[key + "_recv"].at[index if landing is None else landing], device_id=to, device_id_type=MESH,
        )

    def fetch(source, target, index):
        return pltpu.make_async_copy(source, target, sem["fetch"].at[index])

    def rows_of(m):
        return pl.ds(pl.multiple_of(m * rows, rows), rows)

    loads = [fetch(w_out_in, w_out, 0), fetch(w_up_in, w_up, 1), fetch(w_down_in, w_down, 2)]
    loads_qkv = [
        fetch(w_qkv_in.at[:, pl.ds(part * width, width)], w_qkv.at[:, pl.ds(part * width, width)], 3 + part)
        for part in range(3)
    ]
    load_rows = fetch(tokens_in, h, 6)

    @pl.when(leads)
    def _():
        load_rows.start()

    @pl.when(jnp.logical_not(leads))
    def _():
        fetch(cotangent_in, e, 6).start()

    barrier = pltpu.get_barrier_semaphore()
    pl.semaphore_signal(barrier, inc=1, device_id=partner, device_id_type=MESH)
    for step in range(1, GROUP):
        peer = (section, first + (mine + step) % GROUP)
        pl.semaphore_signal(barrier, inc=1, device_id=peer, device_id_type=MESH)

    for load in loads_qkv:
        load.start()
    row_ids = lax.broadcasted_iota(jnp.int32, (rows, rows), 0)
    col_ids = lax.broadcasted_iota(jnp.int32, (rows, rows), 1)
    seen = (row_ids // ITEM_LEN == col_ids // ITEM_LEN) & (col_ids <= row_ids)
    bias[...] = jnp.where(seen, 0.0, -1e30)
    vector[...] = jnp.zeros_like(vector)
    proj[front:rows, width:] = jnp.zeros((rows - front, 2 * width), BF16)
    scale = 1.0 / math.sqrt(HEAD_DIM)


    spans = ((0, front), (front, rows), (rows, 2 * rows))

    def x_forward(i):
        at = pl.ds(spans[i][0], spans[i][1] - spans[i][0])
        return send(result.at[at], h.at[at], "x_forward", i, partner)

    returns = ((0, rows), (rows, rows + front), (rows + front, 2 * rows))

    def returned(i):
        return pl.ds(returns[i][0], returns[i][1] - returns[i][0])

    def x_back(i):
        return send(h.at[returned(i)], e.at[returned(i)], "x_back", i, partner)

    def mixed_store(m):
        return pltpu.make_async_copy(result.at[rows_of(m)], mixed_out.at[rows_of(m)], sem["store"].at[0, m])

    def grads_store(m):
        return pltpu.make_async_copy(h.at[rows_of(m)], grads_out.at[rows_of(m)], sem["store"].at[1, m])

    def twin_left(which, m):
        return send(left.at[which - 1, 0, rows_of(m)], left.at[which - 1, 1, rows_of(m)],
                    "twin_left", (which - 1, m), twin)

    def twin_right_of(which, m):
        start = pl.multiple_of(columns_at[which] + other_core * halves[which], 128)
        return send(right.at[rows_of(m), pl.ds(start, halves[which])],
                    twin_right.at[rows_of(m), pl.ds(twin_at[which], halves[which])],
                    "twin_right", (which, m), twin)

    def a2_beside(m):
        return send(left.at[UP - 1, 0, rows_of(m)], act_beside.at[0, rows_of(m)], "act_beside", (0, m), beside)

    def a2_onward(m):
        return send(act_beside.at[0, rows_of(m)], act_beside.at[1, rows_of(m)], "act_beside", (1, m), twin)

    def e_twin(i):
        return send(e_half.at[0, returned(i)], e_half.at[1, returned(i)], "e_half", (0, i), twin)

    def e_beside(i):
        return send(e_other.at[returned(i)], e_half.at[2, returned(i)], "e_half", (1, i), beside)

    def e_onward(i):
        return send(e_half.at[2, returned(i)], e_half.at[3, returned(i)], "e_half", (2, i), twin)


    def attend(i, load=False):
        low, high = spans[i]
        at, m = slice(low, high), low // rows
        whole = slice(m * rows, (m + 1) * rows)
        unit, unused = normalized(h[at].astype(F32))
        left[QKV - 1, 0, at] = (unit * gains[0:1] + biases[0:1]).astype(BF16)
        for part in range(3):
            cols = slice(part * width, (part + 1) * width)
            if load:
                loads_qkv[part].wait()
                loads[part].start()
            proj[at, cols] = dot(left[QKV - 1, 0, at], w_qkv[:, cols]).astype(BF16)
        for head in range(HEADS):
            q, k, v = (proj[whole, part * width + head * HEAD_DIM : part * width + (head + 1) * HEAD_DIM] for part in range(3))
            scores = dot_nt(q, k) * scale + bias[...]
            weight = jnp.exp(scores - jnp.max(scores, axis=-1, keepdims=True))
            weight = weight / jnp.sum(weight, axis=-1, keepdims=True)
            weight = weight.astype(BF16)
            probs[m * HEADS + head] = weight
            cols = slice(columns_at[OUT] + head * HEAD_DIM, columns_at[OUT] + (head + 1) * HEAD_DIM)
            right[whole, cols] = dot(weight, v).astype(BF16)

    def forward(i, load=False):
        at = slice(*spans[i])
        if load:
            loads[0].wait()
        attended = dot(right[at, columns_at[OUT] : columns_at[OUT] + width], w_out[...])
        middle[at] = h[at].astype(F32) + attended
        unit, unused = normalized(middle[at])
        left[UP - 1, 0, at] = (unit * gains[1:2] + biases[1:2]).astype(BF16)
        if i > 0:
            a2_beside(i - 1).start()
        if load:
            loads[1].wait()
        for part in range(2):
            cols = slice(part * hidden // 2, (part + 1) * hidden // 2)
            upward = dot(left[UP - 1, 0, at], w_up[:, cols])
            active, slope = gelu_and_slope(upward)
            slopes[at, cols] = slope.astype(BF16)
            right[at, cols] = active.astype(BF16)
        if load:
            loads[2].wait()
        result[at] = (middle[at] + dot(right[at, :hidden], w_down[...])).astype(BF16)

        @pl.when(leads)
        def _():
            x_forward(i).start()

    def share(m):
        mixed_store(m).start()
        twin_right_of(DOWN, m).start()
        twin_right_of(OUT, m).start()
        twin_left(QKV, m).start()
        twin_left(UP, m).start()

    def gather_act():
        cols = pl.ds(pl.multiple_of(core * halves[DOWN], 128), halves[DOWN])

        @pl.loop(0, MICRO)
        def _(m):
            a2_beside(m).wait_recv()
            a2_onward(m).start()
            a2_onward(m).wait()

            @pl.loop(0, 2)
            def _(source):
                active, unused = gelu_and_slope(dot(act_beside[source, rows_of(m)], w_up[:, cols]))
                act_beside[source, rows_of(m)] = active.astype(BF16)

    def spread(i):
        at = returned(i)
        for zz in range(LINE):
            cols = pl.ds(zz * chunk, chunk)
            e_half[0, at, cols] = e[at, pl.ds(pl.multiple_of((zz * PAIR + y) * chunk, chunk), chunk)]
            e_other[at, cols] = e[at, pl.ds(pl.multiple_of((zz * PAIR + other_y) * chunk, chunk), chunk)]
        e_beside(i).start()
        e_twin(i).start()

    def backward(m, hooks):
        at = rows_of(m)

        for part in range(2):
            cols = slice(part * hidden // 2, (part + 1) * hidden // 2)
            passed = dot_nt(e[at], w_down[cols])
            slope = slopes[at, cols].astype(F32)
            here = slice(columns_at[UP] + cols.start, columns_at[UP] + cols.stop)
            right[at, here] = (passed * slope).astype(BF16)
        twin_right_of(UP, m).start()

        hooks[0](m)
        grad = dot_nt(right[at, columns_at[UP] : columns_at[UP] + hidden], w_up[...])
        unit, size = normalized(middle[at])
        vector[1:2] += jnp.sum(grad * unit, axis=0, keepdims=True)
        vector[3:4] += jnp.sum(grad, axis=0, keepdims=True)
        middle[at] = e[at].astype(F32) + normalize_back(grad, unit, size, gains[1:2])
        left[OUT - 1, 0, at] = middle[at].astype(BF16)
        twin_left(OUT, m).start()
        dctx[...] = dot_nt(left[OUT - 1, 0, at], w_out[...]).astype(BF16)
        hooks[1](m)

        for head in range(HEADS):
            q, k, v = (proj[at, part * width + head * HEAD_DIM : part * width + (head + 1) * HEAD_DIM] for part in range(3))
            grad_ctx = dctx[:, head * HEAD_DIM : (head + 1) * HEAD_DIM]
            weight = probs[m * HEADS + head]
            grad_weight = dot_nt(grad_ctx, v)
            grad_v = dot_tn(weight, grad_ctx)
            weight = weight.astype(F32)
            total = jnp.sum(weight * grad_weight, axis=-1, keepdims=True)
            grad_scores = (weight * (grad_weight - total)).astype(BF16)
            grad_q = dot(grad_scores, k) * scale
            grad_k = dot_tn(grad_scores, q) * scale
            for part, value in enumerate((grad_q, grad_k, grad_v)):
                start = columns_at[QKV] + part * width + head * HEAD_DIM
                right[at, start : start + HEAD_DIM] = value.astype(BF16)

        twin_right_of(QKV, m).start()
        hooks[2](m)
        grad = dot_nt(right[at, columns_at[QKV] : columns_at[QKV] + 3 * width], w_qkv[...])
        unit, size = normalized(h[at].astype(F32))
        vector[0:1] += jnp.sum(grad * unit, axis=0, keepdims=True)
        vector[2:3] += jnp.sum(grad, axis=0, keepdims=True)
        h[at] = (middle[at] + normalize_back(grad, unit, size, gains[0:1])).astype(BF16)
        grads_store(m).start()

        @pl.when(jnp.logical_not(leads))
        def _():
            @pl.when(m == 0)
            def _():
                x_back(0).start()

            @pl.when(m == 1)
            def _():
                x_back(1).start()


    def beside_of(p):
        i = p - direct
        here, there = i % AHEAD, i % (2 * AHEAD)
        return send(parts.at[here, :, other_y], pair_beside.at[there], "pair_beside", here, beside, there)

    def in_of(p):
        return send(acc.at[p % RING, pl.ds(1, 3)], pair_in.at[p % RING], "pair_in", p % RING, inner)

    def across_of(p):
        return send(acc.at[p % RING, pl.ds(2, 2)], pair_across.at[p % RING], "pair_across", p % RING, across)

    def out_of(p):
        return send(acc.at[p % RING, 0], pair_in.at[p % RING, 0], "pair_out", p % RING, end)

    def strip_columns(p):
        return pl.ds(pl.multiple_of(p * strip, strip), strip)

    def fin_of(g):
        cols = pl.ds(pl.multiple_of(g * LEAVING * strip, LEAVING * strip), LEAVING * strip)
        return send(fin.at[:, cols], out.at[core, :, cols], "fin", g, twin)

    def add(target, *refs):
        total = target[...].astype(F32)
        for ref in refs:
            total = total + ref[...].astype(F32)
        target[...] = total.astype(BF16)

    def own_columns(p):
        place_of = p * PANEL + core * halves[0]
        for i in (1, 2, 3):
            shift = (columns_at[i] - twin_at[i] + core * halves[i]) - (
                columns_at[i - 1] - twin_at[i - 1] + core * halves[i - 1])
            place_of = place_of + jnp.where(p >= starts[i], shift, 0)
        return pl.ds(pl.multiple_of(place_of, 128), PANEL)

    def twin_columns(p):
        return pl.ds(pl.multiple_of(p * PANEL, PANEL), PANEL)

    def wait_for(which):
        for m in range(MICRO):
            twin_left(which, m).wait_recv()
            twin_right_of(which, m).wait_recv()

    def form(p):
        which = 0
        for i in (OUT, QKV):
            which = which + (p >= starts[i]).astype(jnp.int32)

            @pl.when(p == starts[i])
            def _(i=i):
                wait_for(i)

        total = dot_tn(left[which, 0], right[:, own_columns(p)]) + dot_tn(left[which, 1], twin_right[:, twin_columns(p)])
        total = total.astype(BF16).reshape(LINE, PAIR, chunk, PANEL)
        for part in range(STRIPS):
            for zz in range(LINE):
                here = total[zz, :, :, part * strip : (part + 1) * strip]
                parts[(p * STRIPS + part - direct) % AHEAD, numbered(zz)] = here

    def form_up(low, high):
        @pl.loop(starts[UP] + low, starts[UP] + high)
        def _(p):
            form(p)

    def start_strips(low, high):
        @pl.loop(direct + low, direct + high)
        def _(p):
            beside_of(p).start()

    def gather_e(i):
        e_beside(i).wait_recv()
        e_onward(i).start()

    def form_down():
        for m in range(MICRO):
            twin_right_of(DOWN, m).wait_recv()
        for i in range(len(returns)):
            e_twin(i).wait_recv()
            e_onward(i).wait_recv()

        @pl.loop(0, starts[UP])
        def _(p):
            total = dot_tn(e_half[0], right[:, own_columns(p)]) + dot_tn(e_half[1], twin_right[:, twin_columns(p)])
            for source in range(2):
                total = total + dot_tn(e_half[2 + source], act_beside[source, :, twin_columns(p)])
            total = total.astype(BF16).reshape(LINE, chunk, PANEL)
            for part in range(STRIPS):
                for zz in range(LINE):
                    acc[(p * STRIPS + part) % RING, numbered(zz)] = total[zz, :, part * strip : (part + 1) * strip]

            @pl.when(is_end & (p < FIRST // STRIPS))
            def _():
                for part in range(STRIPS):
                    in_of(p * STRIPS + part).start()

    def enter(t):
        @pl.when((t < direct - FIRST) & is_end)
        def _():
            in_of(t + FIRST).start()

    def across_y(t):
        @pl.when((t >= direct) & (t < strips))
        def _():
            i = t - direct
            beside_of(t).wait()
            for d in range(LINE):
                total = parts[i % AHEAD, d, y].astype(F32) + pair_beside[i % (2 * AHEAD), d].astype(F32)
                acc[t % RING, d] = total.astype(BF16)

            @pl.when(is_end)
            def _():
                in_of(t).start()

            @pl.when(t + AHEAD < strips)
            def _():
                @pl.when(t % STRIPS == STRIPS - 1)
                def _():
                    form((t + AHEAD) // STRIPS)
                    for part in range(STRIPS):
                        beside_of(t + AHEAD - STRIPS + 1 + part).start()

    def relay(t):
        p = t - LAG

        @pl.when((p >= 0) & (p < strips) & is_inner)
        def _():
            in_of(p).wait_recv()
            add(acc.at[p % RING, pl.ds(2, 2)], pair_in.at[p % RING, pl.ds(1, 2)])
            across_of(p).start()
            add(acc.at[p % RING, 1], pair_in.at[p % RING, 0])

        q = t - 2 * LAG

        @pl.when((q >= 0) & (q < strips) & is_inner)
        def _():
            across_of(q).wait_recv()
            add(acc.at[q % RING, 0], pair_across.at[q % RING, 1])
            out_of(q).start()
            add(acc.at[q % RING, 1], pair_across.at[q % RING, 0])

        r = t - 3 * LAG

        @pl.when(r >= 0)
        def _():
            @pl.when(is_end)
            def _():
                out_of(r).wait_recv()
                add(acc.at[r % RING, 0], pair_in.at[r % RING, 0])
                in_of(r).wait_send()

            @pl.when(is_inner)
            def _():
                across_of(r).wait_send()
                out_of(r).wait_send()

            def block(which):
                return acc[r % RING, own, pl.ds(pl.multiple_of(which * half_chunk, half_chunk), half_chunk)].astype(F32)

            out[core, :, strip_columns(r)] = block(core)
            fin[:, strip_columns(r)] = block(other_core)

            @pl.when(r % LEAVING == LEAVING - 1)
            def _():
                fin_of(r // LEAVING).start()

    def proceed(low, high, parts_of_step):
        @pl.loop(low, high)
        def _(t):
            for part in parts_of_step:
                part(t)


    def after_du(m):
        @pl.when((m == MICRO - 1) & leads)
        def _():
            for i in range(2):
                gather_e(i)
            wait_for(UP)
            form_up(0, 2)
            start_strips(0, 2 * STRIPS)
            gather_e(2)
            form_down()

    def after_middle(m):
        @pl.when((m == MICRO - 1) & leads)
        def _():
            form_up(2, AHEAD // STRIPS)
            start_strips(2 * STRIPS, AHEAD)
            proceed(0, BEFORE_HEADS, (enter, relay))

    def after_heads(m):
        @pl.when((m == MICRO - 1) & leads)
        def _():
            proceed(BEFORE_HEADS, BEFORE_LAST, (enter, relay))

    @pl.when(leads)
    def _():
        load_rows.wait()
        attend(0, load=True)

    pl.semaphore_wait(barrier, GROUP)

    @pl.when(jnp.logical_not(leads))
    def _():
        load_rows.wait()
        for i in range(len(returns)):
            spread(i)
        x_forward(0).wait_recv()
        attend(0, load=True)

    forward(0, load=True)

    @pl.when(jnp.logical_not(leads))
    def _():
        x_forward(1).wait_recv()

    attend(1)
    forward(1)
    share(0)

    @pl.loop(0, MICRO + 1)
    def _(step):
        @pl.when(step == section)
        def _():
            @pl.when(jnp.logical_not(leads))
            def _():
                x_forward(2).wait_recv()

            attend(2)
            forward(2)
            share(1)

            @pl.when(leads)
            def _():
                gather_act()

        @pl.when(step != section)
        def _():
            m = step // 2

            @pl.when(leads & (m == 0))
            def _():
                x_back(0).wait_recv()
                spread(0)

            @pl.when(leads & (m == 1))
            def _():
                for i in (1, 2):
                    x_back(i).wait_recv()
                    spread(i)

            backward(m, (after_du, after_middle, after_heads))

    def send_vector(step):
        peer = (mine + step) % GROUP
        start = pl.multiple_of((peer // CORES) * chunk, chunk)
        return pltpu.make_async_remote_copy(
            src_ref=vector.at[:, pl.ds(start, chunk)], dst_ref=vectors.at[mine],
            send_sem=sem["vector_send"].at[step], recv_sem=sem["vector_recv"].at[mine],
            device_id=(section, first + peer), device_id_type=MESH,
        )

    @pl.loop(1, GROUP)
    def _(step):
        send_vector(step).start()

    @pl.when(jnp.logical_not(leads))
    def _():
        wait_for(UP)
        form_up(0, AHEAD // STRIPS)
        x_back(2).start()
        start_strips(0, AHEAD)
        for i in range(len(returns)):
            gather_e(i)
        gather_act()
        form_down()

        proceed(0, BEFORE_LAST, (enter, relay))

    proceed(BEFORE_LAST, strips + 3 * LAG, (enter, across_y, relay))

    vector_total = vector[:, pl.ds(pl.multiple_of((mine // CORES) * chunk, chunk), chunk)]
    for step in range(1, GROUP):
        sender = (mine + step) % GROUP
        pltpu.make_async_remote_copy(
            src_ref=vector.at[:, pl.ds(0, chunk)], dst_ref=vectors.at[sender],
            send_sem=sem["vector_send"].at[step], recv_sem=sem["vector_recv"].at[sender],
            device_id=twin, device_id_type=MESH,
        ).wait_recv()
        vector_total = vector_total + vectors[sender]
    vector_out[...] = vector_total

    @pl.loop(1, GROUP)
    def _(step):
        send_vector(step).wait_send()

    for m in range(MICRO):
        for which in (UP, OUT, QKV):
            twin_left(which, m).wait_send()
        for which in range(4):
            twin_right_of(which, m).wait_send()
        a2_beside(m).wait_send()
        grads_store(m).wait()
        mixed_store(m).wait()

    for i in range(len(returns)):
        e_twin(i).wait_send()
        e_beside(i).wait_send()
        e_onward(i).wait_send()

    @pl.when(jnp.logical_not(leads))
    def _():
        for i in range(len(returns)):
            x_back(i).wait_send()

    @pl.when(leads)
    def _():
        for i in range(len(spans)):
            x_forward(i).wait_send()

    @pl.loop(0, strips // LEAVING)
    def _(g):
        fin_of(g).wait()


def layers(tokens, cotangent, gains, biases, w_qkv, w_out, w_up, w_down):
    all_rows, width = tokens.shape
    hidden = w_up.shape[1]
    rows = all_rows // MICRO
    columns = 2 * hidden + 4 * width
    strip = PANEL // STRIPS
    strips = columns // CORES // strip
    chunk = width // (LINE * PAIR)
    dma = pltpu.SemaphoreType.DMA
    shapes = {
        "h": ((all_rows, width), BF16),
        "e": ((all_rows, width), BF16),
        "e_other": ((all_rows, width // 2), BF16),
        "result": ((all_rows, width), BF16),
        "w_qkv": (w_qkv.shape, BF16),
        "w_out": (w_out.shape, BF16),
        "w_up": (w_up.shape, BF16),
        "w_down": (w_down.shape, BF16),
        "left": ((3, CORES, all_rows, width), BF16),
        "e_half": ((4, all_rows, width // 2), BF16),
        "right": ((all_rows, columns), BF16),
        "twin_right": ((all_rows, columns // CORES), BF16),
        "act_beside": ((2, all_rows, hidden // CORES), BF16),
        "proj": ((all_rows, 3 * width), BF16),
        "middle": ((all_rows, width), F32),
        "slopes": ((all_rows, hidden), BF16),
        "probs": ((MICRO * HEADS, rows, rows), BF16),
        "bias": ((rows, rows), F32),
        "dctx": ((rows, width), BF16),
        "vector": ((8, width), F32),
        "parts": ((AHEAD, LINE, PAIR, chunk, strip), BF16),
        "acc": ((RING, LINE, chunk, strip), BF16),
        "fin": ((chunk // 2, columns // CORES), F32),
        "pair_beside": ((2 * AHEAD, LINE, chunk, strip), BF16),
        "pair_in": ((RING, 3, chunk, strip), BF16),
        "pair_across": ((RING, 2, chunk, strip), BF16),
        "vectors": ((GROUP, 8, chunk), F32),
    }
    exchanges = {
        "x_forward": (3,), "x_back": (3,), "twin_left": (3, MICRO), "twin_right": (4, MICRO),
        "act_beside": (2, MICRO), "e_half": (3, 3), "pair_in": (RING,), "pair_across": (RING,), "pair_out": (RING,),
        "fin": (strips // LEAVING,), "vector": (GROUP,),
    }
    semaphores = {"fetch": dma((7,)), "store": dma((2, MICRO))}
    for key, count in exchanges.items():
        semaphores[key + "_send"] = dma(count)
        semaphores[key + "_recv"] = dma(count)
    semaphores["pair_beside_send"], semaphores["pair_beside_recv"] = dma((AHEAD,)), dma((2 * AHEAD,))
    anywhere = pl.BlockSpec(memory_space=pl.ANY)
    in_vmem = pl.BlockSpec(memory_space=pltpu.VMEM)
    return pl.pallas_call(
        layer_kernel,
        out_shape=(
            jax.ShapeDtypeStruct((all_rows, width), BF16),
            jax.ShapeDtypeStruct((all_rows, width), BF16),
            jax.ShapeDtypeStruct((CORES, chunk // 2, columns // CORES), F32),
            jax.ShapeDtypeStruct((8, chunk), F32),
        ),
        in_specs=[anywhere] * 2 + [in_vmem] * 2 + [anywhere] * 4,
        out_specs=(anywhere, anywhere, in_vmem, in_vmem),
        scratch_shapes=[{key: pltpu.VMEM(*shape) for key, shape in shapes.items()}, semaphores],
        compiler_params=pltpu.CompilerParams(
            collective_id=1, has_side_effects=True, vmem_limit_bytes=64 * 2**20
        ),
        name="relay_layers",
    )(tokens, cotangent, gains, biases, w_qkv, w_out, w_up, w_down)


def results_kernel(
    mixed_in, grads_in, block_in, vectors_in, mixed, grads, down, up, out, qkv, gains, biases,
    rows, block, vectors, shares, sem,
):
    started = []

    def copy(source, target):
        started.append(pltpu.make_async_copy(source, target, sem.at[len(started)]))
        started[-1].start()
        return started[-1]

    fetches = [copy(block_in.at[core], block.at[core]) for core in range(CORES)]
    fetches.append(copy(vectors_in, vectors))
    fetches += [copy(ref, rows.at[i]) for i, ref in enumerate((mixed_in, grads_in))]
    stores = []
    for core in range(CORES):
        fetches[core].wait()
        offset = 0
        for ref in (down, up, out, qkv):
            half = ref.shape[1] // CORES
            stores.append(copy(block.at[core, :, pl.ds(offset, half)], ref.at[:, pl.ds(core * half, half)]))
            offset += half
    fetches[CORES].wait()
    share = gains.shape[1]
    mine = lax.axis_index("dp") % CORES
    for core in range(CORES):
        @pl.when(mine == core)
        def _(core=core):
            here = slice(core * share, (core + 1) * share)
            shares[0] = vectors[0:2, here]
            shares[1] = vectors[2:4, here]

    stores += [copy(shares.at[i], ref) for i, ref in enumerate((gains, biases))]
    for i, ref in enumerate((mixed, grads)):
        fetches[CORES + 1 + i].wait()
        stores.append(copy(rows.at[i], ref))
    for store in stores:
        store.wait()


def results(mixed, grads, block, vectors, hidden):
    width, share = mixed.shape[1], block.shape[1]
    anywhere = pl.BlockSpec(memory_space=pl.ANY)
    shapes = ((share, hidden), (share, hidden), (share, width), (share, 3 * width), (2, share), (2, share))
    mixed, grads, down, up, out, qkv, gains, biases = pl.pallas_call(
        results_kernel,
        out_shape=(jax.ShapeDtypeStruct(mixed.shape, BF16), jax.ShapeDtypeStruct(grads.shape, BF16))
        + tuple(jax.ShapeDtypeStruct(shape, F32) for shape in shapes),
        in_specs=[anywhere] * 4,
        out_specs=(anywhere,) * 8,
        scratch_shapes=[
            pltpu.VMEM((2,) + mixed.shape, BF16), pltpu.VMEM(block.shape, F32), pltpu.VMEM(vectors.shape, F32),
            pltpu.VMEM((2, 2, share), F32), pltpu.SemaphoreType.DMA((CORES + 3 + 4 * CORES + 4,)),
        ],
        compiler_params=pltpu.CompilerParams(vmem_limit_bytes=64 * 2**20),
        name="place_results",
    )(mixed, grads, block, vectors)
    return mixed, grads, qkv, out.T, up, down.T, gains, biases


def reordered(member, axis, groups, back=False):
    shape = member.shape
    row = shape[axis] // (groups * GROUP)
    split = (GROUP, groups, row) if back else (groups, GROUP, row)
    apart = member.reshape(shape[:axis] + split + shape[axis + 1 :])
    return jnp.swapaxes(apart, axis, axis + 1).reshape(shape)


def on_device(tokens, cotangent, norm_gains, norm_biases, w_qkv, w_out, w_up, w_down):
    hidden, width = w_up.shape[2], tokens.shape[1]
    operands = (tokens, cotangent, norm_gains[0], norm_biases[0], w_qkv[0], w_out[0], w_up[0], w_down[0])
    groups = lax.axis_size("dp") // GROUP
    if groups > 1:
        axes = (1, 1, 1, 1, 0, 1, 0, 1)
        operands = tuple(reordered(member, axis, groups) for member, axis in zip(operands, axes))
    mixed, grads, block, vector_block = layers(*operands)
    if groups == 1:
        return tuple(member[None] for member in results(mixed, grads, block, vector_block, hidden))
    core = lax.axis_index("dp") % CORES
    share = block.shape[1]
    vector_block = lax.dynamic_slice_in_dim(vector_block[:4], core * share, share, 1)
    pieces = []
    offset = 0
    for member in (hidden, hidden, width, 3 * width):
        half = member // CORES
        part = block[:, :, offset : offset + half]
        pieces.append(jnp.concatenate([part[0], part[1]], axis=1))
        offset += half
    mixed, grads = (reordered(member, 1, groups, back=True) for member in (mixed, grads))
    same = [[g * GROUP + j for g in range(groups)] for j in range(GROUP)]

    def summed(member):
        return lax.psum_scatter(member, "dp", scatter_dimension=0, axis_index_groups=same, tiled=True)

    pieces = [summed(member) for member in pieces]
    vector_block = summed(vector_block.T).T
    down, up, out, qkv = pieces
    return (
        mixed[None], grads[None], qkv[None], out.T[None], up[None], down.T[None],
        vector_block[None, 0:2], vector_block[None, 2:4],
    )


def solution(mesh):
    placed = (P("dp", None),) * 2 + (P("section", None, None),) * 6
    return jax.shard_map(
        on_device,
        mesh=mesh,
        in_specs=placed,
        out_specs=(
            P("section", "dp", None),
            P("section", "dp", None),
            P("section", "dp", None),
            P("section", None, "dp"),
            P("section", "dp", None),
            P("section", None, "dp"),
            P("section", None, "dp"),
            P("section", None, "dp"),
        ),
        check_vma=False,
    )
```

```python
import math

import jax
import jax.numpy as jnp
from jax import lax
from jax.experimental import pallas as pl
from jax.experimental.pallas import tpu as pltpu
from jax.sharding import PartitionSpec as P

HEADS = 8
HEAD_DIM = 128
ITEM_LEN = 15
MICRO = 2
EPSILON = 1e-05

LINE, PAIR, CORES = 4, 2, 2
GROUP = LINE * PAIR * CORES
PANEL = 256
STRIPS = 2
AHEAD = 10
LAG = 2
END_LAG = 5
BEFORE_HEADS, BEFORE_LAST = 4, 5
RING = 8
END_RING = 12
VECTORS = 8, 22
FIRST = 4
LEAVING = 8
MESH = pl.DeviceIdType.MESH
BF16, F32 = jnp.bfloat16, jnp.float32
DOWN, UP, OUT, QKV = range(4)


def dot(left, right):
    return jnp.dot(left, right, preferred_element_type=F32)


def dot_nt(left, right):
    return lax.dot_general(left, right, (((1,), (1,)), ((), ())), preferred_element_type=F32)


def dot_tn(left, right):
    return lax.dot_general(left, right, (((0,), (0,)), ((), ())), preferred_element_type=F32)


def normalized(values):
    centered = values - jnp.mean(values, axis=-1, keepdims=True)
    scale = lax.rsqrt(jnp.mean(centered * centered, axis=-1, keepdims=True) + EPSILON)
    return centered * scale, scale


def normalize_back(grad, unit, scale, gain):
    scaled = grad * gain
    along = jnp.mean(scaled * unit, axis=-1, keepdims=True)
    return scale * (scaled - jnp.mean(scaled, axis=-1, keepdims=True) - unit * along)


def gelu_and_slope(u):
    square = u * u
    inner = jnp.tanh(u * (0.7978845608 + 0.7978845608 * 0.044715 * square))
    part = 0.5 + 0.5 * inner
    steep = 0.5 * 0.7978845608 + 1.5 * 0.7978845608 * 0.044715 * square
    return u * part, part + u * (1.0 - inner * inner) * steep


def layer_kernel(
    tokens_in, cotangent_in, gains, biases, w_qkv_in, w_out_in, w_up_in, w_down_in,
    mixed_out, grads_out, out, vector_out, buf, sem,
):
    h, e, e_other, result = buf["h"], buf["e"], buf["e_other"], buf["result"]
    w_qkv, w_out, w_up, w_down = buf["w_qkv"], buf["w_out"], buf["w_up"], buf["w_down"]
    left, e_half, right, twin_right = buf["left"], buf["e_half"], buf["right"], buf["twin_right"]
    act_beside, proj, middle, slopes = buf["act_beside"], buf["proj"], buf["middle"], buf["slopes"]
    probs, bias, dctx, vector = buf["probs"], buf["bias"], buf["dctx"], buf["vector"]
    parts, acc, fin = buf["parts"], buf["acc"], buf["fin"]
    pair_beside, pair_in, pair_across = buf["pair_beside"], buf["pair_in"], buf["pair_across"]
    vectors, vectors_line = buf["vectors"], buf["vectors_line"]

    all_rows, width = h.shape
    rows = all_rows // MICRO
    front = (rows // 2 + 15) // 16 * 16
    hidden = w_up.shape[1]
    chunk, half_chunk = acc.shape[2], acc.shape[2] // 2
    widths = (hidden, hidden, width, 3 * width)
    columns_at = (0, hidden, 2 * hidden, 2 * hidden + width)
    starts = [0]
    for member in widths:
        starts.append(starts[-1] + member // CORES // PANEL)
    strip = PANEL // STRIPS
    strips, direct = starts[-1] * STRIPS, starts[1] * STRIPS
    halves = [member // CORES for member in widths]
    twin_at = [start * PANEL for start in starts]

    section = lax.axis_index("section")
    place = lax.axis_index("dp")
    first = (place // GROUP) * GROUP
    mine = place - first
    z, y, core = mine // (PAIR * CORES), (mine // CORES) % PAIR, mine % CORES
    other_y, other_core = 1 - y, 1 - core
    far_side = z // 2
    is_end = (z == 0) | (z == LINE - 1)
    is_inner = jnp.logical_not(is_end)
    own = jnp.where(is_end, 0, 1)

    def numbered(zz):
        return zz + far_side * (LINE - 1 - 2 * zz)

    def device(zz, yy, cc):
        return (section, first + (zz * PAIR + yy) * CORES + cc)

    beside, twin = device(z, other_y, core), device(z, y, other_core)
    partner = (1 - section, place)
    leads = section == 0

    def send(source, target, key, index, to, landing=None):
        return pltpu.make_async_remote_copy(
            src_ref=source, dst_ref=target, send_sem=sem[key + "_send"].at[index],
            recv_sem=sem[key + "_recv"].at[index if landing is None else landing], device_id=to, device_id_type=MESH,
        )

    def fetch(source, target, index):
        return pltpu.make_async_copy(source, target, sem["fetch"].at[index])

    def rows_of(m):
        return pl.ds(pl.multiple_of(m * rows, rows), rows)

    loads = [fetch(w_out_in, w_out, 0), fetch(w_up_in, w_up, 1), fetch(w_down_in, w_down, 2)]
    loads_qkv = [
        fetch(w_qkv_in.at[:, pl.ds(part * width, width)], w_qkv.at[:, pl.ds(part * width, width)], 3 + part)
        for part in range(3)
    ]
    load_rows = fetch(tokens_in, h, 6)

    @pl.when(leads)
    def _():
        load_rows.start()

    @pl.when(jnp.logical_not(leads))
    def _():
        fetch(cotangent_in, e, 6).start()

    barrier = pltpu.get_barrier_semaphore()
    lined = [device((z + step) % LINE, y, core) for step in range(1, LINE)]
    inner, end, across, far_end = (device(numbered(zz), y, core) for zz in (1, 0, 2, 3))
    peers = [partner, twin, beside] + lined
    for peer in peers:
        pl.semaphore_signal(barrier, inc=1, device_id=peer, device_id_type=MESH)
    for load in loads_qkv:
        load.start()
    row_ids = lax.broadcasted_iota(jnp.int32, (rows, rows), 0)
    col_ids = lax.broadcasted_iota(jnp.int32, (rows, rows), 1)
    seen = (row_ids // ITEM_LEN == col_ids // ITEM_LEN) & (col_ids <= row_ids)
    bias[...] = jnp.where(seen, 0.0, -1e30)
    vector[...] = jnp.zeros_like(vector)
    proj[front:rows, width:] = jnp.zeros((rows - front, 2 * width), BF16)
    scale = 1.0 / math.sqrt(HEAD_DIM)


    spans = ((0, front), (front, rows), (rows, 2 * rows))

    def x_forward(i):
        at = pl.ds(spans[i][0], spans[i][1] - spans[i][0])
        return send(result.at[at], h.at[at], "x_forward", i, partner)

    late = rows // 5
    returns = ((0, rows), (rows, rows + front), (rows + front, 2 * rows - late), (2 * rows - late, 2 * rows))

    def returned(i):
        return pl.ds(returns[i][0], returns[i][1] - returns[i][0])

    def x_back(i):
        return send(h.at[returned(i)], e.at[returned(i)], "x_back", i, partner)

    def mixed_store(m):
        return pltpu.make_async_copy(result.at[rows_of(m)], mixed_out.at[rows_of(m)], sem["store"].at[0, m])

    def grads_store(m):
        return pltpu.make_async_copy(h.at[rows_of(m)], grads_out.at[rows_of(m)], sem["store"].at[1, m])

    def twin_left(which, m):
        return send(left.at[which - 1, 0, rows_of(m)], left.at[which - 1, 1, rows_of(m)],
                    "twin_left", (which - 1, m), twin)

    def twin_right_of(which, m):
        start = pl.multiple_of(columns_at[which] + other_core * halves[which], 128)
        return send(right.at[rows_of(m), pl.ds(start, halves[which])],
                    twin_right.at[rows_of(m), pl.ds(twin_at[which], halves[which])],
                    "twin_right", (which, m), twin)

    def a2_beside(m):
        return send(left.at[UP - 1, 0, rows_of(m)], act_beside.at[0, rows_of(m)], "act_beside", (0, m), beside)

    def a2_onward(m):
        return send(act_beside.at[0, rows_of(m)], act_beside.at[1, rows_of(m)], "act_beside", (1, m), twin)

    def e_twin(i):
        return send(e_half.at[0, returned(i)], e_half.at[1, returned(i)], "e_half", (0, i), twin)

    def e_beside(i):
        return send(e_other.at[returned(i)], e_half.at[2, returned(i)], "e_half", (1, i), beside)

    def e_onward(i):
        return send(e_half.at[2, returned(i)], e_half.at[3, returned(i)], "e_half", (2, i), twin)


    def attend(i, load=False):
        low, high = spans[i]
        at, m = slice(low, high), low // rows
        whole = slice(m * rows, (m + 1) * rows)
        unit, unused = normalized(h[at].astype(F32))
        left[QKV - 1, 0, at] = (unit * gains[0:1] + biases[0:1]).astype(BF16)
        for part in range(3):
            cols = slice(part * width, (part + 1) * width)
            if load:
                loads_qkv[part].wait()
                loads[part].start()
            proj[at, cols] = dot(left[QKV - 1, 0, at], w_qkv[:, cols]).astype(BF16)
        def heads_of(part, head):
            start = part * width + head * HEAD_DIM
            return proj[whole, start : start + HEAD_DIM]

        for head in range(HEADS):
            scores = dot_nt(heads_of(0, head), heads_of(1, head)) * scale + bias[...]
            weight = jnp.exp(scores - jnp.max(scores, axis=-1, keepdims=True))
            probs[m * HEADS + head] = (weight / jnp.sum(weight, axis=-1, keepdims=True)).astype(BF16)
        for head in range(HEADS):
            cols = slice(columns_at[OUT] + head * HEAD_DIM, columns_at[OUT] + (head + 1) * HEAD_DIM)
            right[whole, cols] = dot(probs[m * HEADS + head], heads_of(2, head)).astype(BF16)

    def forward(i, load=False):
        at = slice(*spans[i])
        if load:
            loads[0].wait()
        attended = dot(right[at, columns_at[OUT] : columns_at[OUT] + width], w_out[...])
        middle[at] = h[at].astype(F32) + attended
        unit, unused = normalized(middle[at])
        left[UP - 1, 0, at] = (unit * gains[1:2] + biases[1:2]).astype(BF16)
        if i > 0:
            a2_beside(i - 1).start()
        if load:
            loads[1].wait()
        for part in range(2):
            cols = slice(part * hidden // 2, (part + 1) * hidden // 2)
            upward = dot(left[UP - 1, 0, at], w_up[:, cols])
            active, slope = gelu_and_slope(upward)
            slopes[at, cols] = slope.astype(BF16)
            right[at, cols] = active.astype(BF16)
        if load:
            loads[2].wait()
        result[at] = (middle[at] + dot(right[at, :hidden], w_down[...])).astype(BF16)

        @pl.when(leads)
        def _():
            x_forward(i).start()

    def share(m):
        mixed_store(m).start()
        twin_right_of(DOWN, m).start()
        twin_right_of(OUT, m).start()
        twin_left(QKV, m).start()
        twin_left(UP, m).start()

    def gather_act():
        cols = pl.ds(pl.multiple_of(core * halves[DOWN], 128), halves[DOWN])

        @pl.loop(0, MICRO)
        def _(m):
            a2_beside(m).wait_recv()
            a2_onward(m).start()
            a2_onward(m).wait()

            @pl.loop(0, 2)
            def _(source):
                active, unused = gelu_and_slope(dot(act_beside[source, rows_of(m)], w_up[:, cols]))
                act_beside[source, rows_of(m)] = active.astype(BF16)

    def spread(i):
        at = returned(i)
        for zz in range(LINE):
            cols = pl.ds(zz * chunk, chunk)
            e_half[0, at, cols] = e[at, pl.ds(pl.multiple_of((zz * PAIR + y) * chunk, chunk), chunk)]
            e_other[at, cols] = e[at, pl.ds(pl.multiple_of((zz * PAIR + other_y) * chunk, chunk), chunk)]
        e_beside(i).start()
        e_twin(i).start()

    def backward(m, hooks):
        at = rows_of(m)

        for part in range(2):
            cols = slice(part * hidden // 2, (part + 1) * hidden // 2)
            passed = dot_nt(e[at], w_down[cols])
            slope = slopes[at, cols].astype(F32)
            here = slice(columns_at[UP] + cols.start, columns_at[UP] + cols.stop)
            right[at, here] = (passed * slope).astype(BF16)
        twin_right_of(UP, m).start()

        hooks[0](m)
        grad = dot_nt(right[at, columns_at[UP] : columns_at[UP] + hidden], w_up[...])
        unit, size = normalized(middle[at])
        vector[1:2] += jnp.sum(grad * unit, axis=0, keepdims=True)
        vector[3:4] += jnp.sum(grad, axis=0, keepdims=True)
        middle[at] = e[at].astype(F32) + normalize_back(grad, unit, size, gains[1:2])
        left[OUT - 1, 0, at] = middle[at].astype(BF16)
        twin_left(OUT, m).start()
        dctx[...] = dot_nt(left[OUT - 1, 0, at], w_out[...]).astype(BF16)
        hooks[1](m)

        def heads_of(part, head):
            start = part * width + head * HEAD_DIM
            return proj[at, start : start + HEAD_DIM]

        def keep(part, head, value):
            start = columns_at[QKV] + part * width + head * HEAD_DIM
            right[at, start : start + HEAD_DIM] = value.astype(BF16)

        def grad_ctx(head):
            return dctx[:, head * HEAD_DIM : (head + 1) * HEAD_DIM]

        grad_scores = []
        for head in range(HEADS):
            weight = probs[m * HEADS + head].astype(F32)
            grad_weight = dot_nt(grad_ctx(head), heads_of(2, head))
            total = jnp.sum(weight * grad_weight, axis=-1, keepdims=True)
            grad_scores.append((weight * (grad_weight - total)).astype(BF16))
        for head in range(HEADS):
            keep(2, head, dot_tn(probs[m * HEADS + head], grad_ctx(head)))
        for head in range(HEADS):
            keep(0, head, dot(grad_scores[head], heads_of(1, head)) * scale)
            keep(1, head, dot_tn(grad_scores[head], heads_of(0, head)) * scale)

        twin_right_of(QKV, m).start()
        hooks[2](m)
        grad = dot_nt(right[at, columns_at[QKV] : columns_at[QKV] + 3 * width], w_qkv[...])
        unit, size = normalized(h[at].astype(F32))
        vector[0:1] += jnp.sum(grad * unit, axis=0, keepdims=True)
        vector[2:3] += jnp.sum(grad, axis=0, keepdims=True)
        h[at] = (middle[at] + normalize_back(grad, unit, size, gains[0:1])).astype(BF16)
        grads_store(m).start()

        @pl.when(jnp.logical_not(leads))
        def _():
            @pl.when(m == 0)
            def _():
                x_back(0).start()

            @pl.when(m == 1)
            def _():
                x_back(1).start()


    def beside_of(p):
        i = p - direct
        here, there = i % AHEAD, i % (2 * AHEAD)
        return send(parts.at[here, :, other_y], pair_beside.at[there], "pair_beside", here, beside, there)

    def in_of(p):
        return send(acc.at[p % RING, pl.ds(1, 3)], pair_in.at[pl.ds(3 * (p % RING), 3)], "pair_in", p % RING, inner)

    def across_of(p):
        return send(acc.at[p % RING, 2], pair_across.at[p % RING], "pair_across", p % RING, across)

    def far_of(p):
        there = p % END_RING
        return send(acc.at[p % RING, 3], pair_in.at[2 * there + 1], "pair_far", p % RING, far_end, there)

    def out_of(p):
        there = p % END_RING
        return send(acc.at[p % RING, 0], pair_in.at[2 * there], "pair_out", p % RING, end, there)

    def chunk_at(zz):
        return pl.ds(pl.multiple_of((zz * PAIR + y) * chunk, chunk), chunk)

    def vector_twin():
        return send(vector, vectors.at[0], "vector", 0, twin)

    def vector_beside():
        return send(vector, vectors.at[1], "vector", 1, beside)

    def vector_line(step):
        return send(vector.at[:, chunk_at((z + step) % LINE)], vectors_line.at[step - 1], "vector", 1 + step, lined[step - 1])

    def strip_columns(p):
        return pl.ds(pl.multiple_of(p * strip, strip), strip)

    def fin_of(g):
        cols = pl.ds(pl.multiple_of(g * LEAVING * strip, LEAVING * strip), LEAVING * strip)
        return send(fin.at[1, :, cols], out.at[core, :, cols], "fin", g, twin)

    def kept_of(g):
        cols = pl.ds(pl.multiple_of(g * LEAVING * strip, LEAVING * strip), LEAVING * strip)
        return pltpu.make_async_copy(fin.at[0, :, cols], out.at[core, :, cols], sem["kept"].at[g])

    def add(target, *refs):
        total = target[...].astype(F32)
        for ref in refs:
            total = total + ref[...].astype(F32)
        target[...] = total.astype(BF16)

    def own_columns(p):
        place_of = p * PANEL + core * halves[0]
        for i in (1, 2, 3):
            shift = (columns_at[i] - twin_at[i] + core * halves[i]) - (
                columns_at[i - 1] - twin_at[i - 1] + core * halves[i - 1])
            place_of = place_of + jnp.where(p >= starts[i], shift, 0)
        return pl.ds(pl.multiple_of(place_of, 128), PANEL)

    def twin_columns(p):
        return pl.ds(pl.multiple_of(p * PANEL, PANEL), PANEL)

    def wait_for(which):
        for m in range(MICRO):
            twin_left(which, m).wait_recv()
            twin_right_of(which, m).wait_recv()

    def form(p):
        which = 0
        for i in (OUT, QKV):
            which = which + (p >= starts[i]).astype(jnp.int32)

            @pl.when(p == starts[i])
            def _(i=i):
                wait_for(i)

        total = dot_tn(left[which, 0], right[:, own_columns(p)]) + dot_tn(left[which, 1], twin_right[:, twin_columns(p)])
        total = total.astype(BF16).reshape(LINE, PAIR, chunk, PANEL)
        for part in range(STRIPS):
            for zz in range(LINE):
                here = total[zz, :, :, part * strip : (part + 1) * strip]
                parts[(p * STRIPS + part - direct) % AHEAD, numbered(zz)] = here

    def form_up(low, high):
        @pl.loop(starts[UP] + low, starts[UP] + high)
        def _(p):
            form(p)

    def start_strips(low, high):
        @pl.loop(direct + low, direct + high)
        def _(p):
            beside_of(p).start()

    def gather_e(i):
        e_beside(i).wait_recv()
        e_onward(i).start()

    def form_down():
        for m in range(MICRO):
            twin_right_of(DOWN, m).wait_recv()
        for i in range(len(returns)):
            e_twin(i).wait_recv()
            e_onward(i).wait_recv()

        @pl.loop(0, starts[UP])
        def _(p):
            total = dot_tn(e_half[0], right[:, own_columns(p)]) + dot_tn(e_half[1], twin_right[:, twin_columns(p)])
            for source in range(2):
                total = total + dot_tn(e_half[2 + source], act_beside[source, :, twin_columns(p)])
            total = total.astype(BF16).reshape(LINE, chunk, PANEL)
            for part in range(STRIPS):
                for zz in range(LINE):
                    acc[(p * STRIPS + part) % RING, numbered(zz)] = total[zz, :, part * strip : (part + 1) * strip]

            @pl.when(is_end & (p < FIRST // STRIPS))
            def _():
                for part in range(STRIPS):
                    in_of(p * STRIPS + part).start()

    def enter(t):
        @pl.when((t < direct - FIRST) & is_end)
        def _():
            in_of(t + FIRST).start()

        @pl.when((t < direct) & is_inner)
        def _():
            out_of(t).start()

    def across_y(t):
        @pl.when((t >= direct) & (t < strips))
        def _():
            i = t - direct
            beside_of(t).wait()
            for d in range(LINE):
                total = parts[i % AHEAD, d, y].astype(F32) + pair_beside[i % (2 * AHEAD), d].astype(F32)
                acc[t % RING, d] = total.astype(BF16)

            @pl.when(is_end)
            def _():
                in_of(t).start()

            @pl.when(is_inner)
            def _():
                out_of(t).start()

            @pl.when(t + AHEAD < strips)
            def _():
                @pl.when(t % STRIPS == STRIPS - 1)
                def _():
                    form((t + AHEAD) // STRIPS)
                    for part in range(STRIPS):
                        beside_of(t + AHEAD - STRIPS + 1 + part).start()

    def relay(t):
        p = t - LAG

        @pl.when((p >= 0) & (p < strips) & is_inner)
        def _():
            in_of(p).wait_recv()
            add(acc.at[p % RING, pl.ds(2, 2)], pair_in.at[pl.ds(3 * (p % RING) + 1, 2)])
            far_of(p).start()
            across_of(p).start()
            add(acc.at[p % RING, 1], pair_in.at[3 * (p % RING)])

        r = t - END_LAG

        @pl.when(r >= 0)
        def _():
            @pl.when(is_end)
            def _():
                out_of(r).wait_recv()
                far_of(r).wait_recv()
                in_of(r).wait_send()
                finish(r, pair_in.at[2 * (r % END_RING)], pair_in.at[2 * (r % END_RING) + 1])

            @pl.when(is_inner)
            def _():
                across_of(r).wait()
                far_of(r).wait_send()
                out_of(r).wait_send()
                finish(r, pair_across.at[r % RING])

    def finish(r, *refs):
        for slot, which in enumerate((core, other_core)):
            here = pl.ds(pl.multiple_of(which * half_chunk, half_chunk), half_chunk)
            total = acc[r % RING, own, here].astype(F32)
            for ref in refs:
                total = total + ref[here].astype(F32)
            fin[slot, :, strip_columns(r)] = total

        @pl.when(r % LEAVING == LEAVING - 1)
        def _():
            fin_of(r // LEAVING).start()
            kept_of(r // LEAVING).start()

    def vectors_step(t):
        @pl.when(t == VECTORS[0])
        def _():
            vector_twin().wait()
            vector[...] += vectors[0]
            vector_beside().start()

        @pl.when(t == VECTORS[1])
        def _():
            vector_beside().wait()
            vector[...] += vectors[1]
            for step in range(1, LINE):
                vector_line(step).start()

    def proceed(low, high, parts_of_step):
        @pl.loop(low, high)
        def _(t):
            for part in parts_of_step:
                part(t)


    def after_du(m):
        @pl.when((m == MICRO - 1) & leads)
        def _():
            wait_for(UP)
            form_up(0, 1)
            start_strips(0, STRIPS)
            for i in range(len(returns)):
                gather_e(i)
            form_up(1, 2)
            start_strips(STRIPS, 2 * STRIPS)
            form_down()

    def after_middle(m):
        @pl.when((m == MICRO - 1) & leads)
        def _():
            form_up(2, AHEAD // STRIPS)
            start_strips(2 * STRIPS, AHEAD)
            proceed(0, BEFORE_HEADS, (enter, relay))

    def after_heads(m):
        @pl.when((m == MICRO - 1) & leads)
        def _():
            proceed(BEFORE_HEADS, BEFORE_LAST, (enter, relay))

    @pl.when(leads)
    def _():
        load_rows.wait()
        attend(0, load=True)

    pl.semaphore_wait(barrier, len(peers))

    @pl.when(jnp.logical_not(leads))
    def _():
        load_rows.wait()
        for i in range(len(returns)):
            spread(i)
        x_forward(0).wait_recv()
        attend(0, load=True)

    forward(0, load=True)

    @pl.when(jnp.logical_not(leads))
    def _():
        x_forward(1).wait_recv()

    attend(1)
    forward(1)
    share(0)

    @pl.loop(0, MICRO + 1)
    def _(step):
        @pl.when(step == section)
        def _():
            @pl.when(jnp.logical_not(leads))
            def _():
                x_forward(2).wait_recv()

            attend(2)
            forward(2)
            share(1)

            @pl.when(leads)
            def _():
                gather_act()

        @pl.when(step != section)
        def _():
            m = step // 2

            @pl.when(leads & (m == 0))
            def _():
                x_back(0).wait_recv()
                spread(0)

            @pl.when(leads & (m == 1))
            def _():
                for i in range(1, len(returns)):
                    x_back(i).wait_recv()
                    spread(i)

            backward(m, (after_du, after_middle, after_heads))

    vector_twin().start()

    @pl.when(jnp.logical_not(leads))
    def _():
        wait_for(UP)
        form_up(0, AHEAD // STRIPS)
        x_back(2).start()
        start_strips(0, AHEAD)
        for i in range(len(returns)):
            gather_e(i)
        x_back(1).wait_send()
        x_back(3).start()
        gather_act()
        form_down()

        proceed(0, BEFORE_LAST, (enter, relay))

    proceed(BEFORE_LAST, strips + END_LAG, (enter, relay, across_y, vectors_step))

    total = vector[:, chunk_at(z)]
    for step in range(1, LINE):
        vector_line(step).wait()
        total = total + vectors_line[step - 1]
    vector_out[...] = total

    for m in range(MICRO):
        for which in (UP, OUT, QKV):
            twin_left(which, m).wait_send()
        for which in range(4):
            twin_right_of(which, m).wait_send()
        a2_beside(m).wait_send()
        grads_store(m).wait()
        mixed_store(m).wait()

    for i in range(len(returns)):
        e_twin(i).wait_send()
        e_beside(i).wait_send()
        e_onward(i).wait_send()

    @pl.when(jnp.logical_not(leads))
    def _():
        for i in (0, 2, 3):
            x_back(i).wait_send()

    @pl.when(leads)
    def _():
        for i in range(len(spans)):
            x_forward(i).wait_send()

    @pl.loop(0, strips // LEAVING)
    def _(g):
        fin_of(g).wait()
        kept_of(g).wait()


def layers(tokens, cotangent, gains, biases, w_qkv, w_out, w_up, w_down):
    all_rows, width = tokens.shape
    hidden = w_up.shape[1]
    rows = all_rows // MICRO
    columns = 2 * hidden + 4 * width
    strip = PANEL // STRIPS
    strips = columns // CORES // strip
    chunk = width // (LINE * PAIR)
    dma = pltpu.SemaphoreType.DMA
    shapes = {
        "h": ((all_rows, width), BF16),
        "e": ((all_rows, width), BF16),
        "e_other": ((all_rows, width // 2), BF16),
        "result": ((all_rows, width), BF16),
        "w_qkv": (w_qkv.shape, BF16),
        "w_out": (w_out.shape, BF16),
        "w_up": (w_up.shape, BF16),
        "w_down": (w_down.shape, BF16),
        "left": ((3, CORES, all_rows, width), BF16),
        "e_half": ((4, all_rows, width // 2), BF16),
        "right": ((all_rows, columns), BF16),
        "twin_right": ((all_rows, columns // CORES), BF16),
        "act_beside": ((2, all_rows, hidden // CORES), BF16),
        "proj": ((all_rows, 3 * width), BF16),
        "middle": ((all_rows, width), F32),
        "slopes": ((all_rows, hidden), BF16),
        "probs": ((MICRO * HEADS, rows, rows), BF16),
        "bias": ((rows, rows), F32),
        "dctx": ((rows, width), BF16),
        "vector": ((8, width), F32),
        "parts": ((AHEAD, LINE, PAIR, chunk, strip), BF16),
        "acc": ((RING, LINE, chunk, strip), BF16),
        "fin": ((2, chunk // 2, columns // CORES), F32),
        "pair_beside": ((2 * AHEAD, LINE, chunk, strip), BF16),
        "pair_in": ((max(3 * RING, 2 * END_RING), chunk, strip), BF16),
        "pair_across": ((RING, chunk, strip), BF16),
        "vectors": ((2, 8, width), F32),
        "vectors_line": ((LINE - 1, 8, chunk), F32),
    }
    exchanges = {
        "x_forward": (3,), "x_back": (4,), "twin_left": (3, MICRO), "twin_right": (4, MICRO),
        "act_beside": (2, MICRO), "e_half": (3, 4), "pair_in": (RING,), "pair_across": (RING,),
        "fin": (strips // LEAVING,), "vector": (LINE + 1,),
    }
    semaphores = {"fetch": dma((7,)), "store": dma((2, MICRO)), "kept": dma((strips // LEAVING,))}
    for key, count in exchanges.items():
        semaphores[key + "_send"] = dma(count)
        semaphores[key + "_recv"] = dma(count)
    for key in ("pair_out", "pair_far"):
        semaphores[key + "_send"], semaphores[key + "_recv"] = dma((RING,)), dma((END_RING,))
    semaphores["pair_beside_send"], semaphores["pair_beside_recv"] = dma((AHEAD,)), dma((2 * AHEAD,))
    anywhere = pl.BlockSpec(memory_space=pl.ANY)
    in_vmem = pl.BlockSpec(memory_space=pltpu.VMEM)
    return pl.pallas_call(
        layer_kernel,
        out_shape=(
            jax.ShapeDtypeStruct((all_rows, width), BF16),
            jax.ShapeDtypeStruct((all_rows, width), BF16),
            jax.ShapeDtypeStruct((CORES, chunk // 2, columns // CORES), F32),
            jax.ShapeDtypeStruct((8, chunk), F32),
        ),
        in_specs=[anywhere] * 2 + [in_vmem] * 2 + [anywhere] * 4,
        out_specs=(anywhere, anywhere, anywhere, in_vmem),
        scratch_shapes=[{key: pltpu.VMEM(*shape) for key, shape in shapes.items()}, semaphores],
        compiler_params=pltpu.CompilerParams(
            collective_id=1, has_side_effects=True, vmem_limit_bytes=64 * 2**20
        ),
        name="relay_layers",
    )(tokens, cotangent, gains, biases, w_qkv, w_out, w_up, w_down)


def results_kernel(
    mixed_in, grads_in, block_in, vectors_in, mixed, grads, down, up, out, qkv, gains, biases,
    rows, block, vectors, shares, sem,
):
    started = []

    def copy(source, target):
        started.append(pltpu.make_async_copy(source, target, sem.at[len(started)]))
        started[-1].start()
        return started[-1]

    fetches = [copy(block_in.at[core], block.at[core]) for core in range(CORES)]
    fetches.append(copy(vectors_in, vectors))
    fetches += [copy(ref, rows.at[i]) for i, ref in enumerate((mixed_in, grads_in))]
    stores = []
    for core in range(CORES):
        fetches[core].wait()
        offset = 0
        for ref in (down, up, out, qkv):
            half = ref.shape[1] // CORES
            stores.append(copy(block.at[core, :, pl.ds(offset, half)], ref.at[:, pl.ds(core * half, half)]))
            offset += half
    fetches[CORES].wait()
    share = gains.shape[1]
    mine = lax.axis_index("dp") % CORES
    for core in range(CORES):
        @pl.when(mine == core)
        def _(core=core):
            here = slice(core * share, (core + 1) * share)
            shares[0] = vectors[0:2, here]
            shares[1] = vectors[2:4, here]

    stores += [copy(shares.at[i], ref) for i, ref in enumerate((gains, biases))]
    for i, ref in enumerate((mixed, grads)):
        fetches[CORES + 1 + i].wait()
        stores.append(copy(rows.at[i], ref))
    for store in stores:
        store.wait()


def results(mixed, grads, block, vectors, hidden):
    width, share = mixed.shape[1], block.shape[1]
    anywhere = pl.BlockSpec(memory_space=pl.ANY)
    shapes = ((share, hidden), (share, hidden), (share, width), (share, 3 * width), (2, share), (2, share))
    mixed, grads, down, up, out, qkv, gains, biases = pl.pallas_call(
        results_kernel,
        out_shape=(jax.ShapeDtypeStruct(mixed.shape, BF16), jax.ShapeDtypeStruct(grads.shape, BF16))
        + tuple(jax.ShapeDtypeStruct(shape, F32) for shape in shapes),
        in_specs=[anywhere] * 4,
        out_specs=(anywhere,) * 8,
        scratch_shapes=[
            pltpu.VMEM((2,) + mixed.shape, BF16), pltpu.VMEM(block.shape, F32), pltpu.VMEM(vectors.shape, F32),
            pltpu.VMEM((2, 2, share), F32), pltpu.SemaphoreType.DMA((CORES + 3 + 4 * CORES + 4,)),
        ],
        compiler_params=pltpu.CompilerParams(vmem_limit_bytes=64 * 2**20),
        name="place_results",
    )(mixed, grads, block, vectors)
    return mixed, grads, qkv, out.T, up, down.T, gains, biases


def reordered(member, axis, groups, back=False):
    shape = member.shape
    row = shape[axis] // (groups * GROUP)
    split = (GROUP, groups, row) if back else (groups, GROUP, row)
    apart = member.reshape(shape[:axis] + split + shape[axis + 1 :])
    return jnp.swapaxes(apart, axis, axis + 1).reshape(shape)


def on_device(tokens, cotangent, norm_gains, norm_biases, w_qkv, w_out, w_up, w_down):
    hidden, width = w_up.shape[2], tokens.shape[1]
    operands = (tokens, cotangent, norm_gains[0], norm_biases[0], w_qkv[0], w_out[0], w_up[0], w_down[0])
    groups = lax.axis_size("dp") // GROUP
    if groups > 1:
        axes = (1, 1, 1, 1, 0, 1, 0, 1)
        operands = tuple(reordered(member, axis, groups) for member, axis in zip(operands, axes))
    mixed, grads, block, vector_block = layers(*operands)
    if groups == 1:
        return tuple(member[None] for member in results(mixed, grads, block, vector_block, hidden))
    core = lax.axis_index("dp") % CORES
    share = block.shape[1]
    vector_block = lax.dynamic_slice_in_dim(vector_block[:4], core * share, share, 1)
    pieces = []
    offset = 0
    for member in (hidden, hidden, width, 3 * width):
        half = member // CORES
        part = block[:, :, offset : offset + half]
        pieces.append(jnp.concatenate([part[0], part[1]], axis=1))
        offset += half
    mixed, grads = (reordered(member, 1, groups, back=True) for member in (mixed, grads))
    same = [[g * GROUP + j for g in range(groups)] for j in range(GROUP)]

    def summed(member):
        return lax.psum_scatter(member, "dp", scatter_dimension=0, axis_index_groups=same, tiled=True)

    pieces = [summed(member) for member in pieces]
    vector_block = summed(vector_block.T).T
    down, up, out, qkv = pieces
    return (
        mixed[None], grads[None], qkv[None], out.T[None], up[None], down.T[None],
        vector_block[None, 0:2], vector_block[None, 2:4],
    )


def solution(mesh):
    placed = (P("dp", None),) * 2 + (P("section", None, None),) * 6
    return jax.shard_map(
        on_device,
        mesh=mesh,
        in_specs=placed,
        out_specs=(
            P("section", "dp", None),
            P("section", "dp", None),
            P("section", "dp", None),
            P("section", None, "dp"),
            P("section", "dp", None),
            P("section", None, "dp"),
            P("section", None, "dp"),
            P("section", None, "dp"),
        ),
        check_vma=False,
    )
```

```python
import math

import jax
import jax.numpy as jnp
from jax import lax
from jax.experimental import pallas as pl
from jax.experimental.pallas import tpu as pltpu
from jax.sharding import PartitionSpec as P

HEADS = 8
HEAD_DIM = 128
ITEM_LEN = 15
MICRO = 2
EPSILON = 1e-05

LINE, PAIR, CORES = 4, 2, 2
GROUP = LINE * PAIR * CORES
PANEL = 256
STRIPS = 2
AHEAD = 10
LAG = 2
END_LAG = 5
BEFORE_HEADS, BEFORE_LAST = 4, 5
RING = 8
END_RING = 12
VECTORS = 8, 20, 28
FIRST = 4
LEAVING = 8
MESH = pl.DeviceIdType.MESH
BF16, F32 = jnp.bfloat16, jnp.float32
DOWN, UP, OUT, QKV = range(4)


def dot(left, right):
    return jnp.dot(left, right, preferred_element_type=F32)


def dot_nt(left, right):
    return lax.dot_general(left, right, (((1,), (1,)), ((), ())), preferred_element_type=F32)


def dot_tn(left, right):
    return lax.dot_general(left, right, (((0,), (0,)), ((), ())), preferred_element_type=F32)


def normalized(values):
    centered = values - jnp.mean(values, axis=-1, keepdims=True)
    scale = lax.rsqrt(jnp.mean(centered * centered, axis=-1, keepdims=True) + EPSILON)
    return centered * scale, scale


def normalize_back(grad, unit, scale, gain):
    scaled = grad * gain
    along = jnp.mean(scaled * unit, axis=-1, keepdims=True)
    return scale * (scaled - jnp.mean(scaled, axis=-1, keepdims=True) - unit * along)


def gelu_and_slope(u):
    square = u * u
    inner = jnp.tanh(u * (0.7978845608 + 0.7978845608 * 0.044715 * square))
    part = 0.5 + 0.5 * inner
    steep = 0.5 * 0.7978845608 + 1.5 * 0.7978845608 * 0.044715 * square
    return u * part, part + u * (1.0 - inner * inner) * steep


def layer_kernel(
    tokens_in, cotangent_in, gains_in, biases_in, w_qkv_in, w_out_in, w_up_in, w_down_in,
    mixed_out, grads_out, out, vector_out, buf, sem,
):
    h, e, e_other, result = buf["h"], buf["e"], buf["e_other"], buf["result"]
    w_qkv, w_out, w_up, w_down = buf["w_qkv"], buf["w_out"], buf["w_up"], buf["w_down"]
    left, e_half, right, twin_right = buf["left"], buf["e_half"], buf["right"], buf["twin_right"]
    act_beside, proj, middle, slopes = buf["act_beside"], buf["proj"], buf["middle"], buf["slopes"]
    probs, bias, dctx, vector = buf["probs"], buf["bias"], buf["dctx"], buf["vector"]
    parts, acc, fin = buf["parts"], buf["acc"], buf["fin"]
    pair_beside, pair_in, pair_across = buf["pair_beside"], buf["pair_in"], buf["pair_across"]
    vectors, vectors_line, vector_total = buf["vectors"], buf["vectors_line"], buf["vector_total"]
    gains, biases = buf["gains"], buf["biases"]

    all_rows, width = h.shape
    rows = all_rows // MICRO
    front = rows // 32 * 16
    hidden = w_up.shape[1]
    chunk, half_chunk = acc.shape[2], acc.shape[2] // 2
    widths = (hidden, hidden, width, 3 * width)
    columns_at = (0, hidden, 2 * hidden, 2 * hidden + width)
    starts = [0]
    for member in widths:
        starts.append(starts[-1] + member // CORES // PANEL)
    strip = PANEL // STRIPS
    strips, direct = starts[-1] * STRIPS, starts[1] * STRIPS
    halves = [member // CORES for member in widths]
    twin_at = [start * PANEL for start in starts]

    section = lax.axis_index("section")
    place = lax.axis_index("dp")
    first = (place // GROUP) * GROUP
    mine = place - first
    z, y, core = mine // (PAIR * CORES), (mine // CORES) % PAIR, mine % CORES
    other_y, other_core = 1 - y, 1 - core
    far_side = z // 2
    is_end = (z == 0) | (z == LINE - 1)
    is_inner = jnp.logical_not(is_end)
    own = jnp.where(is_end, 0, 1)

    def numbered(zz):
        return zz + far_side * (LINE - 1 - 2 * zz)

    def device(zz, yy, cc):
        return (section, first + (zz * PAIR + yy) * CORES + cc)

    beside, twin = device(z, other_y, core), device(z, y, other_core)
    partner = (1 - section, place)
    leads = section == 0

    def send(source, target, key, index, to, landing=None):
        return pltpu.make_async_remote_copy(
            src_ref=source, dst_ref=target, send_sem=sem[key + "_send"].at[index],
            recv_sem=sem[key + "_recv"].at[index if landing is None else landing], device_id=to, device_id_type=MESH,
        )

    def fetch(source, target, index):
        return pltpu.make_async_copy(source, target, sem["fetch"].at[index])

    def rows_of(m):
        return pl.ds(pl.multiple_of(m * rows, rows), rows)

    loads = [fetch(w_out_in, w_out, 0), fetch(w_up_in, w_up, 1), fetch(w_down_in, w_down, 2)]
    loads_qkv = [
        fetch(w_qkv_in.at[:, pl.ds(part * width, width)], w_qkv.at[:, pl.ds(part * width, width)], 3 + part)
        for part in range(3)
    ]
    load_rows = [fetch(tokens_in.at[at], h.at[at], 6 + i) for i, at in enumerate((pl.ds(0, front), pl.ds(front, all_rows - front)))]
    load_cotangent = fetch(cotangent_in, e, 6)
    load_norms = [fetch(gains_in, gains, 8), fetch(biases_in, biases, 9)]

    @pl.when(leads)
    def _():
        load_rows[0].start()

    @pl.when(jnp.logical_not(leads))
    def _():
        load_cotangent.start()

    for load in load_norms + loads_qkv[:2]:
        load.start()
    barrier = pltpu.get_barrier_semaphore()
    lined = [device((z + step) % LINE, y, core) for step in range(1, LINE)]
    inner, end, across, far_end = (device(numbered(zz), y, core) for zz in (1, 0, 2, 3))
    peers = [partner, twin, beside] + lined
    for peer in peers:
        pl.semaphore_signal(barrier, inc=1, device_id=peer, device_id_type=MESH)
    loads_qkv[2].start()

    @pl.when(leads)
    def _():
        load_rows[1].start()

    @pl.when(jnp.logical_not(leads))
    def _():
        for load in loads:
            load.start()

    row_ids = lax.broadcasted_iota(jnp.int32, (rows, 1), 0)
    col_ids = lax.broadcasted_iota(jnp.int32, (1, rows), 1)
    seen = (row_ids // ITEM_LEN == col_ids // ITEM_LEN) & (col_ids <= row_ids)
    bias[...] = jnp.where(seen, 0.0, -1e30)
    vector[...] = jnp.zeros_like(vector)
    proj[front:rows, width:] = jnp.zeros((rows - front, 2 * width), BF16)
    scale = 1.0 / math.sqrt(HEAD_DIM)


    spans = ((0, front), (front, rows), (rows, 2 * rows))

    def x_forward(i):
        at = pl.ds(spans[i][0], spans[i][1] - spans[i][0])
        return send(result.at[at], h.at[at], "x_forward", i, partner)

    late = rows // 5
    returns = ((0, rows), (rows, 2 * rows - front), (2 * rows - front, 2 * rows - late), (2 * rows - late, 2 * rows))

    def returned(i):
        return pl.ds(returns[i][0], returns[i][1] - returns[i][0])

    def x_back(i):
        return send(h.at[returned(i)], e.at[returned(i)], "x_back", i, partner)

    def mixed_store(m):
        return pltpu.make_async_copy(result.at[rows_of(m)], mixed_out.at[rows_of(m)], sem["store"].at[0, m])

    def grads_store(m):
        return pltpu.make_async_copy(h.at[rows_of(m)], grads_out.at[rows_of(m)], sem["store"].at[1, m])

    def twin_left(which, m):
        return send(left.at[which - 1, 0, rows_of(m)], left.at[which - 1, 1, rows_of(m)],
                    "twin_left", (which - 1, m), twin)

    def twin_right_of(which, m):
        start = pl.multiple_of(columns_at[which] + other_core * halves[which], 128)
        return send(right.at[rows_of(m), pl.ds(start, halves[which])],
                    twin_right.at[rows_of(m), pl.ds(twin_at[which], halves[which])],
                    "twin_right", (which, m), twin)

    def a2_beside(m):
        return send(left.at[UP - 1, 0, rows_of(m)], act_beside.at[0, rows_of(m)], "act_beside", (0, m), beside)

    def a2_onward(m):
        return send(act_beside.at[0, rows_of(m)], act_beside.at[1, rows_of(m)], "act_beside", (1, m), twin)

    def e_twin(i):
        return send(e_half.at[0, returned(i)], e_half.at[1, returned(i)], "e_half", (0, i), twin)

    def e_beside(i):
        return send(e_other.at[returned(i)], e_half.at[2, returned(i)], "e_half", (1, i), beside)

    def e_onward(i):
        return send(e_half.at[2, returned(i)], e_half.at[3, returned(i)], "e_half", (2, i), twin)


    def attend(i, load=False, first_section=False):
        low, high = spans[i]
        at, m = slice(low, high), low // rows
        whole = slice(m * rows, (m + 1) * rows)
        unit, unused = normalized(h[at].astype(F32))
        left[QKV - 1, 0, at] = (unit * gains[0:1] + biases[0:1]).astype(BF16)
        for part in range(3):
            cols = slice(part * width, (part + 1) * width)
            if load:
                loads_qkv[part].wait()
            if load and first_section:
                loads[part].start()
            proj[at, cols] = dot(left[QKV - 1, 0, at], w_qkv[:, cols]).astype(BF16)

        def heads_of(part, head):
            start = part * width + head * HEAD_DIM
            return proj[whole, start : start + HEAD_DIM]

        for head in range(HEADS):
            scores = dot_nt(heads_of(0, head), heads_of(1, head)) * scale + bias[...]
            weight = jnp.exp(scores - jnp.max(scores, axis=-1, keepdims=True))
            probs[m * HEADS + head] = (weight / jnp.sum(weight, axis=-1, keepdims=True)).astype(BF16)
        for head in range(HEADS):
            cols = slice(columns_at[OUT] + head * HEAD_DIM, columns_at[OUT] + (head + 1) * HEAD_DIM)
            right[whole, cols] = dot(probs[m * HEADS + head], heads_of(2, head)).astype(BF16)

    def forward(i, load=False):
        at = slice(*spans[i])
        if load:
            loads[0].wait()
        attended = dot(right[at, columns_at[OUT] : columns_at[OUT] + width], w_out[...])
        middle[at] = h[at].astype(F32) + attended
        unit, unused = normalized(middle[at])
        left[UP - 1, 0, at] = (unit * gains[1:2] + biases[1:2]).astype(BF16)
        if i > 0:
            a2_beside(i - 1).start()
        if load:
            loads[1].wait()
        for part in range(2):
            cols = slice(part * hidden // 2, (part + 1) * hidden // 2)
            upward = dot(left[UP - 1, 0, at], w_up[:, cols])
            active, slope = gelu_and_slope(upward)
            slopes[at, cols] = slope.astype(BF16)
            right[at, cols] = active.astype(BF16)
        if load:
            loads[2].wait()
        result[at] = (middle[at] + dot(right[at, :hidden], w_down[...])).astype(BF16)

        @pl.when(leads)
        def _():
            x_forward(i).start()

    def share(m):
        mixed_store(m).start()
        twin_right_of(DOWN, m).start()
        twin_right_of(OUT, m).start()
        twin_left(QKV, m).start()
        twin_left(UP, m).start()

    def gather_act():
        cols = pl.ds(pl.multiple_of(core * halves[DOWN], 128), halves[DOWN])

        @pl.loop(0, MICRO)
        def _(m):
            a2_beside(m).wait_recv()
            a2_onward(m).start()
            a2_onward(m).wait()

            @pl.loop(0, 2)
            def _(source):
                active, unused = gelu_and_slope(dot(act_beside[source, rows_of(m)], w_up[:, cols]))
                act_beside[source, rows_of(m)] = active.astype(BF16)

    def spread(i):
        at = returned(i)
        for zz in range(LINE):
            cols = pl.ds(zz * chunk, chunk)
            e_half[0, at, cols] = e[at, pl.ds(pl.multiple_of((zz * PAIR + y) * chunk, chunk), chunk)]
            e_other[at, cols] = e[at, pl.ds(pl.multiple_of((zz * PAIR + other_y) * chunk, chunk), chunk)]
        e_beside(i).start()
        e_twin(i).start()

    def backward(m, hooks):
        at = rows_of(m)

        for part in (other_core, core):
            start = pl.multiple_of(part * halves[UP], halves[UP])
            cols = pl.ds(start, halves[UP])
            passed = dot_nt(e[at], w_down[cols])
            right[at, pl.ds(columns_at[UP] + start, halves[UP])] = (passed * slopes[at, cols].astype(F32)).astype(BF16)
            if part is other_core:
                twin_right_of(UP, m).start()

        hooks[0](m)
        grad = dot_nt(right[at, columns_at[UP] : columns_at[UP] + hidden], w_up[...])
        unit, size = normalized(middle[at])
        vector[1:2] += jnp.sum(grad * unit, axis=0, keepdims=True)
        vector[3:4] += jnp.sum(grad, axis=0, keepdims=True)
        middle[at] = e[at].astype(F32) + normalize_back(grad, unit, size, gains[1:2])
        left[OUT - 1, 0, at] = middle[at].astype(BF16)
        twin_left(OUT, m).start()
        dctx[...] = dot_nt(left[OUT - 1, 0, at], w_out[...]).astype(BF16)
        hooks[1](m)

        def heads_of(part, head):
            start = part * width + head * HEAD_DIM
            return proj[at, start : start + HEAD_DIM]

        def keep(part, head, value):
            start = columns_at[QKV] + part * width + head * HEAD_DIM
            right[at, start : start + HEAD_DIM] = value.astype(BF16)

        def grad_ctx(head):
            return dctx[:, head * HEAD_DIM : (head + 1) * HEAD_DIM]

        grad_scores = []
        for head in range(HEADS):
            weight = probs[m * HEADS + head].astype(F32)
            grad_weight = dot_nt(grad_ctx(head), heads_of(2, head))
            total = jnp.sum(weight * grad_weight, axis=-1, keepdims=True)
            grad_scores.append((weight * (grad_weight - total)).astype(BF16))
        for head in range(HEADS):
            keep(2, head, dot_tn(probs[m * HEADS + head], grad_ctx(head)))
        for head in range(HEADS):
            keep(0, head, dot(grad_scores[head], heads_of(1, head)) * scale)
            keep(1, head, dot_tn(grad_scores[head], heads_of(0, head)) * scale)

        twin_right_of(QKV, m).start()
        hooks[2](m)
        grad = dot_nt(right[at, columns_at[QKV] : columns_at[QKV] + 3 * width], w_qkv[...])
        unit, size = normalized(h[at].astype(F32))
        vector[0:1] += jnp.sum(grad * unit, axis=0, keepdims=True)
        vector[2:3] += jnp.sum(grad, axis=0, keepdims=True)
        h[at] = (middle[at] + normalize_back(grad, unit, size, gains[0:1])).astype(BF16)
        grads_store(m).start()

        @pl.when(jnp.logical_not(leads))
        def _():
            @pl.when(m == 0)
            def _():
                x_back(0).start()

            @pl.when(m == 1)
            def _():
                x_back(1).start()


    def beside_of(p):
        i = p - direct
        here, there = i % AHEAD, i % (2 * AHEAD)
        return send(parts.at[here, :, other_y], pair_beside.at[there], "pair_beside", here, beside, there)

    def in_of(p):
        return send(acc.at[p % RING, pl.ds(1, 3)], pair_in.at[pl.ds(3 * (p % RING), 3)], "pair_in", p % RING, inner)

    def across_of(p):
        return send(acc.at[p % RING, 2], pair_across.at[p % RING], "pair_across", p % RING, across)

    def far_of(p):
        there = p % END_RING
        return send(acc.at[p % RING, 3], pair_in.at[2 * there + 1], "pair_far", p % RING, far_end, there)

    def out_of(p):
        there = p % END_RING
        return send(acc.at[p % RING, 0], pair_in.at[2 * there], "pair_out", p % RING, end, there)

    def chunk_at(zz):
        return pl.ds(pl.multiple_of((zz * PAIR + y) * chunk, chunk), chunk)

    vector_store = pltpu.make_async_copy(vector_total, vector_out, sem["vector_store"].at[0])

    def vector_twin():
        return send(vector, vectors.at[0], "vector", 0, twin)

    def vector_beside():
        return send(vector, vectors.at[1], "vector", 1, beside)

    def vector_line(step):
        return send(vector.at[:, chunk_at((z + step) % LINE)], vectors_line.at[step - 1], "vector", 1 + step, lined[step - 1])

    def strip_columns(p):
        return pl.ds(pl.multiple_of(p * strip, strip), strip)

    def fin_of(g):
        cols = pl.ds(pl.multiple_of(g * LEAVING * strip, LEAVING * strip), LEAVING * strip)
        return send(fin.at[1, :, cols], out.at[core, :, cols], "fin", g, twin)

    def kept_of(g):
        cols = pl.ds(pl.multiple_of(g * LEAVING * strip, LEAVING * strip), LEAVING * strip)
        return pltpu.make_async_copy(fin.at[0, :, cols], out.at[core, :, cols], sem["kept"].at[g])

    def add(target, *refs):
        total = target[...].astype(F32)
        for ref in refs:
            total = total + ref[...].astype(F32)
        target[...] = total.astype(BF16)

    def own_columns(p):
        place_of = p * PANEL + core * halves[0]
        for i in (1, 2, 3):
            shift = (columns_at[i] - twin_at[i] + core * halves[i]) - (
                columns_at[i - 1] - twin_at[i - 1] + core * halves[i - 1])
            place_of = place_of + jnp.where(p >= starts[i], shift, 0)
        return pl.ds(pl.multiple_of(place_of, 128), PANEL)

    def twin_columns(p):
        return pl.ds(pl.multiple_of(p * PANEL, PANEL), PANEL)

    def wait_for(which):
        for m in range(MICRO):
            twin_left(which, m).wait_recv()
            twin_right_of(which, m).wait_recv()

    def form(p):
        which = 0
        for i in (OUT, QKV):
            which = which + (p >= starts[i]).astype(jnp.int32)

            @pl.when(p == starts[i])
            def _(i=i):
                wait_for(i)

        total = dot_tn(left[which, 0], right[:, own_columns(p)]) + dot_tn(left[which, 1], twin_right[:, twin_columns(p)])
        total = total.astype(BF16).reshape(LINE, PAIR, chunk, PANEL)
        for part in range(STRIPS):
            for zz in range(LINE):
                here = total[zz, :, :, part * strip : (part + 1) * strip]
                parts[(p * STRIPS + part - direct) % AHEAD, numbered(zz)] = here

    def form_up(low, high):
        @pl.loop(starts[UP] + low, starts[UP] + high)
        def _(p):
            form(p)

    def start_strips(low, high):
        @pl.loop(direct + low, direct + high)
        def _(p):
            beside_of(p).start()

    def gather_e(i):
        e_beside(i).wait_recv()
        e_onward(i).start()

    def form_down():
        for m in range(MICRO):
            twin_right_of(DOWN, m).wait_recv()
        for i in range(len(returns)):
            e_twin(i).wait_recv()
            e_onward(i).wait_recv()

        @pl.loop(0, starts[UP])
        def _(p):
            total = dot_tn(e_half[0], right[:, own_columns(p)]) + dot_tn(e_half[1], twin_right[:, twin_columns(p)])
            for source in range(2):
                total = total + dot_tn(e_half[2 + source], act_beside[source, :, twin_columns(p)])
            total = total.astype(BF16).reshape(LINE, chunk, PANEL)
            for part in range(STRIPS):
                for zz in range(LINE):
                    acc[(p * STRIPS + part) % RING, numbered(zz)] = total[zz, :, part * strip : (part + 1) * strip]

            @pl.when(is_end & (p < FIRST // STRIPS))
            def _():
                for part in range(STRIPS):
                    in_of(p * STRIPS + part).start()

    def enter(t):
        @pl.when((t < direct - FIRST) & is_end)
        def _():
            in_of(t + FIRST).start()

        @pl.when((t < direct) & is_inner)
        def _():
            out_of(t).start()

    def across_y(t):
        @pl.when((t >= direct) & (t < strips))
        def _():
            i = t - direct
            beside_of(t).wait()
            for d in range(LINE):
                total = parts[i % AHEAD, d, y].astype(F32) + pair_beside[i % (2 * AHEAD), d].astype(F32)
                acc[t % RING, d] = total.astype(BF16)

            @pl.when(is_end)
            def _():
                in_of(t).start()

            @pl.when(is_inner)
            def _():
                out_of(t).start()

            @pl.when(t + AHEAD < strips)
            def _():
                @pl.when(t % STRIPS == STRIPS - 1)
                def _():
                    form((t + AHEAD) // STRIPS)
                    for part in range(STRIPS):
                        beside_of(t + AHEAD - STRIPS + 1 + part).start()

    def relay(t):
        p = t - LAG

        @pl.when((p >= 0) & (p < strips) & is_inner)
        def _():
            in_of(p).wait_recv()
            add(acc.at[p % RING, pl.ds(2, 2)], pair_in.at[pl.ds(3 * (p % RING) + 1, 2)])
            far_of(p).start()
            across_of(p).start()
            add(acc.at[p % RING, 1], pair_in.at[3 * (p % RING)])

        r = t - END_LAG

        @pl.when(r >= 0)
        def _():
            @pl.when(is_end)
            def _():
                out_of(r).wait_recv()
                far_of(r).wait_recv()
                in_of(r).wait_send()
                finish(r, pair_in.at[2 * (r % END_RING)], pair_in.at[2 * (r % END_RING) + 1])

            @pl.when(is_inner)
            def _():
                across_of(r).wait()
                far_of(r).wait_send()
                out_of(r).wait_send()
                finish(r, pair_across.at[r % RING])

    def finish(r, *refs):
        for slot, which in enumerate((core, other_core)):
            here = pl.ds(pl.multiple_of(which * half_chunk, half_chunk), half_chunk)
            total = acc[r % RING, own, here].astype(F32)
            for ref in refs:
                total = total + ref[here].astype(F32)
            fin[slot, :, strip_columns(r)] = total

        @pl.when(r % LEAVING == LEAVING - 1)
        def _():
            fin_of(r // LEAVING).start()
            kept_of(r // LEAVING).start()

    def vectors_step(t):
        @pl.when(t == VECTORS[0])
        def _():
            vector_twin().wait()
            vector[...] += vectors[0]
            vector_beside().start()

        @pl.when(t == VECTORS[1])
        def _():
            vector_beside().wait()
            vector[...] += vectors[1]
            for step in range(1, LINE):
                vector_line(step).start()

        @pl.when(t == VECTORS[2])
        def _():
            total = vector[:, chunk_at(z)]
            for step in range(1, LINE):
                vector_line(step).wait()
                total = total + vectors_line[step - 1]
            vector_total[...] = total
            vector_store.start()

    def proceed(low, high, parts_of_step):
        @pl.loop(low, high)
        def _(t):
            for part in parts_of_step:
                part(t)


    def after_du(m):
        @pl.when((m == MICRO - 1) & leads)
        def _():
            wait_for(UP)
            form_up(0, 1)
            start_strips(0, STRIPS)
            for i in range(len(returns)):
                gather_e(i)
            form_up(1, 2)
            start_strips(STRIPS, 2 * STRIPS)
            form_down()

    def after_middle(m):
        @pl.when((m == MICRO - 1) & leads)
        def _():
            form_up(2, AHEAD // STRIPS)
            start_strips(2 * STRIPS, AHEAD)
            proceed(0, BEFORE_HEADS, (enter, relay))

    def after_heads(m):
        @pl.when((m == MICRO - 1) & leads)
        def _():
            proceed(BEFORE_HEADS, BEFORE_LAST, (enter, relay))

    @pl.when(leads)
    def _():
        for load in load_rows[:1] + load_norms:
            load.wait()
        attend(0, load=True, first_section=True)

    pl.semaphore_wait(barrier, len(peers))

    @pl.when(jnp.logical_not(leads))
    def _():
        for load in [load_cotangent] + load_norms:
            load.wait()
        for i in range(len(returns)):
            spread(i)
        x_forward(0).wait_recv()
        attend(0, load=True)

    forward(0, load=True)

    @pl.when(leads)
    def _():
        load_rows[1].wait()

    @pl.when(jnp.logical_not(leads))
    def _():
        x_forward(1).wait_recv()

    attend(1)
    forward(1)
    share(0)

    @pl.loop(0, MICRO + 1)
    def _(step):
        @pl.when(step == section)
        def _():
            @pl.when(jnp.logical_not(leads))
            def _():
                x_forward(2).wait_recv()

            attend(2)
            forward(2)
            share(1)

            @pl.when(leads)
            def _():
                gather_act()

        @pl.when(step != section)
        def _():
            m = step // 2

            @pl.when(leads & (m == 0))
            def _():
                x_back(0).wait_recv()
                spread(0)

            @pl.when(leads & (m == 1))
            def _():
                for i in range(1, len(returns)):
                    x_back(i).wait_recv()
                    spread(i)

            backward(m, (after_du, after_middle, after_heads))

    vector_twin().start()

    @pl.when(jnp.logical_not(leads))
    def _():
        wait_for(UP)
        form_up(0, AHEAD // STRIPS)
        x_back(2).start()
        start_strips(0, AHEAD)
        for i in range(len(returns)):
            gather_e(i)
        x_back(1).wait_send()
        x_back(3).start()
        gather_act()
        form_down()

        proceed(0, BEFORE_LAST, (enter, relay))

    proceed(BEFORE_LAST, strips + END_LAG, (enter, relay, across_y, vectors_step))

    vector_store.wait()
    for m in range(MICRO):
        for which in (UP, OUT, QKV):
            twin_left(which, m).wait_send()
        for which in range(4):
            twin_right_of(which, m).wait_send()
        a2_beside(m).wait_send()
        grads_store(m).wait()
        mixed_store(m).wait()

    for i in range(len(returns)):
        e_twin(i).wait_send()
        e_beside(i).wait_send()
        e_onward(i).wait_send()

    @pl.when(jnp.logical_not(leads))
    def _():
        for i in (0, 2, 3):
            x_back(i).wait_send()

    @pl.when(leads)
    def _():
        for i in range(len(spans)):
            x_forward(i).wait_send()

    @pl.loop(0, strips // LEAVING)
    def _(g):
        fin_of(g).wait()
        kept_of(g).wait()


def layers(tokens, cotangent, gains, biases, w_qkv, w_out, w_up, w_down):
    all_rows, width = tokens.shape
    hidden = w_up.shape[1]
    rows = all_rows // MICRO
    columns = 2 * hidden + 4 * width
    strip = PANEL // STRIPS
    strips = columns // CORES // strip
    chunk = width // (LINE * PAIR)
    dma = pltpu.SemaphoreType.DMA
    shapes = {
        "h": ((all_rows, width), BF16),
        "e": ((all_rows, width), BF16),
        "e_other": ((all_rows, width // 2), BF16),
        "result": ((all_rows, width), BF16),
        "w_qkv": (w_qkv.shape, BF16),
        "w_out": (w_out.shape, BF16),
        "w_up": (w_up.shape, BF16),
        "w_down": (w_down.shape, BF16),
        "left": ((3, CORES, all_rows, width), BF16),
        "e_half": ((4, all_rows, width // 2), BF16),
        "right": ((all_rows, columns), BF16),
        "twin_right": ((all_rows, columns // CORES), BF16),
        "act_beside": ((2, all_rows, hidden // CORES), BF16),
        "proj": ((all_rows, 3 * width), BF16),
        "middle": ((all_rows, width), F32),
        "slopes": ((all_rows, hidden), BF16),
        "probs": ((MICRO * HEADS, rows, rows), BF16),
        "bias": ((rows, rows), F32),
        "dctx": ((rows, width), BF16),
        "vector": ((8, width), F32),
        "parts": ((AHEAD, LINE, PAIR, chunk, strip), BF16),
        "acc": ((RING, LINE, chunk, strip), BF16),
        "fin": ((2, chunk // 2, columns // CORES), F32),
        "pair_beside": ((2 * AHEAD, LINE, chunk, strip), BF16),
        "pair_in": ((max(3 * RING, 2 * END_RING), chunk, strip), BF16),
        "pair_across": ((RING, chunk, strip), BF16),
        "vectors": ((2, 8, width), F32),
        "vectors_line": ((LINE - 1, 8, chunk), F32),
        "vector_total": ((8, chunk), F32),
        "gains": (gains.shape, F32),
        "biases": (biases.shape, F32),
    }
    exchanges = {
        "x_forward": (3,), "x_back": (4,), "twin_left": (3, MICRO), "twin_right": (4, MICRO),
        "act_beside": (2, MICRO), "e_half": (3, 4), "pair_in": (RING,), "pair_across": (RING,),
        "fin": (strips // LEAVING,), "vector": (LINE + 1,),
    }
    semaphores = {"fetch": dma((10,)), "vector_store": dma((1,)), "store": dma((2, MICRO)), "kept": dma((strips // LEAVING,))}
    for key, count in exchanges.items():
        semaphores[key + "_send"] = dma(count)
        semaphores[key + "_recv"] = dma(count)
    for key in ("pair_out", "pair_far"):
        semaphores[key + "_send"], semaphores[key + "_recv"] = dma((RING,)), dma((END_RING,))
    semaphores["pair_beside_send"], semaphores["pair_beside_recv"] = dma((AHEAD,)), dma((2 * AHEAD,))
    anywhere = pl.BlockSpec(memory_space=pl.ANY)
    return pl.pallas_call(
        layer_kernel,
        out_shape=(
            jax.ShapeDtypeStruct((all_rows, width), BF16),
            jax.ShapeDtypeStruct((all_rows, width), BF16),
            jax.ShapeDtypeStruct((CORES, chunk // 2, columns // CORES), F32),
            jax.ShapeDtypeStruct((8, chunk), F32),
        ),
        in_specs=[anywhere] * 8,
        out_specs=(anywhere,) * 4,
        scratch_shapes=[{key: pltpu.VMEM(*shape) for key, shape in shapes.items()}, semaphores],
        compiler_params=pltpu.CompilerParams(
            collective_id=1, has_side_effects=True, vmem_limit_bytes=64 * 2**20
        ),
        name="relay_layers",
    )(tokens, cotangent, gains, biases, w_qkv, w_out, w_up, w_down)


def results_kernel(
    mixed_in, grads_in, block_in, vectors_in, mixed, grads, down, up, out, qkv, gains, biases,
    rows, block, vectors, shares, sem,
):
    started = []

    def copy(source, target):
        started.append(pltpu.make_async_copy(source, target, sem.at[len(started)]))
        started[-1].start()
        return started[-1]

    fetches = [copy(block_in.at[core], block.at[core]) for core in range(CORES)]
    fetches.append(copy(vectors_in, vectors))
    fetches += [copy(ref, rows.at[i]) for i, ref in enumerate((mixed_in, grads_in))]
    stores = []
    for core in range(CORES):
        fetches[core].wait()
        offset = 0
        for ref in (down, up, out, qkv):
            half = ref.shape[1] // CORES
            stores.append(copy(block.at[core, :, pl.ds(offset, half)], ref.at[:, pl.ds(core * half, half)]))
            offset += half
    fetches[CORES].wait()
    share = gains.shape[1]
    mine = lax.axis_index("dp") % CORES
    for core in range(CORES):
        @pl.when(mine == core)
        def _(core=core):
            here = slice(core * share, (core + 1) * share)
            shares[0] = vectors[0:2, here]
            shares[1] = vectors[2:4, here]

    stores += [copy(shares.at[i], ref) for i, ref in enumerate((gains, biases))]
    for i, ref in enumerate((mixed, grads)):
        fetches[CORES + 1 + i].wait()
        stores.append(copy(rows.at[i], ref))
    for store in stores:
        store.wait()


def results(mixed, grads, block, vectors, hidden):
    width, share = mixed.shape[1], block.shape[1]
    anywhere = pl.BlockSpec(memory_space=pl.ANY)
    shapes = ((share, hidden), (share, hidden), (share, width), (share, 3 * width), (2, share), (2, share))
    mixed, grads, down, up, out, qkv, gains, biases = pl.pallas_call(
        results_kernel,
        out_shape=(jax.ShapeDtypeStruct(mixed.shape, BF16), jax.ShapeDtypeStruct(grads.shape, BF16))
        + tuple(jax.ShapeDtypeStruct(shape, F32) for shape in shapes),
        in_specs=[anywhere] * 4,
        out_specs=(anywhere,) * 8,
        scratch_shapes=[
            pltpu.VMEM((2,) + mixed.shape, BF16), pltpu.VMEM(block.shape, F32), pltpu.VMEM(vectors.shape, F32),
            pltpu.VMEM((2, 2, share), F32), pltpu.SemaphoreType.DMA((CORES + 3 + 4 * CORES + 4,)),
        ],
        compiler_params=pltpu.CompilerParams(vmem_limit_bytes=64 * 2**20),
        name="place_results",
    )(mixed, grads, block, vectors)
    return mixed, grads, qkv, out.T, up, down.T, gains, biases


def reordered(member, axis, groups, back=False):
    shape = member.shape
    row = shape[axis] // (groups * GROUP)
    split = (GROUP, groups, row) if back else (groups, GROUP, row)
    apart = member.reshape(shape[:axis] + split + shape[axis + 1 :])
    return jnp.swapaxes(apart, axis, axis + 1).reshape(shape)


def on_device(tokens, cotangent, norm_gains, norm_biases, w_qkv, w_out, w_up, w_down):
    hidden, width = w_up.shape[2], tokens.shape[1]
    operands = (tokens, cotangent, norm_gains[0], norm_biases[0], w_qkv[0], w_out[0], w_up[0], w_down[0])
    groups = lax.axis_size("dp") // GROUP
    if groups > 1:
        axes = (1, 1, 1, 1, 0, 1, 0, 1)
        operands = tuple(reordered(member, axis, groups) for member, axis in zip(operands, axes))
    mixed, grads, block, vector_block = layers(*operands)
    if groups == 1:
        return tuple(member[None] for member in results(mixed, grads, block, vector_block, hidden))
    core = lax.axis_index("dp") % CORES
    share = block.shape[1]
    vector_block = lax.dynamic_slice_in_dim(vector_block[:4], core * share, share, 1)
    pieces = []
    offset = 0
    for member in (hidden, hidden, width, 3 * width):
        half = member // CORES
        part = block[:, :, offset : offset + half]
        pieces.append(jnp.concatenate([part[0], part[1]], axis=1))
        offset += half
    mixed, grads = (reordered(member, 1, groups, back=True) for member in (mixed, grads))
    same = [[g * GROUP + j for g in range(groups)] for j in range(GROUP)]

    def summed(member):
        return lax.psum_scatter(member, "dp", scatter_dimension=0, axis_index_groups=same, tiled=True)

    pieces = [summed(member) for member in pieces]
    vector_block = summed(vector_block.T).T
    down, up, out, qkv = pieces
    return (
        mixed[None], grads[None], qkv[None], out.T[None], up[None], down.T[None],
        vector_block[None, 0:2], vector_block[None, 2:4],
    )


def solution(mesh):
    placed = (P("dp", None),) * 2 + (P("section", None, None),) * 6
    return jax.shard_map(
        on_device,
        mesh=mesh,
        in_specs=placed,
        out_specs=(
            P("section", "dp", None),
            P("section", "dp", None),
            P("section", "dp", None),
            P("section", None, "dp"),
            P("section", "dp", None),
            P("section", None, "dp"),
            P("section", None, "dp"),
            P("section", None, "dp"),
        ),
        check_vma=False,
    )
```

```python
import math

import jax
import jax.numpy as jnp
from jax import lax
from jax.experimental import pallas as pl
from jax.experimental.pallas import tpu as pltpu
from jax.sharding import PartitionSpec as P

HEADS = 8
HEAD_DIM = 128
ITEM_LEN = 15
MICRO = 2
EPSILON = 1e-05

LINE, PAIR, CORES = 4, 2, 2
GROUP = LINE * PAIR * CORES
PANEL = 256
STRIPS = 2
AHEAD = 8
LAG = 2
END_LAG = 5
BEFORE_HEADS, BEFORE_LAST = 4, 6
RING = 8
END_RING = 12
VECTORS = 8, 20, 28
SPARE, ACROSS, BACK = 12, 12, 20
FIRST = 4
LEAVING = 8
MESH = pl.DeviceIdType.MESH
BF16, F32 = jnp.bfloat16, jnp.float32
DOWN, UP, OUT, QKV = range(4)


def dot(left, right):
    return jnp.dot(left, right, preferred_element_type=F32)


def dot_nt(left, right):
    return lax.dot_general(left, right, (((1,), (1,)), ((), ())), preferred_element_type=F32)


def dot_tn(left, right):
    return lax.dot_general(left, right, (((0,), (0,)), ((), ())), preferred_element_type=F32)


def normalized(values):
    centered = values - jnp.mean(values, axis=-1, keepdims=True)
    scale = lax.rsqrt(jnp.mean(centered * centered, axis=-1, keepdims=True) + EPSILON)
    return centered * scale, scale


def normalize_back(grad, unit, scale, gain):
    scaled = grad * gain
    along = jnp.mean(scaled * unit, axis=-1, keepdims=True)
    return scale * (scaled - jnp.mean(scaled, axis=-1, keepdims=True) - unit * along)


def gelu_and_slope(u):
    square = u * u
    inner = jnp.tanh(u * (0.7978845608 + 0.7978845608 * 0.044715 * square))
    part = 0.5 + 0.5 * inner
    steep = 0.5 * 0.7978845608 + 1.5 * 0.7978845608 * 0.044715 * square
    return u * part, part + u * (1.0 - inner * inner) * steep


def layer_kernel(
    tokens_in, cotangent_in, gains_in, biases_in, w_qkv_in, w_out_in, w_up_in, w_down_in,
    mixed_out, grads_out, out, vector_out, buf, sem,
):
    h, e, e_other, result = buf["h"], buf["e"], buf["e_other"], buf["result"]
    w_qkv, w_out, w_up, w_down = buf["w_qkv"], buf["w_out"], buf["w_up"], buf["w_down"]
    left, e_half, right, twin_right = buf["left"], buf["e_half"], buf["right"], buf["twin_right"]
    act_beside, proj, middle, slopes = buf["act_beside"], buf["proj"], buf["middle"], buf["slopes"]
    probs, bias, dctx, vector = buf["probs"], buf["bias"], buf["dctx"], buf["vector"]
    parts, acc, fin = buf["parts"], buf["acc"], buf["fin"]
    pair_beside, pair_in, pair_across = buf["pair_beside"], buf["pair_in"], buf["pair_across"]
    vectors, vectors_line, vector_total = buf["vectors"], buf["vectors_line"], buf["vector_total"]
    gains, biases = buf["gains"], buf["biases"]
    spare_parts, spare_in, spare_across = buf["spare_parts"], buf["spare_in"], buf["spare_across"]

    all_rows, width = h.shape
    rows = all_rows // MICRO
    front = rows // 32 * 16
    hidden = w_up.shape[1]
    chunk, half_chunk = acc.shape[2], acc.shape[2] // 2
    widths = (hidden, hidden, width, 3 * width)
    columns_at = (0, hidden, 2 * hidden, 2 * hidden + width)
    starts = [0]
    for member in widths:
        starts.append(starts[-1] + member // CORES // PANEL)
    strip = PANEL // STRIPS
    strips, direct = starts[-1] * STRIPS, starts[1] * STRIPS
    halves = [member // CORES for member in widths]
    twin_at = [start * PANEL for start in starts]

    section = lax.axis_index("section")
    place = lax.axis_index("dp")
    first = (place // GROUP) * GROUP
    mine = place - first
    z, y, core = mine // (PAIR * CORES), (mine // CORES) % PAIR, mine % CORES
    other_y, other_core = 1 - y, 1 - core
    far_side = z // 2
    is_end = (z == 0) | (z == LINE - 1)
    is_inner = jnp.logical_not(is_end)
    own = jnp.where(is_end, 0, 1)

    def numbered(zz):
        return zz + far_side * (LINE - 1 - 2 * zz)

    def device(zz, yy, cc):
        return (section, first + (zz * PAIR + yy) * CORES + cc)

    beside, twin = device(z, other_y, core), device(z, y, other_core)
    partner = (1 - section, place)
    leads = section == 0

    def send(source, target, key, index, to, landing=None):
        return pltpu.make_async_remote_copy(
            src_ref=source, dst_ref=target, send_sem=sem[key + "_send"].at[index],
            recv_sem=sem[key + "_recv"].at[index if landing is None else landing], device_id=to, device_id_type=MESH,
        )

    def fetch(source, target, index):
        return pltpu.make_async_copy(source, target, sem["fetch"].at[index])

    def rows_of(m):
        return pl.ds(pl.multiple_of(m * rows, rows), rows)

    loads = [fetch(w_out_in, w_out, 0), fetch(w_up_in, w_up, 1), fetch(w_down_in, w_down, 2)]
    loads_qkv = [
        fetch(w_qkv_in.at[:, pl.ds(part * width, width)], w_qkv.at[:, pl.ds(part * width, width)], 3 + part)
        for part in range(3)
    ]
    load_rows = [fetch(tokens_in.at[at], h.at[at], 6 + i) for i, at in enumerate((pl.ds(0, front), pl.ds(front, all_rows - front)))]
    load_cotangent = fetch(cotangent_in, e, 6)
    load_norms = [fetch(gains_in, gains, 8), fetch(biases_in, biases, 9)]

    @pl.when(leads)
    def _():
        load_rows[0].start()

    @pl.when(jnp.logical_not(leads))
    def _():
        load_cotangent.start()

    for load in load_norms + loads_qkv[:2]:
        load.start()
    barrier = pltpu.get_barrier_semaphore()
    lined = [device((z + step) % LINE, y, core) for step in range(1, LINE)]
    inner, end, across, far_end = (device(numbered(zz), y, core) for zz in (1, 0, 2, 3))
    peers = [partner, twin, beside] + lined
    for peer in peers:
        pl.semaphore_signal(barrier, inc=1, device_id=peer, device_id_type=MESH)
    loads_qkv[2].start()

    @pl.when(leads)
    def _():
        load_rows[1].start()

    @pl.when(jnp.logical_not(leads))
    def _():
        for load in loads:
            load.start()

    row_ids = lax.broadcasted_iota(jnp.int32, (rows, 1), 0)
    col_ids = lax.broadcasted_iota(jnp.int32, (1, rows), 1)
    seen = (row_ids // ITEM_LEN == col_ids // ITEM_LEN) & (col_ids <= row_ids)
    bias[...] = jnp.where(seen, 0.0, -1e30)
    vector[...] = jnp.zeros_like(vector)
    proj[front:rows, width:] = jnp.zeros((rows - front, 2 * width), BF16)
    scale = 1.0 / math.sqrt(HEAD_DIM)


    spans = ((0, front), (front, rows), (rows, 2 * rows))

    def x_forward(i):
        at = pl.ds(spans[i][0], spans[i][1] - spans[i][0])
        return send(result.at[at], h.at[at], "x_forward", i, partner)

    late = rows // 5
    returns = ((0, rows), (rows, 2 * rows - front), (2 * rows - front, 2 * rows - late), (2 * rows - late, 2 * rows))

    def returned(i):
        return pl.ds(returns[i][0], returns[i][1] - returns[i][0])

    def x_back(i):
        return send(h.at[returned(i)], e.at[returned(i)], "x_back", i, partner)

    def mixed_store(m):
        return pltpu.make_async_copy(result.at[rows_of(m)], mixed_out.at[rows_of(m)], sem["store"].at[0, m])

    def grads_store(m):
        return pltpu.make_async_copy(h.at[rows_of(m)], grads_out.at[rows_of(m)], sem["store"].at[1, m])

    def twin_left(which, m):
        return send(left.at[which - 1, 0, rows_of(m)], left.at[which - 1, 1, rows_of(m)],
                    "twin_left", (which - 1, m), twin)

    def twin_right_of(which, m):
        start = pl.multiple_of(columns_at[which] + other_core * halves[which], 128)
        return send(right.at[rows_of(m), pl.ds(start, halves[which])],
                    twin_right.at[rows_of(m), pl.ds(twin_at[which], halves[which])],
                    "twin_right", (which, m), twin)

    def a2_beside(m):
        return send(left.at[UP - 1, 0, rows_of(m)], act_beside.at[0, rows_of(m)], "act_beside", (0, m), beside)

    def a2_onward(m):
        return send(act_beside.at[0, rows_of(m)], act_beside.at[1, rows_of(m)], "act_beside", (1, m), twin)

    def e_twin(i):
        return send(e_half.at[0, returned(i)], e_half.at[1, returned(i)], "e_half", (0, i), twin)

    def e_beside(i):
        return send(e_other.at[returned(i)], e_half.at[2, returned(i)], "e_half", (1, i), beside)

    def e_onward(i):
        return send(e_half.at[2, returned(i)], e_half.at[3, returned(i)], "e_half", (2, i), twin)


    def attend(i, load=False, first_section=False):
        low, high = spans[i]
        at, m = slice(low, high), low // rows
        whole = slice(m * rows, (m + 1) * rows)
        unit, unused = normalized(h[at].astype(F32))
        left[QKV - 1, 0, at] = (unit * gains[0:1] + biases[0:1]).astype(BF16)
        for part in range(3):
            cols = slice(part * width, (part + 1) * width)
            if load:
                loads_qkv[part].wait()
            if load and first_section:
                loads[part].start()
            proj[at, cols] = dot(left[QKV - 1, 0, at], w_qkv[:, cols]).astype(BF16)

        def heads_of(part, head):
            start = part * width + head * HEAD_DIM
            return proj[whole, start : start + HEAD_DIM]

        for head in range(HEADS):
            scores = dot_nt(heads_of(0, head), heads_of(1, head)) * scale + bias[...]
            weight = jnp.exp(scores - jnp.max(scores, axis=-1, keepdims=True))
            probs[m * HEADS + head] = (weight / jnp.sum(weight, axis=-1, keepdims=True)).astype(BF16)
        for head in range(HEADS):
            cols = slice(columns_at[OUT] + head * HEAD_DIM, columns_at[OUT] + (head + 1) * HEAD_DIM)
            right[whole, cols] = dot(probs[m * HEADS + head], heads_of(2, head)).astype(BF16)

    def forward(i, load=False):
        at = slice(*spans[i])
        if load:
            loads[0].wait()
        attended = dot(right[at, columns_at[OUT] : columns_at[OUT] + width], w_out[...])
        middle[at] = h[at].astype(F32) + attended
        unit, unused = normalized(middle[at])
        left[UP - 1, 0, at] = (unit * gains[1:2] + biases[1:2]).astype(BF16)
        if i > 0:
            a2_beside(i - 1).start()
        if load:
            loads[1].wait()
        for part in range(2):
            cols = slice(part * hidden // 2, (part + 1) * hidden // 2)
            upward = dot(left[UP - 1, 0, at], w_up[:, cols])
            active, slope = gelu_and_slope(upward)
            slopes[at, cols] = slope.astype(BF16)
            right[at, cols] = active.astype(BF16)
        if load:
            loads[2].wait()
        result[at] = (middle[at] + dot(right[at, :hidden], w_down[...])).astype(BF16)

        @pl.when(leads)
        def _():
            x_forward(i).start()

    def share(m):
        mixed_store(m).start()
        twin_right_of(DOWN, m).start()
        twin_right_of(OUT, m).start()
        twin_left(QKV, m).start()
        twin_left(UP, m).start()

    def gather_act():
        cols = pl.ds(pl.multiple_of(core * halves[DOWN], 128), halves[DOWN])

        @pl.loop(0, MICRO)
        def _(m):
            a2_beside(m).wait_recv()
            a2_onward(m).start()
            a2_onward(m).wait()

            @pl.loop(0, 2)
            def _(source):
                active, unused = gelu_and_slope(dot(act_beside[source, rows_of(m)], w_up[:, cols]))
                act_beside[source, rows_of(m)] = active.astype(BF16)

    def spread(i):
        at = returned(i)
        for zz in range(LINE):
            cols = pl.ds(zz * chunk, chunk)
            e_half[0, at, cols] = e[at, pl.ds(pl.multiple_of((zz * PAIR + y) * chunk, chunk), chunk)]
            e_other[at, cols] = e[at, pl.ds(pl.multiple_of((zz * PAIR + other_y) * chunk, chunk), chunk)]
        e_beside(i).start()
        e_twin(i).start()

    def backward(m, hooks):
        at = rows_of(m)

        for part in (other_core, core):
            start = pl.multiple_of(part * halves[UP], halves[UP])
            cols = pl.ds(start, halves[UP])
            passed = dot_nt(e[at], w_down[cols])
            right[at, pl.ds(columns_at[UP] + start, halves[UP])] = (passed * slopes[at, cols].astype(F32)).astype(BF16)
            if part is other_core:
                twin_right_of(UP, m).start()

        hooks[0](m)
        grad = dot_nt(right[at, columns_at[UP] : columns_at[UP] + hidden], w_up[...])
        unit, size = normalized(middle[at])
        vector[1:2] += jnp.sum(grad * unit, axis=0, keepdims=True)
        vector[3:4] += jnp.sum(grad, axis=0, keepdims=True)
        middle[at] = e[at].astype(F32) + normalize_back(grad, unit, size, gains[1:2])
        left[OUT - 1, 0, at] = middle[at].astype(BF16)
        twin_left(OUT, m).start()
        dctx[...] = dot_nt(left[OUT - 1, 0, at], w_out[...]).astype(BF16)
        hooks[1](m)

        def heads_of(part, head):
            start = part * width + head * HEAD_DIM
            return proj[at, start : start + HEAD_DIM]

        def keep(part, head, value):
            start = columns_at[QKV] + part * width + head * HEAD_DIM
            right[at, start : start + HEAD_DIM] = value.astype(BF16)

        def grad_ctx(head):
            return dctx[:, head * HEAD_DIM : (head + 1) * HEAD_DIM]

        grad_scores = []
        for head in range(HEADS):
            weight = probs[m * HEADS + head].astype(F32)
            grad_weight = dot_nt(grad_ctx(head), heads_of(2, head))
            total = jnp.sum(weight * grad_weight, axis=-1, keepdims=True)
            grad_scores.append((weight * (grad_weight - total)).astype(BF16))
        for head in range(HEADS):
            keep(2, head, dot_tn(probs[m * HEADS + head], grad_ctx(head)))
        for head in range(HEADS):
            keep(0, head, dot(grad_scores[head], heads_of(1, head)) * scale)
            keep(1, head, dot_tn(grad_scores[head], heads_of(0, head)) * scale)

        twin_right_of(QKV, m).start()
        hooks[2](m)
        grad = dot_nt(right[at, columns_at[QKV] : columns_at[QKV] + 3 * width], w_qkv[...])
        unit, size = normalized(h[at].astype(F32))
        vector[0:1] += jnp.sum(grad * unit, axis=0, keepdims=True)
        vector[2:3] += jnp.sum(grad, axis=0, keepdims=True)
        h[at] = (middle[at] + normalize_back(grad, unit, size, gains[0:1])).astype(BF16)
        grads_store(m).start()

        @pl.when(jnp.logical_not(leads))
        def _():
            @pl.when(m == 0)
            def _():
                x_back(0).start()

            @pl.when(m == 1)
            def _():
                x_back(1).start()


    def beside_of(p):
        i = p - direct
        here, there = i % AHEAD, i % (2 * AHEAD)
        return send(parts.at[here, :, other_y], pair_beside.at[there], "pair_beside", here, beside, there)

    def spare_out(part):
        return send(spare_parts.at[part, :, other_y], spare_in.at[part], "spare", part, partner)

    def spare_beside(part, d):
        return send(spare_in.at[part, d], spare_across.at[part, d], "spare_across", (part, d), beside)

    def spare_back(part):
        return send(spare_across.at[part], spare_in.at[part], "spare", part, partner)

    def each_spare(act):
        for part in range(STRIPS):
            for d in range(LINE):
                act(spare_beside(part, d))

    def in_of(p):
        return send(acc.at[p % RING, pl.ds(1, 3)], pair_in.at[pl.ds(3 * (p % RING), 3)], "pair_in", p % RING, inner)

    def across_of(p):
        return send(acc.at[p % RING, 2], pair_across.at[p % RING], "pair_across", p % RING, across)

    def far_of(p):
        there = p % END_RING
        return send(acc.at[p % RING, 3], pair_in.at[2 * there + 1], "pair_far", p % RING, far_end, there)

    def out_of(p):
        there = p % END_RING
        return send(acc.at[p % RING, 0], pair_in.at[2 * there], "pair_out", p % RING, end, there)

    def chunk_at(zz):
        return pl.ds(pl.multiple_of((zz * PAIR + y) * chunk, chunk), chunk)

    vector_store = pltpu.make_async_copy(vector_total, vector_out, sem["vector_store"].at[0])

    def vector_twin():
        return send(vector, vectors.at[0], "vector", 0, twin)

    def vector_beside():
        return send(vector, vectors.at[1], "vector", 1, beside)

    def vector_line(step):
        return send(vector.at[:, chunk_at((z + step) % LINE)], vectors_line.at[step - 1], "vector", 1 + step, lined[step - 1])

    def strip_columns(p):
        return pl.ds(pl.multiple_of(p * strip, strip), strip)

    def fin_of(g):
        cols = pl.ds(pl.multiple_of(g * LEAVING * strip, LEAVING * strip), LEAVING * strip)
        return send(fin.at[1, :, cols], out.at[core, :, cols], "fin", g, twin)

    def kept_of(g):
        cols = pl.ds(pl.multiple_of(g * LEAVING * strip, LEAVING * strip), LEAVING * strip)
        return pltpu.make_async_copy(fin.at[0, :, cols], out.at[core, :, cols], sem["kept"].at[g])

    def add(target, *refs):
        total = target[...].astype(F32)
        for ref in refs:
            total = total + ref[...].astype(F32)
        target[...] = total.astype(BF16)

    def own_columns(p):
        place_of = p * PANEL + core * halves[0]
        for i in (1, 2, 3):
            shift = (columns_at[i] - twin_at[i] + core * halves[i]) - (
                columns_at[i - 1] - twin_at[i - 1] + core * halves[i - 1])
            place_of = place_of + jnp.where(p >= starts[i], shift, 0)
        return pl.ds(pl.multiple_of(place_of, 128), PANEL)

    def twin_columns(p):
        return pl.ds(pl.multiple_of(p * PANEL, PANEL), PANEL)

    def wait_for(which):
        for m in range(MICRO):
            twin_left(which, m).wait_recv()
            twin_right_of(which, m).wait_recv()

    def form(p, spare=False):
        which = QKV - 1 if spare else 0
        for i in () if spare else (OUT, QKV):
            which = which + (p >= starts[i]).astype(jnp.int32)
            due = p == starts[i] if i == OUT else (p == starts[i]) & jnp.logical_not(leads)

            @pl.when(due)
            def _(i=i):
                wait_for(i)

        total = dot_tn(left[which, 0], right[:, own_columns(p)]) + dot_tn(left[which, 1], twin_right[:, twin_columns(p)])
        total = total.astype(BF16).reshape(LINE, PAIR, chunk, PANEL)
        for part in range(STRIPS):
            for zz in range(LINE):
                here = total[zz, :, :, part * strip : (part + 1) * strip]
                if spare:
                    spare_parts[part, numbered(zz)] = here
                else:
                    parts[(p * STRIPS + part - direct) % AHEAD, numbered(zz)] = here

    def form_up(low, high):
        @pl.loop(starts[UP] + low, starts[UP] + high)
        def _(p):
            form(p)

    def start_strips(low, high):
        @pl.loop(direct + low, direct + high)
        def _(p):
            beside_of(p).start()

    def gather_e(i):
        e_beside(i).wait_recv()
        e_onward(i).start()

    def form_down():
        for m in range(MICRO):
            twin_right_of(DOWN, m).wait_recv()
        for i in range(len(returns)):
            e_twin(i).wait_recv()
            e_onward(i).wait_recv()

        @pl.loop(0, starts[UP])
        def _(p):
            total = dot_tn(e_half[0], right[:, own_columns(p)]) + dot_tn(e_half[1], twin_right[:, twin_columns(p)])
            for source in range(2):
                total = total + dot_tn(e_half[2 + source], act_beside[source, :, twin_columns(p)])
            total = total.astype(BF16).reshape(LINE, chunk, PANEL)
            for part in range(STRIPS):
                for zz in range(LINE):
                    acc[(p * STRIPS + part) % RING, numbered(zz)] = total[zz, :, part * strip : (part + 1) * strip]

            @pl.when(is_end & (p < FIRST // STRIPS))
            def _():
                for part in range(STRIPS):
                    in_of(p * STRIPS + part).start()

    def enter(t):
        @pl.when((t < direct - FIRST) & is_end)
        def _():
            in_of(t + FIRST).start()

        @pl.when((t < direct) & is_inner)
        def _():
            out_of(t).start()

    def across_y(t):
        def enter_line(mine_of, theirs_of):
            for d in range(LINE):
                acc[t % RING, d] = (mine_of(d).astype(F32) + theirs_of(d).astype(F32)).astype(BF16)

            @pl.when(is_end)
            def _():
                in_of(t).start()

            @pl.when(is_inner)
            def _():
                out_of(t).start()

        spared = leads & (t // STRIPS == SPARE)

        @pl.when((t >= direct) & (t < strips) & jnp.logical_not(spared))
        def _():
            i = t - direct
            beside_of(t).wait()
            enter_line(lambda d: parts[i % AHEAD, d, y], lambda d: pair_beside[i % (2 * AHEAD), d])

            panel = (t + AHEAD) // STRIPS

            @pl.when((t + AHEAD < strips) & (t % STRIPS == STRIPS - 1) & jnp.logical_not(leads & (panel == SPARE)))
            def _():
                form(panel)
                for part in range(STRIPS):
                    beside_of(t + AHEAD - STRIPS + 1 + part).start()

        @pl.when(spared)
        def _():
            part = t % STRIPS
            spare_back(part).wait_recv()
            enter_line(lambda d: spare_parts[part, d, y], lambda d: spare_in[part, d])

        @pl.when((t == ACROSS) & jnp.logical_not(leads))
        def _():
            for part in range(STRIPS):
                spare_out(part).wait_recv()
            each_spare(lambda message: message.start())

        @pl.when((t == BACK) & jnp.logical_not(leads))
        def _():
            each_spare(lambda message: message.wait_recv())
            for part in range(STRIPS):
                spare_back(part).start()

    def relay(t):
        p = t - LAG

        @pl.when((p >= 0) & (p < strips) & is_inner)
        def _():
            in_of(p).wait_recv()
            add(acc.at[p % RING, pl.ds(2, 2)], pair_in.at[pl.ds(3 * (p % RING) + 1, 2)])
            far_of(p).start()
            across_of(p).start()
            add(acc.at[p % RING, 1], pair_in.at[3 * (p % RING)])

        r = t - END_LAG

        @pl.when(r >= 0)
        def _():
            @pl.when(is_end)
            def _():
                out_of(r).wait_recv()
                far_of(r).wait_recv()
                in_of(r).wait_send()
                finish(r, pair_in.at[2 * (r % END_RING)], pair_in.at[2 * (r % END_RING) + 1])

            @pl.when(is_inner)
            def _():
                across_of(r).wait()
                far_of(r).wait_send()
                out_of(r).wait_send()
                finish(r, pair_across.at[r % RING])

    def finish(r, *refs):
        for slot, which in enumerate((core, other_core)):
            here = pl.ds(pl.multiple_of(which * half_chunk, half_chunk), half_chunk)
            total = acc[r % RING, own, here].astype(F32)
            for ref in refs:
                total = total + ref[here].astype(F32)
            fin[slot, :, strip_columns(r)] = total

        @pl.when(r % LEAVING == LEAVING - 1)
        def _():
            fin_of(r // LEAVING).start()
            kept_of(r // LEAVING).start()

    def vectors_step(t):
        @pl.when(t == VECTORS[0])
        def _():
            vector_twin().wait()
            vector[...] += vectors[0]
            vector_beside().start()

        @pl.when(t == VECTORS[1])
        def _():
            vector_beside().wait()
            vector[...] += vectors[1]
            for step in range(1, LINE):
                vector_line(step).start()

        @pl.when(t == VECTORS[2])
        def _():
            total = vector[:, chunk_at(z)]
            for step in range(1, LINE):
                vector_line(step).wait()
                total = total + vectors_line[step - 1]
            vector_total[...] = total
            vector_store.start()

    def proceed(low, high, parts_of_step):
        @pl.loop(low, high)
        def _(t):
            for part in parts_of_step:
                part(t)


    def after_du(m):
        @pl.when((m == MICRO - 1) & leads)
        def _():
            wait_for(UP)
            form_up(0, 1)
            start_strips(0, STRIPS)
            for i in range(len(returns)):
                gather_e(i)
            form_up(1, 2)
            start_strips(STRIPS, 2 * STRIPS)
            form_down()

    def after_middle(m):
        @pl.when((m == MICRO - 1) & leads)
        def _():
            form_up(2, AHEAD // STRIPS)
            start_strips(2 * STRIPS, AHEAD)
            proceed(0, BEFORE_HEADS, (enter, relay))

    def after_heads(m):
        @pl.when((m == MICRO - 1) & leads)
        def _():
            proceed(BEFORE_HEADS, BEFORE_LAST, (enter, relay))

    @pl.when(leads)
    def _():
        for load in load_rows[:1] + load_norms:
            load.wait()
        attend(0, load=True, first_section=True)

    pl.semaphore_wait(barrier, len(peers))

    @pl.when(jnp.logical_not(leads))
    def _():
        for load in [load_cotangent] + load_norms:
            load.wait()
        for i in range(len(returns)):
            spread(i)
        x_forward(0).wait_recv()
        attend(0, load=True)

    forward(0, load=True)

    @pl.when(leads)
    def _():
        load_rows[1].wait()

    @pl.when(jnp.logical_not(leads))
    def _():
        x_forward(1).wait_recv()

    attend(1)
    forward(1)
    share(0)

    @pl.loop(0, MICRO + 1)
    def _(step):
        @pl.when(step == section)
        def _():
            @pl.when(jnp.logical_not(leads))
            def _():
                x_forward(2).wait_recv()

            attend(2)
            forward(2)
            share(1)

            @pl.when(leads)
            def _():
                gather_act()

        @pl.when(step != section)
        def _():
            m = step // 2

            @pl.when(leads & (m == 0))
            def _():
                x_back(0).wait_recv()
                spread(0)

            @pl.when(leads & (m == 1))
            def _():
                for i in range(1, len(returns)):
                    x_back(i).wait_recv()
                    spread(i)

            backward(m, (after_du, after_middle, after_heads))

    vector_twin().start()

    @pl.when(leads)
    def _():
        wait_for(QKV)
        form(SPARE, spare=True)
        for part in range(STRIPS):
            spare_out(part).start()

    @pl.when(jnp.logical_not(leads))
    def _():
        wait_for(UP)
        form_up(0, AHEAD // STRIPS)
        x_back(2).start()
        start_strips(0, AHEAD)
        for i in range(len(returns)):
            gather_e(i)
        x_back(1).wait_send()
        x_back(3).start()
        gather_act()
        form_down()

        proceed(0, BEFORE_LAST, (enter, relay))

    proceed(BEFORE_LAST, strips + END_LAG, (enter, relay, across_y, vectors_step))

    vector_store.wait()
    for part in range(STRIPS):
        spare_out(part).wait_send()

    @pl.when(jnp.logical_not(leads))
    def _():
        each_spare(lambda message: message.wait_send())

    for m in range(MICRO):
        for which in (UP, OUT, QKV):
            twin_left(which, m).wait_send()
        for which in range(4):
            twin_right_of(which, m).wait_send()
        a2_beside(m).wait_send()
        grads_store(m).wait()
        mixed_store(m).wait()

    for i in range(len(returns)):
        e_twin(i).wait_send()
        e_beside(i).wait_send()
        e_onward(i).wait_send()

    @pl.when(jnp.logical_not(leads))
    def _():
        for i in (0, 2, 3):
            x_back(i).wait_send()

    @pl.when(leads)
    def _():
        for i in range(len(spans)):
            x_forward(i).wait_send()

    @pl.loop(0, strips // LEAVING)
    def _(g):
        fin_of(g).wait()
        kept_of(g).wait()


def layers(tokens, cotangent, gains, biases, w_qkv, w_out, w_up, w_down):
    all_rows, width = tokens.shape
    hidden = w_up.shape[1]
    rows = all_rows // MICRO
    columns = 2 * hidden + 4 * width
    strip = PANEL // STRIPS
    strips = columns // CORES // strip
    chunk = width // (LINE * PAIR)
    dma = pltpu.SemaphoreType.DMA
    shapes = {
        "h": ((all_rows, width), BF16),
        "e": ((all_rows, width), BF16),
        "e_other": ((all_rows, width // 2), BF16),
        "result": ((all_rows, width), BF16),
        "w_qkv": (w_qkv.shape, BF16),
        "w_out": (w_out.shape, BF16),
        "w_up": (w_up.shape, BF16),
        "w_down": (w_down.shape, BF16),
        "left": ((3, CORES, all_rows, width), BF16),
        "e_half": ((4, all_rows, width // 2), BF16),
        "right": ((all_rows, columns), BF16),
        "twin_right": ((all_rows, columns // CORES), BF16),
        "act_beside": ((2, all_rows, hidden // CORES), BF16),
        "proj": ((all_rows, 3 * width), BF16),
        "middle": ((all_rows, width), F32),
        "slopes": ((all_rows, hidden), BF16),
        "probs": ((MICRO * HEADS, rows, rows), BF16),
        "bias": ((rows, rows), F32),
        "dctx": ((rows, width), BF16),
        "vector": ((8, width), F32),
        "parts": ((AHEAD, LINE, PAIR, chunk, strip), BF16),
        "acc": ((RING, LINE, chunk, strip), BF16),
        "fin": ((2, chunk // 2, columns // CORES), F32),
        "pair_beside": ((2 * AHEAD, LINE, chunk, strip), BF16),
        "pair_in": ((max(3 * RING, 2 * END_RING), chunk, strip), BF16),
        "pair_across": ((RING, chunk, strip), BF16),
        "spare_parts": ((STRIPS, LINE, PAIR, chunk, strip), BF16),
        "spare_in": ((STRIPS, LINE, chunk, strip), BF16),
        "spare_across": ((STRIPS, LINE, chunk, strip), BF16),
        "vectors": ((2, 8, width), F32),
        "vectors_line": ((LINE - 1, 8, chunk), F32),
        "vector_total": ((8, chunk), F32),
        "gains": (gains.shape, F32),
        "biases": (biases.shape, F32),
    }
    exchanges = {
        "x_forward": (3,), "x_back": (4,), "twin_left": (3, MICRO), "twin_right": (4, MICRO),
        "act_beside": (2, MICRO), "e_half": (3, 4), "pair_in": (RING,), "pair_across": (RING,),
        "fin": (strips // LEAVING,), "spare": (STRIPS,), "spare_across": (STRIPS, LINE), "vector": (LINE + 1,),
    }
    semaphores = {"fetch": dma((10,)), "vector_store": dma((1,)), "store": dma((2, MICRO)), "kept": dma((strips // LEAVING,))}
    for key, count in exchanges.items():
        semaphores[key + "_send"] = dma(count)
        semaphores[key + "_recv"] = dma(count)
    for key in ("pair_out", "pair_far"):
        semaphores[key + "_send"], semaphores[key + "_recv"] = dma((RING,)), dma((END_RING,))
    semaphores["pair_beside_send"], semaphores["pair_beside_recv"] = dma((AHEAD,)), dma((2 * AHEAD,))
    anywhere = pl.BlockSpec(memory_space=pl.ANY)
    return pl.pallas_call(
        layer_kernel,
        out_shape=(
            jax.ShapeDtypeStruct((all_rows, width), BF16),
            jax.ShapeDtypeStruct((all_rows, width), BF16),
            jax.ShapeDtypeStruct((CORES, chunk // 2, columns // CORES), F32),
            jax.ShapeDtypeStruct((8, chunk), F32),
        ),
        in_specs=[anywhere] * 8,
        out_specs=(anywhere,) * 4,
        scratch_shapes=[{key: pltpu.VMEM(*shape) for key, shape in shapes.items()}, semaphores],
        compiler_params=pltpu.CompilerParams(
            collective_id=1, has_side_effects=True, vmem_limit_bytes=64 * 2**20
        ),
        name="relay_layers",
    )(tokens, cotangent, gains, biases, w_qkv, w_out, w_up, w_down)


def results_kernel(
    mixed_in, grads_in, block_in, vectors_in, mixed, grads, down, up, out, qkv, gains, biases,
    rows, block, vectors, shares, sem,
):
    started = []

    def copy(source, target):
        started.append(pltpu.make_async_copy(source, target, sem.at[len(started)]))
        started[-1].start()
        return started[-1]

    fetches = [copy(block_in.at[core], block.at[core]) for core in range(CORES)]
    fetches.append(copy(vectors_in, vectors))
    fetches += [copy(ref, rows.at[i]) for i, ref in enumerate((mixed_in, grads_in))]
    stores = []
    for core in range(CORES):
        fetches[core].wait()
        offset = 0
        for ref in (down, up, out, qkv):
            half = ref.shape[1] // CORES
            stores.append(copy(block.at[core, :, pl.ds(offset, half)], ref.at[:, pl.ds(core * half, half)]))
            offset += half
    fetches[CORES].wait()
    share = gains.shape[1]
    mine = lax.axis_index("dp") % CORES
    for core in range(CORES):
        @pl.when(mine == core)
        def _(core=core):
            here = slice(core * share, (core + 1) * share)
            shares[0] = vectors[0:2, here]
            shares[1] = vectors[2:4, here]

    stores += [copy(shares.at[i], ref) for i, ref in enumerate((gains, biases))]
    for i, ref in enumerate((mixed, grads)):
        fetches[CORES + 1 + i].wait()
        stores.append(copy(rows.at[i], ref))
    for store in stores:
        store.wait()


def results(mixed, grads, block, vectors, hidden):
    width, share = mixed.shape[1], block.shape[1]
    anywhere = pl.BlockSpec(memory_space=pl.ANY)
    shapes = ((share, hidden), (share, hidden), (share, width), (share, 3 * width), (2, share), (2, share))
    mixed, grads, down, up, out, qkv, gains, biases = pl.pallas_call(
        results_kernel,
        out_shape=(jax.ShapeDtypeStruct(mixed.shape, BF16), jax.ShapeDtypeStruct(grads.shape, BF16))
        + tuple(jax.ShapeDtypeStruct(shape, F32) for shape in shapes),
        in_specs=[anywhere] * 4,
        out_specs=(anywhere,) * 8,
        scratch_shapes=[
            pltpu.VMEM((2,) + mixed.shape, BF16), pltpu.VMEM(block.shape, F32), pltpu.VMEM(vectors.shape, F32),
            pltpu.VMEM((2, 2, share), F32), pltpu.SemaphoreType.DMA((CORES + 3 + 4 * CORES + 4,)),
        ],
        compiler_params=pltpu.CompilerParams(vmem_limit_bytes=64 * 2**20),
        name="place_results",
    )(mixed, grads, block, vectors)
    return mixed, grads, qkv, out.T, up, down.T, gains, biases


def reordered(member, axis, groups, back=False):
    shape = member.shape
    row = shape[axis] // (groups * GROUP)
    split = (GROUP, groups, row) if back else (groups, GROUP, row)
    apart = member.reshape(shape[:axis] + split + shape[axis + 1 :])
    return jnp.swapaxes(apart, axis, axis + 1).reshape(shape)


def on_device(tokens, cotangent, norm_gains, norm_biases, w_qkv, w_out, w_up, w_down):
    hidden, width = w_up.shape[2], tokens.shape[1]
    operands = (tokens, cotangent, norm_gains[0], norm_biases[0], w_qkv[0], w_out[0], w_up[0], w_down[0])
    groups = lax.axis_size("dp") // GROUP
    if groups > 1:
        axes = (1, 1, 1, 1, 0, 1, 0, 1)
        operands = tuple(reordered(member, axis, groups) for member, axis in zip(operands, axes))
    mixed, grads, block, vector_block = layers(*operands)
    if groups == 1:
        return tuple(member[None] for member in results(mixed, grads, block, vector_block, hidden))
    core = lax.axis_index("dp") % CORES
    share = block.shape[1]
    vector_block = lax.dynamic_slice_in_dim(vector_block[:4], core * share, share, 1)
    pieces = []
    offset = 0
    for member in (hidden, hidden, width, 3 * width):
        half = member // CORES
        part = block[:, :, offset : offset + half]
        pieces.append(jnp.concatenate([part[0], part[1]], axis=1))
        offset += half
    mixed, grads = (reordered(member, 1, groups, back=True) for member in (mixed, grads))
    same = [[g * GROUP + j for g in range(groups)] for j in range(GROUP)]

    def summed(member):
        return lax.psum_scatter(member, "dp", scatter_dimension=0, axis_index_groups=same, tiled=True)

    pieces = [summed(member) for member in pieces]
    vector_block = summed(vector_block.T).T
    down, up, out, qkv = pieces
    return (
        mixed[None], grads[None], qkv[None], out.T[None], up[None], down.T[None],
        vector_block[None, 0:2], vector_block[None, 2:4],
    )


def solution(mesh):
    placed = (P("dp", None),) * 2 + (P("section", None, None),) * 6
    return jax.shard_map(
        on_device,
        mesh=mesh,
        in_specs=placed,
        out_specs=(
            P("section", "dp", None),
            P("section", "dp", None),
            P("section", "dp", None),
            P("section", None, "dp"),
            P("section", "dp", None),
            P("section", None, "dp"),
            P("section", None, "dp"),
            P("section", None, "dp"),
        ),
        check_vma=False,
    )
```

```python
import math

import jax
import jax.numpy as jnp
from jax import lax
from jax.experimental import pallas as pl
from jax.experimental.pallas import tpu as pltpu
from jax.sharding import PartitionSpec as P

HEADS = 8
HEAD_DIM = 128
ITEM_LEN = 15
MICRO = 2
EPSILON = 1e-05

LINE, PAIR, CORES = 4, 2, 2
GROUP = LINE * PAIR * CORES
PANEL = 256
STRIPS = 2
AHEAD = 8
LAG = 2
END_LAG = 5
BEFORE_HEADS, BEFORE_LAST = 4, 6
RING = 8
END_RING = 12
VECTORS = 8, 20, 28
SPARE, ACROSS, BACK = 12, 12, 20
FIRST = 4
LEAVING = 8
MESH = pl.DeviceIdType.MESH
BF16, F32 = jnp.bfloat16, jnp.float32
DOWN, UP, OUT, QKV = range(4)


def dot(left, right):
    return jnp.dot(left, right, preferred_element_type=F32)


def dot_nt(left, right):
    return lax.dot_general(left, right, (((1,), (1,)), ((), ())), preferred_element_type=F32)


def dot_tn(left, right):
    return lax.dot_general(left, right, (((0,), (0,)), ((), ())), preferred_element_type=F32)


def normalized(values):
    centered = values - jnp.mean(values, axis=-1, keepdims=True)
    scale = lax.rsqrt(jnp.mean(centered * centered, axis=-1, keepdims=True) + EPSILON)
    return centered * scale, scale


def normalize_back(grad, unit, scale, gain):
    scaled = grad * gain
    along = jnp.mean(scaled * unit, axis=-1, keepdims=True)
    return scale * (scaled - jnp.mean(scaled, axis=-1, keepdims=True) - unit * along)


def gelu_and_slope(u):
    square = u * u
    inner = jnp.tanh(u * (0.7978845608 + 0.7978845608 * 0.044715 * square))
    part = 0.5 + 0.5 * inner
    steep = 0.5 * 0.7978845608 + 1.5 * 0.7978845608 * 0.044715 * square
    return u * part, part + u * (1.0 - inner * inner) * steep


def layer_kernel(
    tokens_in, cotangent_in, gains_in, biases_in, w_qkv_in, w_out_in, w_up_in, w_down_in,
    mixed_out, grads_out, out, vector_out, buf, sem,
):
    h, e, e_other, result = buf["h"], buf["e"], buf["e_other"], buf["result"]
    w_qkv, w_out, w_up, w_down = buf["w_qkv"], buf["w_out"], buf["w_up"], buf["w_down"]
    left, e_half, right, twin_right = buf["left"], buf["e_half"], buf["right"], buf["twin_right"]
    act_beside, proj, middle, slopes = buf["act_beside"], buf["proj"], buf["middle"], buf["slopes"]
    probs, bias, dctx, vector = buf["probs"], buf["bias"], buf["dctx"], buf["vector"]
    parts, acc, fin = buf["parts"], buf["acc"], buf["fin"]
    pair_beside, pair_in, pair_across = buf["pair_beside"], buf["pair_in"], buf["pair_across"]
    vectors, vectors_line, vector_total = buf["vectors"], buf["vectors_line"], buf["vector_total"]
    gains, biases = buf["gains"], buf["biases"]
    spare_parts, spare_in, spare_across = buf["spare_parts"], buf["spare_in"], buf["spare_across"]

    all_rows, width = h.shape
    rows = all_rows // MICRO
    front = rows // 32 * 16
    hidden = w_up.shape[1]
    chunk, half_chunk = acc.shape[2], acc.shape[2] // 2
    widths = (hidden, hidden, width, 3 * width)
    columns_at = (0, hidden, 2 * hidden, 2 * hidden + width)
    starts = [0]
    for member in widths:
        starts.append(starts[-1] + member // CORES // PANEL)
    strip = PANEL // STRIPS
    strips, direct = starts[-1] * STRIPS, starts[1] * STRIPS
    halves = [member // CORES for member in widths]
    twin_at = [start * PANEL for start in starts]

    section = lax.axis_index("section")
    place = lax.axis_index("dp")
    first = (place // GROUP) * GROUP
    mine = place - first
    z, y, core = mine // (PAIR * CORES), (mine // CORES) % PAIR, mine % CORES
    other_y, other_core = 1 - y, 1 - core
    far_side = z // 2
    is_end = (z == 0) | (z == LINE - 1)
    is_inner = jnp.logical_not(is_end)
    own = jnp.where(is_end, 0, 1)

    def numbered(zz):
        return zz + far_side * (LINE - 1 - 2 * zz)

    def device(zz, yy, cc):
        return (section, first + (zz * PAIR + yy) * CORES + cc)

    beside, twin = device(z, other_y, core), device(z, y, other_core)
    partner = (1 - section, place)
    leads = section == 0

    def send(source, target, key, index, to, landing=None):
        return pltpu.make_async_remote_copy(
            src_ref=source, dst_ref=target, send_sem=sem[key + "_send"].at[index],
            recv_sem=sem[key + "_recv"].at[index if landing is None else landing], device_id=to, device_id_type=MESH,
        )

    def fetch(source, target, index):
        return pltpu.make_async_copy(source, target, sem["fetch"].at[index])

    def rows_of(m):
        return pl.ds(pl.multiple_of(m * rows, rows), rows)

    loads = [fetch(w_out_in, w_out, 0), fetch(w_up_in, w_up, 1), fetch(w_down_in, w_down, 2)]
    loads_qkv = [
        fetch(w_qkv_in.at[:, pl.ds(part * width, width)], w_qkv.at[:, pl.ds(part * width, width)], 3 + part)
        for part in range(3)
    ]
    load_rows = [fetch(tokens_in.at[at], h.at[at], 6 + i) for i, at in enumerate((pl.ds(0, front), pl.ds(front, all_rows - front)))]
    load_cotangent = fetch(cotangent_in, e, 6)
    load_norms = [fetch(gains_in, gains, 8), fetch(biases_in, biases, 9)]

    @pl.when(leads)
    def _():
        load_rows[0].start()

    @pl.when(jnp.logical_not(leads))
    def _():
        load_cotangent.start()

    for load in load_norms + loads_qkv[:2]:
        load.start()
    barrier = pltpu.get_barrier_semaphore()
    lined = [device((z + step) % LINE, y, core) for step in range(1, LINE)]
    inner, end, across, far_end = (device(numbered(zz), y, core) for zz in (1, 0, 2, 3))
    peers = [partner, twin, beside] + lined
    for peer in peers:
        pl.semaphore_signal(barrier, inc=1, device_id=peer, device_id_type=MESH)
    loads_qkv[2].start()

    @pl.when(leads)
    def _():
        load_rows[1].start()

    @pl.when(jnp.logical_not(leads))
    def _():
        for load in loads:
            load.start()

    row_ids = lax.broadcasted_iota(jnp.int32, (rows, 1), 0)
    col_ids = lax.broadcasted_iota(jnp.int32, (1, rows), 1)
    seen = (row_ids // ITEM_LEN == col_ids // ITEM_LEN) & (col_ids <= row_ids)
    bias[...] = jnp.where(seen, 0.0, -1e30)
    vector[...] = jnp.zeros_like(vector)
    proj[front:rows, width:] = jnp.zeros((rows - front, 2 * width), BF16)
    scale = 1.0 / math.sqrt(HEAD_DIM)


    spans = ((0, front), (front, rows), (rows, 2 * rows))

    def x_forward(i):
        at = pl.ds(spans[i][0], spans[i][1] - spans[i][0])
        return send(result.at[at], h.at[at], "x_forward", i, partner)

    late = rows // 5
    returns = ((0, rows), (rows, 2 * rows - front), (2 * rows - front, 2 * rows - late), (2 * rows - late, 2 * rows))

    def returned(i):
        return pl.ds(returns[i][0], returns[i][1] - returns[i][0])

    def x_back(i):
        return send(h.at[returned(i)], e.at[returned(i)], "x_back", i, partner)

    def mixed_store(m):
        return pltpu.make_async_copy(result.at[rows_of(m)], mixed_out.at[rows_of(m)], sem["store"].at[0, m])

    def grads_store(m):
        return pltpu.make_async_copy(h.at[rows_of(m)], grads_out.at[rows_of(m)], sem["store"].at[1, m])

    def twin_left(which, m):
        return send(left.at[which - 1, 0, rows_of(m)], left.at[which - 1, 1, rows_of(m)],
                    "twin_left", (which - 1, m), twin)

    def twin_right_of(which, m):
        start = pl.multiple_of(columns_at[which] + other_core * halves[which], 128)
        return send(right.at[rows_of(m), pl.ds(start, halves[which])],
                    twin_right.at[rows_of(m), pl.ds(twin_at[which], halves[which])],
                    "twin_right", (which, m), twin)

    def a2_beside(m):
        return send(left.at[UP - 1, 0, rows_of(m)], act_beside.at[0, rows_of(m)], "act_beside", (0, m), beside)

    def a2_onward(m):
        return send(act_beside.at[0, rows_of(m)], act_beside.at[1, rows_of(m)], "act_beside", (1, m), twin)

    def e_twin(i):
        return send(e_half.at[0, returned(i)], e_half.at[1, returned(i)], "e_half", (0, i), twin)

    def e_beside(i):
        return send(e_other.at[returned(i)], e_half.at[2, returned(i)], "e_half", (1, i), beside)

    def e_onward(i):
        return send(e_half.at[2, returned(i)], e_half.at[3, returned(i)], "e_half", (2, i), twin)


    def attend(i, load=False, first_section=False):
        low, high = spans[i]
        at, m = slice(low, high), low // rows
        whole = slice(m * rows, (m + 1) * rows)
        unit, unused = normalized(h[at].astype(F32))
        left[QKV - 1, 0, at] = (unit * gains[0:1] + biases[0:1]).astype(BF16)
        def project(part):
            cols = slice(part * width, (part + 1) * width)
            if load:
                loads_qkv[part].wait()
            if load and first_section:
                loads[part].start()
            proj[at, cols] = dot(left[QKV - 1, 0, at], w_qkv[:, cols]).astype(BF16)

        project(0)
        project(1)

        def heads_of(part, head):
            start = part * width + head * HEAD_DIM
            return proj[whole, start : start + HEAD_DIM]

        for head in range(HEADS):
            scores = dot_nt(heads_of(0, head), heads_of(1, head)) * scale + bias[...]
            weight = jnp.exp(scores - jnp.max(scores, axis=-1, keepdims=True))
            probs[m * HEADS + head] = (weight / jnp.sum(weight, axis=-1, keepdims=True)).astype(BF16)
        project(2)
        for head in range(HEADS):
            cols = slice(columns_at[OUT] + head * HEAD_DIM, columns_at[OUT] + (head + 1) * HEAD_DIM)
            right[whole, cols] = dot(probs[m * HEADS + head], heads_of(2, head)).astype(BF16)

    def forward(i, load=False):
        at = slice(*spans[i])
        if load:
            loads[0].wait()
        attended = dot(right[at, columns_at[OUT] : columns_at[OUT] + width], w_out[...])
        middle[at] = h[at].astype(F32) + attended
        unit, unused = normalized(middle[at])
        left[UP - 1, 0, at] = (unit * gains[1:2] + biases[1:2]).astype(BF16)
        if i > 0:
            a2_beside(i - 1).start()
        if load:
            loads[1].wait()
        for part in range(2):
            cols = slice(part * hidden // 2, (part + 1) * hidden // 2)
            upward = dot(left[UP - 1, 0, at], w_up[:, cols])
            active, slope = gelu_and_slope(upward)
            slopes[at, cols] = slope.astype(BF16)
            right[at, cols] = active.astype(BF16)
        if load:
            loads[2].wait()
        result[at] = (middle[at] + dot(right[at, :hidden], w_down[...])).astype(BF16)

        @pl.when(leads)
        def _():
            x_forward(i).start()

    def share(m):
        twin_left(UP, m).start()
        twin_right_of(DOWN, m).start()
        twin_right_of(OUT, m).start()
        twin_left(QKV, m).start()
        mixed_store(m).start()

    def gather_act():
        cols = pl.ds(pl.multiple_of(core * halves[DOWN], 128), halves[DOWN])

        @pl.loop(0, MICRO)
        def _(m):
            a2_beside(m).wait_recv()
            a2_onward(m).start()
            a2_onward(m).wait()

            @pl.loop(0, 2)
            def _(source):
                active, unused = gelu_and_slope(dot(act_beside[source, rows_of(m)], w_up[:, cols]))
                act_beside[source, rows_of(m)] = active.astype(BF16)

    def spread(i):
        at = returned(i)
        for zz in range(LINE):
            cols = pl.ds(zz * chunk, chunk)
            e_half[0, at, cols] = e[at, pl.ds(pl.multiple_of((zz * PAIR + y) * chunk, chunk), chunk)]
            e_other[at, cols] = e[at, pl.ds(pl.multiple_of((zz * PAIR + other_y) * chunk, chunk), chunk)]
        e_beside(i).start()
        e_twin(i).start()

    def backward(m, hooks):
        at = rows_of(m)

        for part in (other_core, core):
            start = pl.multiple_of(part * halves[UP], halves[UP])
            cols = pl.ds(start, halves[UP])
            passed = dot_nt(e[at], w_down[cols])
            right[at, pl.ds(columns_at[UP] + start, halves[UP])] = (passed * slopes[at, cols].astype(F32)).astype(BF16)
            if part is other_core:
                twin_right_of(UP, m).start()

        hooks[0](m)
        grad = dot_nt(right[at, columns_at[UP] : columns_at[UP] + hidden], w_up[...])
        unit, size = normalized(middle[at])
        vector[1:2] += jnp.sum(grad * unit, axis=0, keepdims=True)
        vector[3:4] += jnp.sum(grad, axis=0, keepdims=True)
        middle[at] = e[at].astype(F32) + normalize_back(grad, unit, size, gains[1:2])
        left[OUT - 1, 0, at] = middle[at].astype(BF16)
        twin_left(OUT, m).start()
        dctx[...] = dot_nt(left[OUT - 1, 0, at], w_out[...]).astype(BF16)
        hooks[1](m)

        def heads_of(part, head):
            start = part * width + head * HEAD_DIM
            return proj[at, start : start + HEAD_DIM]

        def keep(part, head, value):
            start = columns_at[QKV] + part * width + head * HEAD_DIM
            right[at, start : start + HEAD_DIM] = value.astype(BF16)

        def grad_ctx(head):
            return dctx[:, head * HEAD_DIM : (head + 1) * HEAD_DIM]

        grad_scores = []
        for head in range(HEADS):
            weight = probs[m * HEADS + head].astype(F32)
            grad_weight = dot_nt(grad_ctx(head), heads_of(2, head))
            total = jnp.sum(weight * grad_weight, axis=-1, keepdims=True)
            grad_scores.append((weight * (grad_weight - total)).astype(BF16))
        for head in range(HEADS):
            keep(2, head, dot_tn(probs[m * HEADS + head], grad_ctx(head)))
        for head in range(HEADS):
            keep(0, head, dot(grad_scores[head], heads_of(1, head)) * scale)
            keep(1, head, dot_tn(grad_scores[head], heads_of(0, head)) * scale)

        twin_right_of(QKV, m).start()
        hooks[2](m)
        grad = dot_nt(right[at, columns_at[QKV] : columns_at[QKV] + 3 * width], w_qkv[...])
        unit, size = normalized(h[at].astype(F32))
        vector[0:1] += jnp.sum(grad * unit, axis=0, keepdims=True)
        vector[2:3] += jnp.sum(grad, axis=0, keepdims=True)
        h[at] = (middle[at] + normalize_back(grad, unit, size, gains[0:1])).astype(BF16)
        grads_store(m).start()

        @pl.when(jnp.logical_not(leads))
        def _():
            @pl.when(m == 0)
            def _():
                x_back(0).start()

            @pl.when(m == 1)
            def _():
                x_back(1).start()


    def beside_of(p):
        i = p - direct
        here, there = i % AHEAD, i % (2 * AHEAD)
        return send(parts.at[here, :, other_y], pair_beside.at[there], "pair_beside", here, beside, there)

    def spare_out(part):
        return send(spare_parts.at[part, :, other_y], spare_in.at[part], "spare", part, partner)

    def spare_beside(part, d):
        return send(spare_in.at[part, d], spare_across.at[part, d], "spare_across", (part, d), beside)

    def spare_back(part):
        return send(spare_across.at[part], spare_in.at[part], "spare", part, partner)

    def each_spare(act):
        for part in range(STRIPS):
            for d in range(LINE):
                act(spare_beside(part, d))

    def in_of(p):
        return send(acc.at[p % RING, pl.ds(1, 3)], pair_in.at[pl.ds(3 * (p % RING), 3)], "pair_in", p % RING, inner)

    def across_of(p):
        return send(acc.at[p % RING, 2], pair_across.at[p % RING], "pair_across", p % RING, across)

    def far_of(p):
        there = p % END_RING
        return send(acc.at[p % RING, 3], pair_in.at[2 * there + 1], "pair_far", p % RING, far_end, there)

    def out_of(p):
        there = p % END_RING
        return send(acc.at[p % RING, 0], pair_in.at[2 * there], "pair_out", p % RING, end, there)

    def chunk_at(zz):
        return pl.ds(pl.multiple_of((zz * PAIR + y) * chunk, chunk), chunk)

    vector_store = pltpu.make_async_copy(vector_total, vector_out, sem["vector_store"].at[0])

    def vector_twin():
        return send(vector, vectors.at[0], "vector", 0, twin)

    def vector_beside():
        return send(vector, vectors.at[1], "vector", 1, beside)

    def vector_line(step):
        return send(vector.at[:, chunk_at((z + step) % LINE)], vectors_line.at[step - 1], "vector", 1 + step, lined[step - 1])

    def strip_columns(p):
        return pl.ds(pl.multiple_of(p * strip, strip), strip)

    def fin_of(g):
        cols = pl.ds(pl.multiple_of(g * LEAVING * strip, LEAVING * strip), LEAVING * strip)
        return send(fin.at[1, :, cols], out.at[core, :, cols], "fin", g, twin)

    def kept_of(g):
        cols = pl.ds(pl.multiple_of(g * LEAVING * strip, LEAVING * strip), LEAVING * strip)
        return pltpu.make_async_copy(fin.at[0, :, cols], out.at[core, :, cols], sem["kept"].at[g])

    def add(target, *refs):
        total = target[...].astype(F32)
        for ref in refs:
            total = total + ref[...].astype(F32)
        target[...] = total.astype(BF16)

    def own_columns(p):
        place_of = p * PANEL + core * halves[0]
        for i in (1, 2, 3):
            shift = (columns_at[i] - twin_at[i] + core * halves[i]) - (
                columns_at[i - 1] - twin_at[i - 1] + core * halves[i - 1])
            place_of = place_of + jnp.where(p >= starts[i], shift, 0)
        return pl.ds(pl.multiple_of(place_of, 128), PANEL)

    def twin_columns(p):
        return pl.ds(pl.multiple_of(p * PANEL, PANEL), PANEL)

    def wait_for(which):
        for m in range(MICRO):
            twin_left(which, m).wait_recv()
            twin_right_of(which, m).wait_recv()

    def form(p, spare=False):
        which = QKV - 1 if spare else 0
        for i in () if spare else (OUT, QKV):
            which = which + (p >= starts[i]).astype(jnp.int32)
            due = p == starts[i] if i == OUT else (p == starts[i]) & jnp.logical_not(leads)

            @pl.when(due)
            def _(i=i):
                wait_for(i)

        total = dot_tn(left[which, 0], right[:, own_columns(p)]) + dot_tn(left[which, 1], twin_right[:, twin_columns(p)])
        total = total.astype(BF16).reshape(LINE, PAIR, chunk, PANEL)
        for part in range(STRIPS):
            for zz in range(LINE):
                here = total[zz, :, :, part * strip : (part + 1) * strip]
                if spare:
                    spare_parts[part, numbered(zz)] = here
                else:
                    parts[(p * STRIPS + part - direct) % AHEAD, numbered(zz)] = here

    def form_up(low, high):
        @pl.loop(starts[UP] + low, starts[UP] + high)
        def _(p):
            form(p)

    def start_strips(low, high):
        @pl.loop(direct + low, direct + high)
        def _(p):
            beside_of(p).start()

    def gather_e(i):
        e_beside(i).wait_recv()
        e_onward(i).start()

    def form_down():
        for m in range(MICRO):
            twin_right_of(DOWN, m).wait_recv()
        for i in range(len(returns)):
            e_twin(i).wait_recv()
            e_onward(i).wait_recv()

        @pl.loop(0, starts[UP])
        def _(p):
            total = dot_tn(e_half[0], right[:, own_columns(p)]) + dot_tn(e_half[1], twin_right[:, twin_columns(p)])
            for source in range(2):
                total = total + dot_tn(e_half[2 + source], act_beside[source, :, twin_columns(p)])
            total = total.astype(BF16).reshape(LINE, chunk, PANEL)
            for part in range(STRIPS):
                for zz in range(LINE):
                    acc[(p * STRIPS + part) % RING, numbered(zz)] = total[zz, :, part * strip : (part + 1) * strip]

            @pl.when(is_end & (p < FIRST // STRIPS))
            def _():
                for part in range(STRIPS):
                    in_of(p * STRIPS + part).start()

    def enter(t):
        @pl.when((t < direct - FIRST) & is_end)
        def _():
            in_of(t + FIRST).start()

        @pl.when((t < direct) & is_inner)
        def _():
            out_of(t).start()

    def across_y(t):
        def enter_line(mine_of, theirs_of):
            for d in range(LINE):
                acc[t % RING, d] = (mine_of(d).astype(F32) + theirs_of(d).astype(F32)).astype(BF16)

            @pl.when(is_end)
            def _():
                in_of(t).start()

            @pl.when(is_inner)
            def _():
                out_of(t).start()

        spared = leads & (t // STRIPS == SPARE)

        @pl.when((t >= direct) & (t < strips) & jnp.logical_not(spared))
        def _():
            i = t - direct
            beside_of(t).wait()
            enter_line(lambda d: parts[i % AHEAD, d, y], lambda d: pair_beside[i % (2 * AHEAD), d])

            panel = (t + AHEAD) // STRIPS

            @pl.when((t + AHEAD < strips) & (t % STRIPS == STRIPS - 1) & jnp.logical_not(leads & (panel == SPARE)))
            def _():
                form(panel)
                for part in range(STRIPS):
                    beside_of(t + AHEAD - STRIPS + 1 + part).start()

        @pl.when(spared)
        def _():
            part = t % STRIPS
            spare_back(part).wait_recv()
            enter_line(lambda d: spare_parts[part, d, y], lambda d: spare_in[part, d])

        @pl.when((t == ACROSS) & jnp.logical_not(leads))
        def _():
            for part in range(STRIPS):
                spare_out(part).wait_recv()
            each_spare(lambda message: message.start())

        @pl.when((t == BACK) & jnp.logical_not(leads))
        def _():
            each_spare(lambda message: message.wait_recv())
            for part in range(STRIPS):
                spare_back(part).start()

    def relay(t):
        p = t - LAG

        @pl.when((p >= 0) & (p < strips) & is_inner)
        def _():
            in_of(p).wait_recv()
            add(acc.at[p % RING, pl.ds(2, 2)], pair_in.at[pl.ds(3 * (p % RING) + 1, 2)])
            far_of(p).start()
            across_of(p).start()
            add(acc.at[p % RING, 1], pair_in.at[3 * (p % RING)])

        r = t - END_LAG

        @pl.when(r >= 0)
        def _():
            @pl.when(is_end)
            def _():
                out_of(r).wait_recv()
                far_of(r).wait_recv()
                in_of(r).wait_send()
                finish(r, pair_in.at[2 * (r % END_RING)], pair_in.at[2 * (r % END_RING) + 1])

            @pl.when(is_inner)
            def _():
                across_of(r).wait()
                far_of(r).wait_send()
                out_of(r).wait_send()
                finish(r, pair_across.at[r % RING])

    def finish(r, *refs):
        for slot, which in enumerate((core, other_core)):
            here = pl.ds(pl.multiple_of(which * half_chunk, half_chunk), half_chunk)
            total = acc[r % RING, own, here].astype(F32)
            for ref in refs:
                total = total + ref[here].astype(F32)
            fin[slot, :, strip_columns(r)] = total

        @pl.when(r % LEAVING == LEAVING - 1)
        def _():
            fin_of(r // LEAVING).start()
            kept_of(r // LEAVING).start()

    def vectors_step(t):
        @pl.when(t == VECTORS[0])
        def _():
            vector_twin().wait()
            vector[...] += vectors[0]
            vector_beside().start()

        @pl.when(t == VECTORS[1])
        def _():
            vector_beside().wait()
            vector[...] += vectors[1]
            for step in range(1, LINE):
                vector_line(step).start()

        @pl.when(t == VECTORS[2])
        def _():
            total = vector[:, chunk_at(z)]
            for step in range(1, LINE):
                vector_line(step).wait()
                total = total + vectors_line[step - 1]
            vector_total[...] = total
            vector_store.start()

    def proceed(low, high, parts_of_step):
        @pl.loop(low, high)
        def _(t):
            for part in parts_of_step:
                part(t)


    def after_du(m):
        @pl.when((m == MICRO - 1) & leads)
        def _():
            wait_for(UP)
            form_up(0, 1)
            start_strips(0, STRIPS)
            for i in range(len(returns)):
                gather_e(i)
            form_up(1, 2)
            start_strips(STRIPS, 2 * STRIPS)
            form_down()

    def after_middle(m):
        @pl.when((m == MICRO - 1) & leads)
        def _():
            form_up(2, AHEAD // STRIPS)
            start_strips(2 * STRIPS, AHEAD)
            proceed(0, BEFORE_HEADS, (enter, relay))

    def after_heads(m):
        @pl.when((m == MICRO - 1) & leads)
        def _():
            proceed(BEFORE_HEADS, BEFORE_LAST, (enter, relay))

    @pl.when(leads)
    def _():
        for load in load_rows[:1] + load_norms:
            load.wait()
        attend(0, load=True, first_section=True)

    pl.semaphore_wait(barrier, len(peers))

    @pl.when(jnp.logical_not(leads))
    def _():
        for load in [load_cotangent] + load_norms:
            load.wait()
        for i in range(len(returns)):
            spread(i)
        x_forward(0).wait_recv()
        attend(0, load=True)

    forward(0, load=True)

    @pl.when(leads)
    def _():
        load_rows[1].wait()

    @pl.when(jnp.logical_not(leads))
    def _():
        x_forward(1).wait_recv()

    attend(1)
    forward(1)

    @pl.when(leads)
    def _():
        share(0)

    @pl.loop(0, MICRO + 1)
    def _(step):
        @pl.when(step == section)
        def _():
            @pl.when(jnp.logical_not(leads))
            def _():
                x_forward(2).wait_recv()

            attend(2)
            forward(2)

            @pl.when(leads)
            def _():
                share(1)
                gather_act()

        @pl.when(step != section)
        def _():
            m = step // 2

            @pl.when(leads & (m == 0))
            def _():
                x_back(0).wait_recv()
                spread(0)

            @pl.when(leads & (m == 1))
            def _():
                for i in range(1, len(returns)):
                    x_back(i).wait_recv()
                    spread(i)

            backward(m, (after_du, after_middle, after_heads))

    vector_twin().start()

    @pl.when(leads)
    def _():
        wait_for(QKV)
        form(SPARE, spare=True)
        for part in range(STRIPS):
            spare_out(part).start()

    @pl.when(jnp.logical_not(leads))
    def _():
        for m in range(MICRO):
            share(m)
        for i in range(len(returns)):
            gather_e(i)
        x_back(2).start()
        wait_for(UP)
        form_up(0, 2)
        start_strips(0, 2 * STRIPS)
        x_back(1).wait_send()
        x_back(3).start()
        gather_act()
        form_down()
        form_up(2, AHEAD // STRIPS)
        start_strips(2 * STRIPS, AHEAD)

        proceed(0, BEFORE_LAST, (enter, relay))

    proceed(BEFORE_LAST, strips + END_LAG, (enter, relay, across_y, vectors_step))

    vector_store.wait()
    for part in range(STRIPS):
        spare_out(part).wait_send()

    @pl.when(jnp.logical_not(leads))
    def _():
        each_spare(lambda message: message.wait_send())

    for m in range(MICRO):
        for which in (UP, OUT, QKV):
            twin_left(which, m).wait_send()
        for which in range(4):
            twin_right_of(which, m).wait_send()
        a2_beside(m).wait_send()
        grads_store(m).wait()
        mixed_store(m).wait()

    for i in range(len(returns)):
        e_twin(i).wait_send()
        e_beside(i).wait_send()
        e_onward(i).wait_send()

    @pl.when(jnp.logical_not(leads))
    def _():
        for i in (0, 2, 3):
            x_back(i).wait_send()

    @pl.when(leads)
    def _():
        for i in range(len(spans)):
            x_forward(i).wait_send()

    @pl.loop(0, strips // LEAVING)
    def _(g):
        fin_of(g).wait()
        kept_of(g).wait()


def layers(tokens, cotangent, gains, biases, w_qkv, w_out, w_up, w_down):
    all_rows, width = tokens.shape
    hidden = w_up.shape[1]
    rows = all_rows // MICRO
    columns = 2 * hidden + 4 * width
    strip = PANEL // STRIPS
    strips = columns // CORES // strip
    chunk = width // (LINE * PAIR)
    dma = pltpu.SemaphoreType.DMA
    shapes = {
        "h": ((all_rows, width), BF16),
        "e": ((all_rows, width), BF16),
        "e_other": ((all_rows, width // 2), BF16),
        "result": ((all_rows, width), BF16),
        "w_qkv": (w_qkv.shape, BF16),
        "w_out": (w_out.shape, BF16),
        "w_up": (w_up.shape, BF16),
        "w_down": (w_down.shape, BF16),
        "left": ((3, CORES, all_rows, width), BF16),
        "e_half": ((4, all_rows, width // 2), BF16),
        "right": ((all_rows, columns), BF16),
        "twin_right": ((all_rows, columns // CORES), BF16),
        "act_beside": ((2, all_rows, hidden // CORES), BF16),
        "proj": ((all_rows, 3 * width), BF16),
        "middle": ((all_rows, width), F32),
        "slopes": ((all_rows, hidden), BF16),
        "probs": ((MICRO * HEADS, rows, rows), BF16),
        "bias": ((rows, rows), F32),
        "dctx": ((rows, width), BF16),
        "vector": ((8, width), F32),
        "parts": ((AHEAD, LINE, PAIR, chunk, strip), BF16),
        "acc": ((RING, LINE, chunk, strip), BF16),
        "fin": ((2, chunk // 2, columns // CORES), F32),
        "pair_beside": ((2 * AHEAD, LINE, chunk, strip), BF16),
        "pair_in": ((max(3 * RING, 2 * END_RING), chunk, strip), BF16),
        "pair_across": ((RING, chunk, strip), BF16),
        "spare_parts": ((STRIPS, LINE, PAIR, chunk, strip), BF16),
        "spare_in": ((STRIPS, LINE, chunk, strip), BF16),
        "spare_across": ((STRIPS, LINE, chunk, strip), BF16),
        "vectors": ((2, 8, width), F32),
        "vectors_line": ((LINE - 1, 8, chunk), F32),
        "vector_total": ((8, chunk), F32),
        "gains": (gains.shape, F32),
        "biases": (biases.shape, F32),
    }
    exchanges = {
        "x_forward": (3,), "x_back": (4,), "twin_left": (3, MICRO), "twin_right": (4, MICRO),
        "act_beside": (2, MICRO), "e_half": (3, 4), "pair_in": (RING,), "pair_across": (RING,),
        "fin": (strips // LEAVING,), "spare": (STRIPS,), "spare_across": (STRIPS, LINE), "vector": (LINE + 1,),
    }
    semaphores = {"fetch": dma((10,)), "vector_store": dma((1,)), "store": dma((2, MICRO)), "kept": dma((strips // LEAVING,))}
    for key, count in exchanges.items():
        semaphores[key + "_send"] = dma(count)
        semaphores[key + "_recv"] = dma(count)
    for key in ("pair_out", "pair_far"):
        semaphores[key + "_send"], semaphores[key + "_recv"] = dma((RING,)), dma((END_RING,))
    semaphores["pair_beside_send"], semaphores["pair_beside_recv"] = dma((AHEAD,)), dma((2 * AHEAD,))
    anywhere = pl.BlockSpec(memory_space=pl.ANY)
    return pl.pallas_call(
        layer_kernel,
        out_shape=(
            jax.ShapeDtypeStruct((all_rows, width), BF16),
            jax.ShapeDtypeStruct((all_rows, width), BF16),
            jax.ShapeDtypeStruct((CORES, chunk // 2, columns // CORES), F32),
            jax.ShapeDtypeStruct((8, chunk), F32),
        ),
        in_specs=[anywhere] * 8,
        out_specs=(anywhere,) * 4,
        scratch_shapes=[{key: pltpu.VMEM(*shape) for key, shape in shapes.items()}, semaphores],
        compiler_params=pltpu.CompilerParams(
            collective_id=1, has_side_effects=True, vmem_limit_bytes=64 * 2**20
        ),
        name="relay_layers",
    )(tokens, cotangent, gains, biases, w_qkv, w_out, w_up, w_down)


def results_kernel(
    mixed_in, grads_in, block_in, vectors_in, mixed, grads, down, up, out, qkv, gains, biases,
    rows, block, vectors, shares, sem,
):
    started = []

    def copy(source, target):
        started.append(pltpu.make_async_copy(source, target, sem.at[len(started)]))
        started[-1].start()
        return started[-1]

    fetches = [copy(block_in.at[core], block.at[core]) for core in range(CORES)]
    fetches.append(copy(vectors_in, vectors))
    fetches += [copy(ref, rows.at[i]) for i, ref in enumerate((mixed_in, grads_in))]
    stores = []
    for core in range(CORES):
        fetches[core].wait()
        offset = 0
        for ref in (down, up, out, qkv):
            half = ref.shape[1] // CORES
            stores.append(copy(block.at[core, :, pl.ds(offset, half)], ref.at[:, pl.ds(core * half, half)]))
            offset += half
    fetches[CORES].wait()
    share = gains.shape[1]
    mine = lax.axis_index("dp") % CORES
    for core in range(CORES):
        @pl.when(mine == core)
        def _(core=core):
            here = slice(core * share, (core + 1) * share)
            shares[0] = vectors[0:2, here]
            shares[1] = vectors[2:4, here]

    stores += [copy(shares.at[i], ref) for i, ref in enumerate((gains, biases))]
    for i, ref in enumerate((mixed, grads)):
        fetches[CORES + 1 + i].wait()
        stores.append(copy(rows.at[i], ref))
    for store in stores:
        store.wait()


def results(mixed, grads, block, vectors, hidden):
    width, share = mixed.shape[1], block.shape[1]
    anywhere = pl.BlockSpec(memory_space=pl.ANY)
    shapes = ((share, hidden), (share, hidden), (share, width), (share, 3 * width), (2, share), (2, share))
    mixed, grads, down, up, out, qkv, gains, biases = pl.pallas_call(
        results_kernel,
        out_shape=(jax.ShapeDtypeStruct(mixed.shape, BF16), jax.ShapeDtypeStruct(grads.shape, BF16))
        + tuple(jax.ShapeDtypeStruct(shape, F32) for shape in shapes),
        in_specs=[anywhere] * 4,
        out_specs=(anywhere,) * 8,
        scratch_shapes=[
            pltpu.VMEM((2,) + mixed.shape, BF16), pltpu.VMEM(block.shape, F32), pltpu.VMEM(vectors.shape, F32),
            pltpu.VMEM((2, 2, share), F32), pltpu.SemaphoreType.DMA((CORES + 3 + 4 * CORES + 4,)),
        ],
        compiler_params=pltpu.CompilerParams(vmem_limit_bytes=64 * 2**20),
        name="place_results",
    )(mixed, grads, block, vectors)
    return mixed, grads, qkv, out.T, up, down.T, gains, biases


def reordered(member, axis, groups, back=False):
    shape = member.shape
    row = shape[axis] // (groups * GROUP)
    split = (GROUP, groups, row) if back else (groups, GROUP, row)
    apart = member.reshape(shape[:axis] + split + shape[axis + 1 :])
    return jnp.swapaxes(apart, axis, axis + 1).reshape(shape)


def on_device(tokens, cotangent, norm_gains, norm_biases, w_qkv, w_out, w_up, w_down):
    hidden, width = w_up.shape[2], tokens.shape[1]
    operands = (tokens, cotangent, norm_gains[0], norm_biases[0], w_qkv[0], w_out[0], w_up[0], w_down[0])
    groups = lax.axis_size("dp") // GROUP
    if groups > 1:
        axes = (1, 1, 1, 1, 0, 1, 0, 1)
        operands = tuple(reordered(member, axis, groups) for member, axis in zip(operands, axes))
    mixed, grads, block, vector_block = layers(*operands)
    if groups == 1:
        return tuple(member[None] for member in results(mixed, grads, block, vector_block, hidden))
    core = lax.axis_index("dp") % CORES
    share = block.shape[1]
    vector_block = lax.dynamic_slice_in_dim(vector_block[:4], core * share, share, 1)
    pieces = []
    offset = 0
    for member in (hidden, hidden, width, 3 * width):
        half = member // CORES
        part = block[:, :, offset : offset + half]
        pieces.append(jnp.concatenate([part[0], part[1]], axis=1))
        offset += half
    mixed, grads = (reordered(member, 1, groups, back=True) for member in (mixed, grads))
    same = [[g * GROUP + j for g in range(groups)] for j in range(GROUP)]

    def summed(member):
        return lax.psum_scatter(member, "dp", scatter_dimension=0, axis_index_groups=same, tiled=True)

    pieces = [summed(member) for member in pieces]
    vector_block = summed(vector_block.T).T
    down, up, out, qkv = pieces
    return (
        mixed[None], grads[None], qkv[None], out.T[None], up[None], down.T[None],
        vector_block[None, 0:2], vector_block[None, 2:4],
    )


def solution(mesh):
    placed = (P("dp", None),) * 2 + (P("section", None, None),) * 6
    return jax.shard_map(
        on_device,
        mesh=mesh,
        in_specs=placed,
        out_specs=(
            P("section", "dp", None),
            P("section", "dp", None),
            P("section", "dp", None),
            P("section", None, "dp"),
            P("section", "dp", None),
            P("section", None, "dp"),
            P("section", None, "dp"),
            P("section", None, "dp"),
        ),
        check_vma=False,
    )
```

```python
import math

import jax
import jax.numpy as jnp
from jax import lax
from jax.experimental import pallas as pl
from jax.experimental.pallas import tpu as pltpu
from jax.sharding import PartitionSpec as P

HEADS = 8
HEAD_DIM = 128
ITEM_LEN = 15
MICRO = 2
EPSILON = 1e-05

LINE, PAIR, CORES = 4, 2, 2
GROUP = LINE * PAIR * CORES
PANEL = 256
STRIPS = 2
AHEAD = 8
LAG = 2
END_LAG = 5
BEFORE_HEADS, BEFORE_LAST = 4, 6
RING = 8
END_RING = 12
VECTORS = 8, 20, 28
SPARE, ACROSS, BACK = 12, 12, 20
FIRST = 4
LEAVING = 8
MESH = pl.DeviceIdType.MESH
BF16, F32 = jnp.bfloat16, jnp.float32
DOWN, UP, OUT, QKV = range(4)


def dot(left, right):
    return jnp.dot(left, right, preferred_element_type=F32)


def dot_nt(left, right):
    return lax.dot_general(left, right, (((1,), (1,)), ((), ())), preferred_element_type=F32)


def dot_tn(left, right):
    return lax.dot_general(left, right, (((0,), (0,)), ((), ())), preferred_element_type=F32)


def normalized(values):
    centered = values - jnp.mean(values, axis=-1, keepdims=True)
    scale = lax.rsqrt(jnp.mean(centered * centered, axis=-1, keepdims=True) + EPSILON)
    return centered * scale, scale


def normalize_back(grad, unit, scale, gain):
    scaled = grad * gain
    along = jnp.mean(scaled * unit, axis=-1, keepdims=True)
    return scale * (scaled - jnp.mean(scaled, axis=-1, keepdims=True) - unit * along)


def gelu_and_slope(u):
    square = u * u
    inner = jnp.tanh(u * (0.7978845608 + 0.7978845608 * 0.044715 * square))
    part = 0.5 + 0.5 * inner
    steep = 0.5 * 0.7978845608 + 1.5 * 0.7978845608 * 0.044715 * square
    return u * part, part + u * (1.0 - inner * inner) * steep


def layer_kernel(
    tokens_in, cotangent_in, gains_in, biases_in, w_qkv_in, w_out_in, w_up_in, w_down_in,
    mixed_out, grads_out, out, vector_out, buf, sem,
):
    h, e, e_other, result = buf["h"], buf["e"], buf["e_other"], buf["result"]
    w_qkv, w_out, w_up, w_down = buf["w_qkv"], buf["w_out"], buf["w_up"], buf["w_down"]
    left, e_half, right, twin_right = buf["left"], buf["e_half"], buf["right"], buf["twin_right"]
    act_beside, proj, middle, slopes = buf["act_beside"], buf["proj"], buf["middle"], buf["slopes"]
    probs, bias, dctx, vector = buf["probs"], buf["bias"], buf["dctx"], buf["vector"]
    parts, acc, fin = buf["parts"], buf["acc"], buf["fin"]
    pair_beside, pair_in, pair_across = buf["pair_beside"], buf["pair_in"], buf["pair_across"]
    vectors, vectors_line, vector_total = buf["vectors"], buf["vectors_line"], buf["vector_total"]
    gains, biases = buf["gains"], buf["biases"]
    spare_parts, spare_in, spare_across = buf["spare_parts"], buf["spare_in"], buf["spare_across"]

    all_rows, width = h.shape
    rows = all_rows // MICRO
    front = rows // 32 * 16
    hidden = w_up.shape[1]
    chunk, half_chunk = acc.shape[2], acc.shape[2] // 2
    widths = (hidden, hidden, width, 3 * width)
    columns_at = (0, hidden, 2 * hidden, 2 * hidden + width)
    starts = [0]
    for member in widths:
        starts.append(starts[-1] + member // CORES // PANEL)
    strip = PANEL // STRIPS
    strips, direct = starts[-1] * STRIPS, starts[1] * STRIPS
    halves = [member // CORES for member in widths]
    twin_at = [start * PANEL for start in starts]

    section = lax.axis_index("section")
    place = lax.axis_index("dp")
    first = (place // GROUP) * GROUP
    mine = place - first
    z, y, core = mine // (PAIR * CORES), (mine // CORES) % PAIR, mine % CORES
    other_y, other_core = 1 - y, 1 - core
    far_side = z // 2
    is_end = (z == 0) | (z == LINE - 1)
    is_inner = jnp.logical_not(is_end)
    own = jnp.where(is_end, 0, 1)

    def numbered(zz):
        return zz + far_side * (LINE - 1 - 2 * zz)

    def device(zz, yy, cc):
        return (section, first + (zz * PAIR + yy) * CORES + cc)

    beside, twin = device(z, other_y, core), device(z, y, other_core)
    partner = (1 - section, place)
    leads = section == 0

    def send(source, target, key, index, to, landing=None):
        return pltpu.make_async_remote_copy(
            src_ref=source, dst_ref=target, send_sem=sem[key + "_send"].at[index],
            recv_sem=sem[key + "_recv"].at[index if landing is None else landing], device_id=to, device_id_type=MESH,
        )

    def fetch(source, target, index):
        return pltpu.make_async_copy(source, target, sem["fetch"].at[index])

    def rows_of(m):
        return pl.ds(pl.multiple_of(m * rows, rows), rows)

    loads = [fetch(w_out_in, w_out, 0), fetch(w_up_in, w_up, 1), fetch(w_down_in, w_down, 2)]
    loads_qkv = [
        fetch(w_qkv_in.at[:, pl.ds(part * width, width)], w_qkv.at[:, pl.ds(part * width, width)], 3 + part)
        for part in range(3)
    ]
    load_rows = [fetch(tokens_in.at[at], h.at[at], 6 + i) for i, at in enumerate((pl.ds(0, front), pl.ds(front, all_rows - front)))]
    load_cotangent = fetch(cotangent_in, e, 6)
    load_norms = [fetch(gains_in, gains, 8), fetch(biases_in, biases, 9)]

    @pl.when(leads)
    def _():
        load_rows[0].start()

    @pl.when(jnp.logical_not(leads))
    def _():
        load_cotangent.start()

    for load in load_norms + loads_qkv[:2]:
        load.start()
    barrier = pltpu.get_barrier_semaphore()
    lined = [device((z + step) % LINE, y, core) for step in range(1, LINE)]
    inner, end, across, far_end = (device(numbered(zz), y, core) for zz in (1, 0, 2, 3))
    peers = [partner, twin, beside] + lined
    for peer in peers:
        pl.semaphore_signal(barrier, inc=1, device_id=peer, device_id_type=MESH)
    loads_qkv[2].start()

    @pl.when(leads)
    def _():
        load_rows[1].start()

    @pl.when(jnp.logical_not(leads))
    def _():
        for load in loads:
            load.start()

    row_ids = lax.broadcasted_iota(jnp.int32, (rows, 1), 0)
    col_ids = lax.broadcasted_iota(jnp.int32, (1, rows), 1)
    seen = (row_ids // ITEM_LEN == col_ids // ITEM_LEN) & (col_ids <= row_ids)
    bias[...] = jnp.where(seen, 0.0, -1e30)
    vector[...] = jnp.zeros_like(vector)
    proj[front:rows, width:] = jnp.zeros((rows - front, 2 * width), BF16)
    scale = 1.0 / math.sqrt(HEAD_DIM)


    spans = ((0, front), (front, rows), (rows, 2 * rows))

    def x_forward(i):
        at = pl.ds(spans[i][0], spans[i][1] - spans[i][0])
        return send(result.at[at], h.at[at], "x_forward", i, partner)

    late = rows // 5
    returns = ((0, rows), (rows, 2 * rows - front), (2 * rows - front, 2 * rows - late), (2 * rows - late, 2 * rows))

    def returned(i):
        return pl.ds(returns[i][0], returns[i][1] - returns[i][0])

    def x_back(i):
        return send(h.at[returned(i)], e.at[returned(i)], "x_back", i, partner)

    def mixed_store(m):
        return pltpu.make_async_copy(result.at[rows_of(m)], mixed_out.at[rows_of(m)], sem["store"].at[0, m])

    def grads_store(m):
        return pltpu.make_async_copy(h.at[rows_of(m)], grads_out.at[rows_of(m)], sem["store"].at[1, m])

    def twin_left(which, m):
        return send(left.at[which - 1, 0, rows_of(m)], left.at[which - 1, 1, rows_of(m)],
                    "twin_left", (which - 1, m), twin)

    def twin_right_of(which, m):
        start = pl.multiple_of(columns_at[which] + other_core * halves[which], 128)
        return send(right.at[rows_of(m), pl.ds(start, halves[which])],
                    twin_right.at[rows_of(m), pl.ds(twin_at[which], halves[which])],
                    "twin_right", (which, m), twin)

    def a2_beside(m):
        return send(left.at[UP - 1, 0, rows_of(m)], act_beside.at[0, rows_of(m)], "act_beside", (0, m), beside)

    def a2_onward(m):
        return send(act_beside.at[0, rows_of(m)], act_beside.at[1, rows_of(m)], "act_beside", (1, m), twin)

    def e_twin(i):
        return send(e_half.at[0, returned(i)], e_half.at[1, returned(i)], "e_half", (0, i), twin)

    def e_beside(i):
        return send(e_other.at[returned(i)], e_half.at[2, returned(i)], "e_half", (1, i), beside)

    def e_onward(i):
        return send(e_half.at[2, returned(i)], e_half.at[3, returned(i)], "e_half", (2, i), twin)


    def attend(i, load=False, first_section=False):
        low, high = spans[i]
        at, m = slice(low, high), low // rows
        whole = slice(m * rows, (m + 1) * rows)
        unit, unused = normalized(h[at].astype(F32))
        left[QKV - 1, 0, at] = (unit * gains[0:1] + biases[0:1]).astype(BF16)
        def project(part):
            cols = slice(part * width, (part + 1) * width)
            if load:
                loads_qkv[part].wait()
            if load and first_section:
                loads[part].start()
            proj[at, cols] = dot(left[QKV - 1, 0, at], w_qkv[:, cols]).astype(BF16)

        project(0)
        project(1)

        def heads_of(part, head):
            start = part * width + head * HEAD_DIM
            return proj[whole, start : start + HEAD_DIM]

        for head in range(HEADS):
            scores = dot_nt(heads_of(0, head), heads_of(1, head)) * scale + bias[...]
            weight = jnp.exp(scores - jnp.max(scores, axis=-1, keepdims=True))
            probs[m * HEADS + head] = (weight / jnp.sum(weight, axis=-1, keepdims=True)).astype(BF16)
        project(2)
        for head in range(HEADS):
            cols = slice(columns_at[OUT] + head * HEAD_DIM, columns_at[OUT] + (head + 1) * HEAD_DIM)
            right[whole, cols] = dot(probs[m * HEADS + head], heads_of(2, head)).astype(BF16)

    def forward(i, load=False):
        at = slice(*spans[i])
        if load:
            loads[0].wait()
        attended = dot(right[at, columns_at[OUT] : columns_at[OUT] + width], w_out[...])
        middle[at] = h[at].astype(F32) + attended
        unit, unused = normalized(middle[at])
        left[UP - 1, 0, at] = (unit * gains[1:2] + biases[1:2]).astype(BF16)
        if i > 0:
            a2_beside(i - 1).start()
        if load:
            loads[1].wait()
        for part in range(2):
            cols = slice(part * hidden // 2, (part + 1) * hidden // 2)
            upward = dot(left[UP - 1, 0, at], w_up[:, cols])
            active, slope = gelu_and_slope(upward)
            slopes[at, cols] = slope.astype(BF16)
            right[at, cols] = active.astype(BF16)
        if load:
            loads[2].wait()
        result[at] = (middle[at] + dot(right[at, :hidden], w_down[...])).astype(BF16)

        @pl.when(leads)
        def _():
            x_forward(i).start()

    def share(m):
        twin_left(UP, m).start()
        twin_right_of(DOWN, m).start()
        twin_right_of(OUT, m).start()
        twin_left(QKV, m).start()
        mixed_store(m).start()

    def gather_act():
        cols = pl.ds(pl.multiple_of(core * halves[DOWN], 128), halves[DOWN])

        @pl.loop(0, MICRO)
        def _(m):
            a2_beside(m).wait_recv()
            a2_onward(m).start()
            a2_onward(m).wait()

            @pl.loop(0, 2)
            def _(source):
                active, unused = gelu_and_slope(dot(act_beside[source, rows_of(m)], w_up[:, cols]))
                act_beside[source, rows_of(m)] = active.astype(BF16)

    def spread(i):
        at = returned(i)
        for zz in range(LINE):
            cols = pl.ds(zz * chunk, chunk)
            e_half[0, at, cols] = e[at, pl.ds(pl.multiple_of((zz * PAIR + y) * chunk, chunk), chunk)]
            e_other[at, cols] = e[at, pl.ds(pl.multiple_of((zz * PAIR + other_y) * chunk, chunk), chunk)]
        e_beside(i).start()
        e_twin(i).start()

    def backward(m, hooks):
        at = rows_of(m)

        for part in (other_core, core):
            start = pl.multiple_of(part * halves[UP], halves[UP])
            cols = pl.ds(start, halves[UP])
            passed = dot_nt(e[at], w_down[cols])
            right[at, pl.ds(columns_at[UP] + start, halves[UP])] = (passed * slopes[at, cols].astype(F32)).astype(BF16)
            if part is other_core:
                twin_right_of(UP, m).start()

        hooks[0](m)
        grad = dot_nt(right[at, columns_at[UP] : columns_at[UP] + hidden], w_up[...])
        unit, size = normalized(middle[at])
        vector[1:2] += jnp.sum(grad * unit, axis=0, keepdims=True)
        vector[3:4] += jnp.sum(grad, axis=0, keepdims=True)
        middle[at] = e[at].astype(F32) + normalize_back(grad, unit, size, gains[1:2])
        left[OUT - 1, 0, at] = middle[at].astype(BF16)
        twin_left(OUT, m).start()
        dctx[...] = dot_nt(left[OUT - 1, 0, at], w_out[...]).astype(BF16)
        hooks[1](m)

        def heads_of(part, head):
            start = part * width + head * HEAD_DIM
            return proj[at, start : start + HEAD_DIM]

        def keep(part, head, value):
            start = columns_at[QKV] + part * width + head * HEAD_DIM
            right[at, start : start + HEAD_DIM] = value.astype(BF16)

        def grad_ctx(head):
            return dctx[:, head * HEAD_DIM : (head + 1) * HEAD_DIM]

        grad_scores = []
        for head in range(HEADS):
            weight = probs[m * HEADS + head].astype(F32)
            grad_weight = dot_nt(grad_ctx(head), heads_of(2, head))
            total = jnp.sum(weight * grad_weight, axis=-1, keepdims=True)
            grad_scores.append((weight * (grad_weight - total)).astype(BF16))
        for head in range(HEADS):
            keep(2, head, dot_tn(probs[m * HEADS + head], grad_ctx(head)))
        for head in range(HEADS):
            keep(0, head, dot(grad_scores[head], heads_of(1, head)) * scale)
            keep(1, head, dot_tn(grad_scores[head], heads_of(0, head)) * scale)

        twin_right_of(QKV, m).start()
        hooks[2](m)
        grad = dot_nt(right[at, columns_at[QKV] : columns_at[QKV] + 3 * width], w_qkv[...])
        unit, size = normalized(h[at].astype(F32))
        vector[0:1] += jnp.sum(grad * unit, axis=0, keepdims=True)
        vector[2:3] += jnp.sum(grad, axis=0, keepdims=True)
        h[at] = (middle[at] + normalize_back(grad, unit, size, gains[0:1])).astype(BF16)
        grads_store(m).start()

        @pl.when(jnp.logical_not(leads))
        def _():
            @pl.when(m == 0)
            def _():
                x_back(0).start()

            @pl.when(m == 1)
            def _():
                x_back(1).start()


    def beside_of(p):
        i = p - direct
        here, there = i % AHEAD, i % (2 * AHEAD)
        return send(parts.at[here, :, other_y], pair_beside.at[there], "pair_beside", here, beside, there)

    def spare_out(part):
        return send(spare_parts.at[part, :, other_y], spare_in.at[part], "spare", part, partner)

    def spare_beside(part, d):
        return send(spare_in.at[part, d], spare_across.at[part, d], "spare_across", (part, d), beside)

    def spare_back(part):
        return send(spare_across.at[part], spare_in.at[part], "spare", part, partner)

    def each_spare(act):
        for part in range(STRIPS):
            for d in range(LINE):
                act(spare_beside(part, d))

    def in_of(p):
        return send(acc.at[p % RING, pl.ds(1, 3)], pair_in.at[pl.ds(3 * (p % RING), 3)], "pair_in", p % RING, inner)

    def across_of(p):
        return send(acc.at[p % RING, 2], pair_across.at[p % RING], "pair_across", p % RING, across)

    def far_of(p):
        there = p % END_RING
        return send(acc.at[p % RING, 3], pair_in.at[2 * there + 1], "pair_far", p % RING, far_end, there)

    def out_of(p):
        there = p % END_RING
        return send(acc.at[p % RING, 0], pair_in.at[2 * there], "pair_out", p % RING, end, there)

    def chunk_at(zz):
        return pl.ds(pl.multiple_of((zz * PAIR + y) * chunk, chunk), chunk)

    vector_store = pltpu.make_async_copy(vector_total, vector_out, sem["vector_store"].at[0])

    def vector_twin():
        return send(vector, vectors.at[0], "vector", 0, twin)

    def vector_beside():
        return send(vector, vectors.at[1], "vector", 1, beside)

    def vector_line(step):
        return send(vector.at[:, chunk_at((z + step) % LINE)], vectors_line.at[step - 1], "vector", 1 + step, lined[step - 1])

    def strip_columns(p):
        return pl.ds(pl.multiple_of(p * strip, strip), strip)

    def fin_of(g):
        cols = pl.ds(pl.multiple_of(g * LEAVING * strip, LEAVING * strip), LEAVING * strip)
        return send(fin.at[1, :, cols], out.at[core, :, cols], "fin", g, twin)

    def kept_of(g):
        cols = pl.ds(pl.multiple_of(g * LEAVING * strip, LEAVING * strip), LEAVING * strip)
        return pltpu.make_async_copy(fin.at[0, :, cols], out.at[core, :, cols], sem["kept"].at[g])

    def add(target, *refs):
        total = target[...].astype(F32)
        for ref in refs:
            total = total + ref[...].astype(F32)
        target[...] = total.astype(BF16)

    def own_columns(p):
        place_of = p * PANEL + core * halves[0]
        for i in (1, 2, 3):
            shift = (columns_at[i] - twin_at[i] + core * halves[i]) - (
                columns_at[i - 1] - twin_at[i - 1] + core * halves[i - 1])
            place_of = place_of + jnp.where(p >= starts[i], shift, 0)
        return pl.ds(pl.multiple_of(place_of, 128), PANEL)

    def twin_columns(p):
        return pl.ds(pl.multiple_of(p * PANEL, PANEL), PANEL)

    def wait_for(which):
        for m in range(MICRO):
            twin_left(which, m).wait_recv()
            twin_right_of(which, m).wait_recv()

    def form(p, spare=False):
        which = QKV - 1 if spare else 0
        for i in () if spare else (OUT, QKV):
            which = which + (p >= starts[i]).astype(jnp.int32)
            due = p == starts[i] if i == OUT else (p == starts[i]) & jnp.logical_not(leads)

            @pl.when(due)
            def _(i=i):
                wait_for(i)

        total = dot_tn(left[which, 0], right[:, own_columns(p)]) + dot_tn(left[which, 1], twin_right[:, twin_columns(p)])
        total = total.astype(BF16).reshape(LINE, PAIR, chunk, PANEL)
        for part in range(STRIPS):
            for zz in range(LINE):
                here = total[zz, :, :, part * strip : (part + 1) * strip]
                if spare:
                    spare_parts[part, numbered(zz)] = here
                else:
                    parts[(p * STRIPS + part - direct) % AHEAD, numbered(zz)] = here

    def form_up(low, high):
        @pl.loop(starts[UP] + low, starts[UP] + high)
        def _(p):
            form(p)

    def start_strips(low, high):
        @pl.loop(direct + low, direct + high)
        def _(p):
            beside_of(p).start()

    def gather_e(i):
        e_beside(i).wait_recv()
        e_onward(i).start()

    def form_down():
        for m in range(MICRO):
            twin_right_of(DOWN, m).wait_recv()
        for i in range(len(returns)):
            e_twin(i).wait_recv()
            e_onward(i).wait_recv()

        @pl.loop(0, starts[UP])
        def _(p):
            total = dot_tn(e_half[0], right[:, own_columns(p)]) + dot_tn(e_half[1], twin_right[:, twin_columns(p)])
            for source in range(2):
                total = total + dot_tn(e_half[2 + source], act_beside[source, :, twin_columns(p)])
            total = total.astype(BF16).reshape(LINE, chunk, PANEL)
            for part in range(STRIPS):
                for zz in range(LINE):
                    acc[(p * STRIPS + part) % RING, numbered(zz)] = total[zz, :, part * strip : (part + 1) * strip]

            @pl.when(is_end & (p < FIRST // STRIPS))
            def _():
                for part in range(STRIPS):
                    in_of(p * STRIPS + part).start()

    def enter(t):
        @pl.when((t < direct - FIRST) & is_end)
        def _():
            in_of(t + FIRST).start()

        @pl.when((t < direct) & is_inner)
        def _():
            out_of(t).start()

    def across_y(t):
        def enter_line(mine_of, theirs_of):
            for d in range(LINE):
                acc[t % RING, d] = (mine_of(d).astype(F32) + theirs_of(d).astype(F32)).astype(BF16)

            @pl.when(is_end)
            def _():
                in_of(t).start()

            @pl.when(is_inner)
            def _():
                out_of(t).start()

        spared = leads & (t // STRIPS == SPARE)

        @pl.when((t >= direct) & (t < strips) & jnp.logical_not(spared))
        def _():
            i = t - direct
            beside_of(t).wait()
            enter_line(lambda d: parts[i % AHEAD, d, y], lambda d: pair_beside[i % (2 * AHEAD), d])

            panel = (t + AHEAD) // STRIPS

            @pl.when((t + AHEAD < strips) & (t % STRIPS == STRIPS - 1) & jnp.logical_not(leads & (panel == SPARE)))
            def _():
                form(panel)
                for part in range(STRIPS):
                    beside_of(t + AHEAD - STRIPS + 1 + part).start()

        @pl.when(spared)
        def _():
            part = t % STRIPS
            spare_back(part).wait_recv()
            enter_line(lambda d: spare_parts[part, d, y], lambda d: spare_in[part, d])

        @pl.when((t == ACROSS) & jnp.logical_not(leads))
        def _():
            for part in range(STRIPS):
                spare_out(part).wait_recv()
            each_spare(lambda message: message.start())

        @pl.when((t == BACK) & jnp.logical_not(leads))
        def _():
            each_spare(lambda message: message.wait_recv())
            for part in range(STRIPS):
                spare_back(part).start()

    def relay(t):
        p = t - LAG

        @pl.when((p >= 0) & (p < strips) & is_inner)
        def _():
            in_of(p).wait_recv()
            add(acc.at[p % RING, pl.ds(2, 2)], pair_in.at[pl.ds(3 * (p % RING) + 1, 2)])
            far_of(p).start()
            across_of(p).start()
            add(acc.at[p % RING, 1], pair_in.at[3 * (p % RING)])

        r = t - END_LAG

        @pl.when(r >= 0)
        def _():
            @pl.when(is_end)
            def _():
                out_of(r).wait_recv()
                far_of(r).wait_recv()
                in_of(r).wait_send()
                finish(r, pair_in.at[2 * (r % END_RING)], pair_in.at[2 * (r % END_RING) + 1])

            @pl.when(is_inner)
            def _():
                across_of(r).wait()
                far_of(r).wait_send()
                out_of(r).wait_send()
                finish(r, pair_across.at[r % RING])

    def finish(r, *refs):
        for slot, which in enumerate((core, other_core)):
            here = pl.ds(pl.multiple_of(which * half_chunk, half_chunk), half_chunk)
            total = acc[r % RING, own, here].astype(F32)
            for ref in refs:
                total = total + ref[here].astype(F32)
            fin[slot, :, strip_columns(r)] = total

        @pl.when(r % LEAVING == LEAVING - 1)
        def _():
            fin_of(r // LEAVING).start()
            kept_of(r // LEAVING).start()

    def vectors_step(t):
        @pl.when(t == VECTORS[0])
        def _():
            vector_twin().wait()
            vector[...] += vectors[0]
            vector_beside().start()

        @pl.when(t == VECTORS[1])
        def _():
            vector_beside().wait()
            vector[...] += vectors[1]
            for step in range(1, LINE):
                vector_line(step).start()

        @pl.when(t == VECTORS[2])
        def _():
            total = vector[:, chunk_at(z)]
            for step in range(1, LINE):
                vector_line(step).wait()
                total = total + vectors_line[step - 1]
            vector_total[...] = total
            vector_store.start()

    def proceed(low, high, parts_of_step):
        @pl.loop(low, high)
        def _(t):
            for part in parts_of_step:
                part(t)


    def after_du(m):
        @pl.when((m == MICRO - 1) & leads)
        def _():
            wait_for(UP)
            form_up(0, 1)
            start_strips(0, STRIPS)
            for i in range(len(returns)):
                gather_e(i)
            form_up(1, 2)
            start_strips(STRIPS, 2 * STRIPS)
            form_down()

    def after_middle(m):
        @pl.when((m == MICRO - 1) & leads)
        def _():
            form_up(2, AHEAD // STRIPS)
            start_strips(2 * STRIPS, AHEAD)
            proceed(0, BEFORE_HEADS, (enter, relay))

    def after_heads(m):
        @pl.when((m == MICRO - 1) & leads)
        def _():
            proceed(BEFORE_HEADS, BEFORE_LAST, (enter, relay))

    @pl.when(leads)
    def _():
        for load in load_rows[:1] + load_norms:
            load.wait()
        attend(0, load=True, first_section=True)

    pl.semaphore_wait(barrier, len(peers))

    @pl.when(jnp.logical_not(leads))
    def _():
        for load in [load_cotangent] + load_norms:
            load.wait()
        for i in range(len(returns)):
            spread(i)
        x_forward(0).wait_recv()
        attend(0, load=True)

    forward(0, load=True)

    @pl.when(leads)
    def _():
        load_rows[1].wait()

    @pl.when(jnp.logical_not(leads))
    def _():
        x_forward(1).wait_recv()

    attend(1)
    forward(1)

    @pl.when(leads)
    def _():
        share(0)

    @pl.loop(0, MICRO + 1)
    def _(step):
        @pl.when(step == section)
        def _():
            @pl.when(jnp.logical_not(leads))
            def _():
                x_forward(2).wait_recv()

            attend(2)
            forward(2)

            @pl.when(leads)
            def _():
                share(1)
                gather_act()

        @pl.when(step != section)
        def _():
            m = step // 2

            @pl.when(leads & (m == 0))
            def _():
                x_back(0).wait_recv()
                spread(0)

            @pl.when(leads & (m == 1))
            def _():
                for i in range(1, len(returns)):
                    x_back(i).wait_recv()
                    spread(i)

            backward(m, (after_du, after_middle, after_heads))

    vector_twin().start()

    @pl.when(leads)
    def _():
        wait_for(QKV)
        form(SPARE, spare=True)
        for part in range(STRIPS):
            spare_out(part).start()

    @pl.when(jnp.logical_not(leads))
    def _():
        for m in range(MICRO):
            share(m)
        for i in range(len(returns)):
            gather_e(i)
        x_back(2).start()
        wait_for(UP)
        form_up(0, 2)
        start_strips(0, 2 * STRIPS)
        x_back(1).wait_send()
        x_back(3).start()
        gather_act()
        form_down()
        form_up(2, AHEAD // STRIPS)
        start_strips(2 * STRIPS, AHEAD)

        proceed(0, BEFORE_LAST, (enter, relay))

    proceed(BEFORE_LAST, strips + END_LAG, (enter, relay, across_y, vectors_step))

    vector_store.wait()
    for part in range(STRIPS):
        spare_out(part).wait_send()

    @pl.when(jnp.logical_not(leads))
    def _():
        each_spare(lambda message: message.wait_send())

    for m in range(MICRO):
        for which in (UP, OUT, QKV):
            twin_left(which, m).wait_send()
        for which in range(4):
            twin_right_of(which, m).wait_send()
        a2_beside(m).wait_send()
        grads_store(m).wait()
        mixed_store(m).wait()

    for i in range(len(returns)):
        e_twin(i).wait_send()
        e_beside(i).wait_send()
        e_onward(i).wait_send()

    @pl.when(jnp.logical_not(leads))
    def _():
        for i in (0, 2, 3):
            x_back(i).wait_send()

    @pl.when(leads)
    def _():
        for i in range(len(spans)):
            x_forward(i).wait_send()

    @pl.loop(0, strips // LEAVING)
    def _(g):
        fin_of(g).wait()
        kept_of(g).wait()


def layers(tokens, cotangent, gains, biases, w_qkv, w_out, w_up, w_down):
    all_rows, width = tokens.shape
    hidden = w_up.shape[1]
    rows = all_rows // MICRO
    columns = 2 * hidden + 4 * width
    strip = PANEL // STRIPS
    strips = columns // CORES // strip
    chunk = width // (LINE * PAIR)
    dma = pltpu.SemaphoreType.DMA
    shapes = {
        "h": ((all_rows, width), BF16),
        "e": ((all_rows, width), BF16),
        "e_other": ((all_rows, width // 2), BF16),
        "result": ((all_rows, width), BF16),
        "w_qkv": (w_qkv.shape, BF16),
        "w_out": (w_out.shape, BF16),
        "w_up": (w_up.shape, BF16),
        "w_down": (w_down.shape, BF16),
        "left": ((3, CORES, all_rows, width), BF16),
        "e_half": ((4, all_rows, width // 2), BF16),
        "right": ((all_rows, columns), BF16),
        "twin_right": ((all_rows, columns // CORES), BF16),
        "act_beside": ((2, all_rows, hidden // CORES), BF16),
        "proj": ((all_rows, 3 * width), BF16),
        "middle": ((all_rows, width), F32),
        "slopes": ((all_rows, hidden), BF16),
        "probs": ((MICRO * HEADS, rows, rows), BF16),
        "bias": ((rows, rows), F32),
        "dctx": ((rows, width), BF16),
        "vector": ((8, width), F32),
        "parts": ((AHEAD, LINE, PAIR, chunk, strip), BF16),
        "acc": ((RING, LINE, chunk, strip), BF16),
        "fin": ((2, chunk // 2, columns // CORES), F32),
        "pair_beside": ((2 * AHEAD, LINE, chunk, strip), BF16),
        "pair_in": ((max(3 * RING, 2 * END_RING), chunk, strip), BF16),
        "pair_across": ((RING, chunk, strip), BF16),
        "spare_parts": ((STRIPS, LINE, PAIR, chunk, strip), BF16),
        "spare_in": ((STRIPS, LINE, chunk, strip), BF16),
        "spare_across": ((STRIPS, LINE, chunk, strip), BF16),
        "vectors": ((2, 8, width), F32),
        "vectors_line": ((LINE - 1, 8, chunk), F32),
        "vector_total": ((8, chunk), F32),
        "gains": (gains.shape, F32),
        "biases": (biases.shape, F32),
    }
    exchanges = {
        "x_forward": (3,), "x_back": (4,), "twin_left": (3, MICRO), "twin_right": (4, MICRO),
        "act_beside": (2, MICRO), "e_half": (3, 4), "pair_in": (RING,), "pair_across": (RING,),
        "fin": (strips // LEAVING,), "spare": (STRIPS,), "spare_across": (STRIPS, LINE), "vector": (LINE + 1,),
    }
    semaphores = {"fetch": dma((10,)), "vector_store": dma((1,)), "store": dma((2, MICRO)), "kept": dma((strips // LEAVING,))}
    for key, count in exchanges.items():
        semaphores[key + "_send"] = dma(count)
        semaphores[key + "_recv"] = dma(count)
    for key in ("pair_out", "pair_far"):
        semaphores[key + "_send"], semaphores[key + "_recv"] = dma((RING,)), dma((END_RING,))
    semaphores["pair_beside_send"], semaphores["pair_beside_recv"] = dma((AHEAD,)), dma((2 * AHEAD,))
    anywhere = pl.BlockSpec(memory_space=pl.ANY)
    return pl.pallas_call(
        layer_kernel,
        out_shape=(
            jax.ShapeDtypeStruct((all_rows, width), BF16),
            jax.ShapeDtypeStruct((all_rows, width), BF16),
            jax.ShapeDtypeStruct((CORES, chunk // 2, columns // CORES), F32),
            jax.ShapeDtypeStruct((8, chunk), F32),
        ),
        in_specs=[anywhere] * 8,
        out_specs=(anywhere,) * 4,
        scratch_shapes=[{key: pltpu.VMEM(*shape) for key, shape in shapes.items()}, semaphores],
        compiler_params=pltpu.CompilerParams(
            collective_id=1, has_side_effects=True, vmem_limit_bytes=64 * 2**20
        ),
        name="relay_layers",
    )(tokens, cotangent, gains, biases, w_qkv, w_out, w_up, w_down)


def results_kernel(
    mixed_in, grads_in, block_in, vectors_in, mixed, grads, down, up, out, qkv, gains, biases,
    rows, block, vectors, shares, sem,
):
    started = []

    def copy(source, target):
        started.append(pltpu.make_async_copy(source, target, sem.at[len(started)]))
        started[-1].start()
        return started[-1]

    row_fetches = [copy(ref, rows.at[i]) for i, ref in enumerate((mixed_in, grads_in))]
    fetches = [copy(vectors_in, vectors)] + [copy(block_in.at[core], block.at[core]) for core in range(CORES)]
    stores = []
    for i, ref in enumerate((mixed, grads)):
        row_fetches[i].wait()
        stores.append(copy(rows.at[i], ref))
    for core in range(CORES):
        fetches[1 + core].wait()
        offset = 0
        for ref in (down, up, out, qkv):
            half = ref.shape[1] // CORES
            stores.append(copy(block.at[core, :, pl.ds(offset, half)], ref.at[:, pl.ds(core * half, half)]))
            offset += half
    fetches[0].wait()
    share = gains.shape[1]
    mine = lax.axis_index("dp") % CORES
    for core in range(CORES):
        @pl.when(mine == core)
        def _(core=core):
            here = slice(core * share, (core + 1) * share)
            shares[0] = vectors[0:2, here]
            shares[1] = vectors[2:4, here]

    stores += [copy(shares.at[i], ref) for i, ref in enumerate((gains, biases))]
    for store in stores:
        store.wait()


def results(mixed, grads, block, vectors, hidden):
    width, share = mixed.shape[1], block.shape[1]
    anywhere = pl.BlockSpec(memory_space=pl.ANY)
    shapes = ((share, hidden), (share, hidden), (share, width), (share, 3 * width), (2, share), (2, share))
    mixed, grads, down, up, out, qkv, gains, biases = pl.pallas_call(
        results_kernel,
        out_shape=(jax.ShapeDtypeStruct(mixed.shape, BF16), jax.ShapeDtypeStruct(grads.shape, BF16))
        + tuple(jax.ShapeDtypeStruct(shape, F32) for shape in shapes),
        in_specs=[anywhere] * 4,
        out_specs=(anywhere,) * 8,
        scratch_shapes=[
            pltpu.VMEM((2,) + mixed.shape, BF16), pltpu.VMEM(block.shape, F32), pltpu.VMEM(vectors.shape, F32),
            pltpu.VMEM((2, 2, share), F32), pltpu.SemaphoreType.DMA((CORES + 3 + 4 * CORES + 4,)),
        ],
        compiler_params=pltpu.CompilerParams(vmem_limit_bytes=64 * 2**20),
        name="place_results",
    )(mixed, grads, block, vectors)
    return mixed, grads, qkv, out.T, up, down.T, gains, biases


def reordered(member, axis, groups, back=False):
    shape = member.shape
    row = shape[axis] // (groups * GROUP)
    split = (GROUP, groups, row) if back else (groups, GROUP, row)
    apart = member.reshape(shape[:axis] + split + shape[axis + 1 :])
    return jnp.swapaxes(apart, axis, axis + 1).reshape(shape)


def on_device(tokens, cotangent, norm_gains, norm_biases, w_qkv, w_out, w_up, w_down):
    hidden, width = w_up.shape[2], tokens.shape[1]
    operands = (tokens, cotangent, norm_gains[0], norm_biases[0], w_qkv[0], w_out[0], w_up[0], w_down[0])
    groups = lax.axis_size("dp") // GROUP
    if groups > 1:
        axes = (1, 1, 1, 1, 0, 1, 0, 1)
        operands = tuple(reordered(member, axis, groups) for member, axis in zip(operands, axes))
    mixed, grads, block, vector_block = layers(*operands)
    if groups == 1:
        return tuple(member[None] for member in results(mixed, grads, block, vector_block, hidden))
    core = lax.axis_index("dp") % CORES
    share = block.shape[1]
    vector_block = lax.dynamic_slice_in_dim(vector_block[:4], core * share, share, 1)
    pieces = []
    offset = 0
    for member in (hidden, hidden, width, 3 * width):
        half = member // CORES
        part = block[:, :, offset : offset + half]
        pieces.append(jnp.concatenate([part[0], part[1]], axis=1))
        offset += half
    mixed, grads = (reordered(member, 1, groups, back=True) for member in (mixed, grads))
    same = [[g * GROUP + j for g in range(groups)] for j in range(GROUP)]

    def summed(member):
        return lax.psum_scatter(member, "dp", scatter_dimension=0, axis_index_groups=same, tiled=True)

    pieces = [summed(member) for member in pieces]
    vector_block = summed(vector_block.T).T
    down, up, out, qkv = pieces
    return (
        mixed[None], grads[None], qkv[None], out.T[None], up[None], down.T[None],
        vector_block[None, 0:2], vector_block[None, 2:4],
    )


def solution(mesh):
    placed = (P("dp", None),) * 2 + (P("section", None, None),) * 6
    return jax.shard_map(
        on_device,
        mesh=mesh,
        in_specs=placed,
        out_specs=(
            P("section", "dp", None),
            P("section", "dp", None),
            P("section", "dp", None),
            P("section", None, "dp"),
            P("section", "dp", None),
            P("section", None, "dp"),
            P("section", None, "dp"),
            P("section", None, "dp"),
        ),
        check_vma=False,
    )
```
